32 devices in a mesh: img: 4 (over y, x), seq: 8 (over z, core).
Axes of the slice: x: 2, y: 2, z: 4, core: 2. Of those that a mesh axis runs over, the one named last changes fastest.
Arguments:
- patches: bfloat16 [20, 1024, 768], P('img', 'seq'), may hold values from -6 to 6
- counts: int32 [20], P('img'), may hold values from 128 to 1024, as said below
- norm_gain_one: bfloat16 [768], replicated, may hold values from 0.099609375 to 1.8984375
- w_query: bfloat16 [768, 768], replicated, may hold values from -0.21875 to 0.21875
- w_key: bfloat16 [768, 768], replicated, may hold values from -0.21875 to 0.21875
- w_value: bfloat16 [768, 768], replicated, may hold values from -0.21875 to 0.21875
- w_out: bfloat16 [768, 768], replicated, may hold values from -3.5 to 3.5
- norm_gain_two: bfloat16 [768], replicated, may hold values from 0.099609375 to 1.8984375
- w_gate: bfloat16 [768, 2048], replicated, may hold values from -0.21875 to 0.21875
- w_up: bfloat16 [768, 2048], replicated, may hold values from -0.21875 to 0.21875
- w_down: bfloat16 [2048, 768], replicated, may hold values from -0.125 to 0.125
- cotangent: bfloat16 [20, 1024, 768], P('img', 'seq'), may hold values from -6 to 6
Outputs:
- layer_out: bfloat16 [20, 1024, 768], P('img', 'seq')
- grad_input: bfloat16 [20, 1024, 768], P('img', 'seq')
- grad_gain_one: float32 [768], replicated
- grad_w_query: float32 [768, 768], replicated
- grad_w_key: float32 [768, 768], replicated
- grad_w_value: float32 [768, 768], replicated
- grad_w_out: float32 [768, 768], replicated
- grad_gain_two: float32 [768], replicated
- grad_w_gate: float32 [768, 2048], replicated
- grad_w_up: float32 [768, 2048], replicated
- grad_w_down: float32 [2048, 768], replicated
- rms_stats: float32 [4], replicated
The draws below stay inside these ranges and needn't reach their ends.
Inputs may be any that keep to these rules, and one draw needn't show every extreme that they name: The valid patches of chart c are its first counts[c] positions. In every run of 5 charts that share an index of img, one chart, drawn from the seed, has all 1024 patches valid.
All inputs are finite; a program needn't handle non-finite values.
Results may differ from the reference program's by a relative error of at most 0.019.
Values may be sent and summed in bfloat16 or wider, within the bound.
No kernel may reach another device: no remote copies, remote signals or barrier semaphores. Data moves between devices by JAX's collectives and lax.ppermute only.
A program may use at most 384 MiB of HBM per device.

```python
import jax
import jax.numpy as jnp
from jax import lax

D = 768
HEADS = 12
HEAD_DIM = 64
FF = 2048
CH_DEV = 5
SEQ = 1024
CHARTS = 20


def draw_counts(key, part):
    key = jax.random.fold_in(key, 11)
    key_len, key_full = jax.random.split(key)
    lengths = jax.random.randint(key_len, (CHARTS,), SEQ // 8, SEQ + 1)
    chosen = jax.random.randint(key_full, (CHARTS // CH_DEV,), 0, CH_DEV)
    position = jnp.arange(CHARTS, dtype=jnp.int32)
    is_full = position % CH_DEV == jnp.repeat(chosen, CH_DEV)
    return jnp.where(is_full, SEQ, lengths).astype(jnp.int32)


def block_levels(stream_key, extent, cuts, low, high):
    loudness, own = 1.0, jax.random.fold_in(stream_key, 6)
    for axis_at, blocks in cuts:
        steps = jnp.exp(jax.random.uniform(jax.random.fold_in(own, axis_at), (blocks,), jnp.float32, low / len(cuts), high / len(cuts)))
        loudness = loudness * jnp.repeat(steps, extent[axis_at] // blocks).reshape([-1 if axis == axis_at else 1 for axis in range(len(extent))])
    return loudness


def centred(own_key, shape, spread, bound, pieces=(), kind=jnp.bfloat16):
    values = spread * jax.random.normal(own_key, shape, jnp.float32)
    if pieces:
        values = values * block_levels(own_key, shape, pieces, -0.22, 0.18)
    return jnp.clip(values, -bound, bound).astype(kind)


def setup_inputs(seed: int = 0) -> dict:
    key_list = jax.random.split(jax.random.key(seed), 13)
    patches = centred(key_list[0], (CHARTS, SEQ, D), 1.0, 6.0, ((0, 4), (1, 8)))
    counts = draw_counts(jax.random.fold_in(key_list[12], 71), 0)
    norm_gain_one = jnp.clip(1.0 + 0.18 * jax.random.normal(key_list[2], (D,), jnp.float32), 0.099609375, 1.8984375).astype(jnp.bfloat16)
    w_query = centred(key_list[3], (D, D), D ** -0.5, 0.21875)
    w_key = centred(key_list[4], (D, D), D ** -0.5, 0.21875)
    w_value = centred(key_list[5], (D, D), D ** -0.5, 0.21875)
    w_out = centred(key_list[6], (D, D), (max(1, 4 * D // SEQ)) ** -0.5, 3.5)
    norm_gain_two = jnp.clip(1.0 + 0.18 * jax.random.normal(key_list[7], (D,), jnp.float32), 0.099609375, 1.8984375).astype(jnp.bfloat16)
    w_gate = centred(key_list[8], (D, FF), D ** -0.5, 0.21875)
    w_up = centred(key_list[9], (D, FF), D ** -0.5, 0.21875)
    w_down = centred(key_list[10], (FF, D), FF ** -0.5, 0.125)
    cotangent = centred(key_list[11], (CHARTS, SEQ, D), 1.0, 6.0, ((0, 4), (1, 8)))
    return dict(patches=patches, counts=counts, norm_gain_one=norm_gain_one, w_query=w_query, w_key=w_key, w_value=w_value, w_out=w_out, norm_gain_two=norm_gain_two, w_gate=w_gate, w_up=w_up, w_down=w_down, cotangent=cotangent)


@jax.custom_vjp
def low(v):
    return lax.optimization_barrier(v.astype(jnp.bfloat16)).astype(jnp.float32)

@jax.custom_vjp
def low_back(v):
    return v

def low_keep(v):
    return (low(v), None)

def low_pass(kept, grad):
    return (grad,)

def back_keep(v):
    return (v, None)

def back_low(kept, grad):
    return (low(grad),)
low.defvjp(low_keep, low_pass)
low_back.defvjp(back_keep, back_low)
eps_norm = 1e-06
big_negative = -1000000000.0
score_scale = 0.125

def rms_scale(values_in, gain_vec):
    return values_in * lax.rsqrt(lax.optimization_barrier(jnp.mean(values_in * values_in, axis=-1, keepdims=True)) + eps_norm) * gain_vec

def mlp_core(gate_in, up_in):
    return jax.nn.gelu(gate_in, approximate=True) * up_in

def project(left_in, weight_in):
    return jnp.dot(left_in, weight_in, precision=lax.Precision.HIGHEST)

def attend_chart(query_one, key_one, value_one, chart_count):
    query_split = query_one.reshape(SEQ, HEADS, HEAD_DIM)
    key_split = key_one.reshape(SEQ, HEADS, HEAD_DIM)
    value_split = value_one.reshape(SEQ, HEADS, HEAD_DIM)
    scores = jnp.einsum('qhd,khd->hqk', query_split, key_split, precision=lax.Precision.HIGHEST) * score_scale
    scores = low_back(scores)
    key_valid = jnp.arange(SEQ, dtype=jnp.int32) < chart_count
    scores = jnp.where(key_valid[None, None, :], scores, big_negative)
    row_max = lax.optimization_barrier(jnp.max(scores, axis=-1, keepdims=True))
    expo = jnp.exp(scores - row_max)
    probs = low(expo / lax.optimization_barrier(jnp.sum(expo, axis=-1, keepdims=True)))
    mixed = jnp.einsum('hqk,khd->qhd', probs, value_split, precision=lax.Precision.HIGHEST)
    return mixed.reshape(SEQ, D)

def reference(patches, counts, norm_gain_one, w_query, w_key, w_value, w_out, norm_gain_two, w_gate, w_up, w_down, cotangent):
    chart_step = jax.checkpoint(attend_chart)

    def per_chart(bundle):
        return chart_step(bundle[0], bundle[1], bundle[2], bundle[3])

    def layer(resid_in, gain_one, wq_in, wk_in, wv_in, wo_in, gain_two, wg_in, wu_in, wd_in):
        first_in = low(rms_scale(resid_in, gain_one))
        query_rows = low_back(low(project(first_in, wq_in)))
        key_rows = low_back(low(project(first_in, wk_in)))
        value_rows = low_back(low(project(first_in, wv_in)))
        mixed = lax.map(per_chart, (query_rows.reshape(CHARTS, SEQ, D), key_rows.reshape(CHARTS, SEQ, D), value_rows.reshape(CHARTS, SEQ, D), counts))
        attn_in = low_back(low(mixed.reshape(CHARTS * SEQ, D)))
        branch_one = low_back(project(attn_in, wo_in))
        middle = resid_in + branch_one
        second_in = low(rms_scale(middle, gain_two))
        gate_rows = low_back(project(second_in, wg_in))
        up_rows = low_back(project(second_in, wu_in))
        inner = low(mlp_core(gate_rows, up_rows))
        branch_two = low_back(project(inner, wd_in))
        result = middle + branch_two
        return (result, (branch_one, branch_two))
    resid = patches.astype(jnp.float32).reshape(CHARTS * SEQ, D)
    params = (resid, norm_gain_one.astype(jnp.float32), w_query.astype(jnp.float32), w_key.astype(jnp.float32), w_value.astype(jnp.float32), w_out.astype(jnp.float32), norm_gain_two.astype(jnp.float32), w_gate.astype(jnp.float32), w_up.astype(jnp.float32), w_down.astype(jnp.float32))
    result, pullback, extras = jax.vjp(layer, *params, has_aux=True)
    grads = pullback(cotangent.astype(jnp.float32).reshape(CHARTS * SEQ, D))
    row_mask = (jnp.arange(SEQ, dtype=jnp.int32)[None, :] < counts[:, None]).reshape(CHARTS * SEQ).astype(jnp.float32)
    total_valid = jnp.sum(counts.astype(jnp.float32)) * D
    squares = jnp.stack([jnp.sum(row_mask * lax.optimization_barrier(jnp.sum(member * member, axis=-1))) for member in (resid, extras[0], extras[1], result)])
    rms_stats = jnp.sqrt(squares / total_valid)
    return (result.astype(jnp.bfloat16).reshape(CHARTS, SEQ, D), grads[0].astype(jnp.bfloat16).reshape(CHARTS, SEQ, D), grads[1], grads[2], grads[3], grads[4], grads[5], grads[6], grads[7], grads[8], grads[9], rms_stats)
```

```python
import functools
import math

import jax
import jax.numpy as jnp
from jax import lax
from jax.experimental import pallas as pl
from jax.experimental.pallas import tpu as pltpu
from jax.sharding import PartitionSpec as P

HEADS = 12
GROUPS = 4
EPS = 1e-06
NEG = -1000000000.0
LOG2E = 1.4426950408889634
LN2 = 0.6931471805599453
BF = jnp.bfloat16
F32 = jnp.float32
VMEM_LIMIT = 56 * 1024 * 1024


def dot(left, right):
    return jnp.dot(left, right, preferred_element_type=F32)


def dot_nt(left, right):
    return lax.dot_general(left, right, (((1,), (1,)), ((), ())), preferred_element_type=F32)


def dot_tn(left, right):
    return lax.dot_general(left, right, (((0,), (0,)), ((), ())), preferred_element_type=F32)


def split_three(column):
    hi = column.astype(BF).astype(F32)
    rest = column - hi
    mid = rest.astype(BF).astype(F32)
    return hi, mid, rest - mid


def with_extras(values, half, extras):
    lane = lax.broadcasted_iota(jnp.int32, values.shape, 1)
    mine = (lane < 64) if half == 0 else (lane >= 64)
    base = 64 if half == 0 else 0
    out = jnp.where(mine, values, 0.0)
    for offset, column in enumerate(extras):
        if column is not None:
            out = jnp.where(lane == base + offset, column, out)
    return out.astype(BF)


def attend_kernel(q_rows, place_ref, fiq_ref, fik_ref, wq_ref, wk_ref, wv_ref, bias_ref,
                  qx_ref, kx_ref, vx_ref, out_ref):
    del place_ref
    scale = LOG2E / math.sqrt(64.0)
    bias = bias_ref[...]
    key_rows = dot(fik_ref[...], wk_ref[...]).astype(BF).astype(F32)
    value_rows = dot(fik_ref[...], wv_ref[...]).astype(BF).astype(F32)
    for half in range(2):
        kx_ref[half] = with_extras(key_rows, half, (1.0, 1.0, 1.0, bias))
        vx_ref[half] = with_extras(value_rows, half, (1.0, 1.0, 1.0))
    total = fiq_ref.shape[0]
    for start in range(0, total, q_rows):
        rows = pl.ds(start, q_rows)
        query = dot(fiq_ref[rows, :], wq_ref[...]) * scale
        results = []
        for half in range(2):
            base = 64 if half == 0 else 0
            plain = with_extras(query, half, (None, None, None, 1.0))
            scores = dot_nt(plain, kx_ref[half])
            top = jnp.max(scores, axis=1, keepdims=True)
            weights = jnp.exp2(scores - top).astype(BF)
            mixed = dot(weights, vx_ref[half])
            norm = mixed[:, base:base + 1]
            log_total = top + jnp.log2(norm)
            hi, mid, low = split_three(-log_total)
            qx_ref[half, rows, :] = with_extras(query, half, (hi, mid, low, 1.0))
            results.append(mixed / norm)
        lane = lax.broadcasted_iota(jnp.int32, results[0].shape, 1)
        out_ref[rows, :] = jnp.where(lane < 64, results[0], results[1]).astype(BF)


def attend(place, fi_q, fi_k, w_query, w_key, w_value, bias, pairs, q_rows):
    q_total, width = fi_q.shape
    k_total = fi_k.shape[0]
    column = lambda i, place_ref: (0, place_ref[0] * pairs + i)
    whole = lambda i, place_ref: (0, 0)
    stacked = lambda i, place_ref: (i, 0, 0)
    return pl.pallas_call(
        functools.partial(attend_kernel, q_rows),
        grid_spec=pltpu.PrefetchScalarGridSpec(
            num_scalar_prefetch=1,
            grid=(pairs,),
            in_specs=[
                pl.BlockSpec((q_total, width), whole),
                pl.BlockSpec((k_total, width), whole),
                pl.BlockSpec((width, 128), column),
                pl.BlockSpec((width, 128), column),
                pl.BlockSpec((width, 128), column),
                pl.BlockSpec((k_total, 1), whole),
            ],
            out_specs=[
                pl.BlockSpec((2, q_total, 128), stacked),
                pl.BlockSpec((2, k_total, 128), stacked),
                pl.BlockSpec((2, k_total, 128), stacked),
                pl.BlockSpec((q_total, 128), lambda i, place_ref: (0, i)),
            ],
        ),
        out_shape=[
            jax.ShapeDtypeStruct((2 * pairs, q_total, 128), BF),
            jax.ShapeDtypeStruct((2 * pairs, k_total, 128), BF),
            jax.ShapeDtypeStruct((2 * pairs, k_total, 128), BF),
            jax.ShapeDtypeStruct((q_total, pairs * 128), BF),
        ],
        compiler_params=pltpu.CompilerParams(vmem_limit_bytes=VMEM_LIMIT),
        cost_estimate=pl.CostEstimate(
            flops=2 * 128 * pairs * (2 * q_total * k_total + width * (q_total + 2 * k_total)),
            bytes_accessed=2 * (q_total + k_total) * width * 4,
            transcendentals=2 * pairs * q_total * k_total,
        ),
    )(place, fi_q, fi_k, w_query, w_key, w_value, bias)


def attend_back_kernel(q_rows, qx_ref, kx_ref, vx_ref, out_ref, grad_ref, dq_ref, dk_ref, dv_ref):
    q_total, k_total = qx_ref.shape[1], kx_ref.shape[1]
    dk_all, dv_all = [], []
    lane_k = lax.broadcasted_iota(jnp.int32, (k_total, 128), 1)
    keys_pair = jnp.where(lane_k < 64, kx_ref[0], kx_ref[1])
    keys_trans = jnp.transpose(keys_pair.astype(F32)).astype(BF)
    dq_trans = [[], []]
    for half in range(2):
        dk_sum = jnp.zeros((k_total, 128), F32)
        dv_sum = jnp.zeros((k_total, 128), F32)
        for start in range(0, q_total, q_rows):
            rows = pl.ds(start, q_rows)
            grad = grad_ref[rows, :].astype(F32)
            lane = lax.broadcasted_iota(jnp.int32, grad.shape, 1)
            mine = (lane < 64) if half == 0 else (lane >= 64)
            delta = jnp.sum(jnp.where(mine, grad * out_ref[rows, :].astype(F32), 0.0), axis=1, keepdims=True)
            hi, mid, low = split_three(-delta)
            grad_x = with_extras(grad, half, (hi, mid, low))
            query_x = qx_ref[half, rows, :]
            probs = jnp.exp2(dot_nt(kx_ref[half], query_x))
            centred = dot_nt(vx_ref[half], grad_x)
            grad_scores = (probs * centred).astype(BF)
            dv_sum = dv_sum + dot(probs.astype(BF), grad_x)
            dk_sum = dk_sum + dot(grad_scores, query_x)
            dq_trans[half].append(dot(keys_trans[64 * half:64 * half + 64, :], grad_scores))
        dk_all.append(dk_sum)
        dv_all.append(dv_sum)
    for index, start in enumerate(range(0, q_total, q_rows)):
        joined = jnp.concatenate([dq_trans[0][index], dq_trans[1][index]], axis=0)
        dq_ref[pl.ds(start, q_rows), :] = (jnp.transpose(joined) * 0.125).astype(BF)
    dk_ref[...] = (jnp.where(lane_k < 64, dk_all[0], dk_all[1]) * LN2).astype(BF)
    dv_ref[...] = jnp.where(lane_k < 64, dv_all[0], dv_all[1]).astype(BF)


def attend_back(qx, kx, vx, out, grad, q_rows):
    heads, q_total, _ = qx.shape
    k_total = kx.shape[1]
    pairs = heads // 2
    stacked = lambda i: (i, 0, 0)
    flat = lambda i: (0, i)
    return pl.pallas_call(
        functools.partial(attend_back_kernel, q_rows),
        grid=(pairs,),
        in_specs=[
            pl.BlockSpec((2, q_total, 128), stacked),
            pl.BlockSpec((2, k_total, 128), stacked),
            pl.BlockSpec((2, k_total, 128), stacked),
            pl.BlockSpec((q_total, 128), flat),
            pl.BlockSpec((q_total, 128), flat),
        ],
        out_specs=[
            pl.BlockSpec((q_total, 128), flat),
            pl.BlockSpec((k_total, 128), flat),
            pl.BlockSpec((k_total, 128), flat),
        ],
        out_shape=[
            jax.ShapeDtypeStruct((q_total, pairs * 128), BF),
            jax.ShapeDtypeStruct((k_total, pairs * 128), BF),
            jax.ShapeDtypeStruct((k_total, pairs * 128), BF),
        ],
        compiler_params=pltpu.CompilerParams(vmem_limit_bytes=VMEM_LIMIT),
        cost_estimate=pl.CostEstimate(
            flops=2 * 128 * pairs * 5 * q_total * k_total,
            bytes_accessed=2 * 128 * heads * (q_total + 2 * k_total),
            transcendentals=heads * q_total * k_total,
        ),
    )(qx, kx, vx, out, grad)


def norm_scale(values):
    return lax.rsqrt(jnp.mean(values * values, axis=-1, keepdims=True) + EPS)


def norm_back(values, gain, grad):
    scale = norm_scale(values)
    scaled = values * scale
    weighted = grad * gain
    inner = jnp.mean(weighted * scaled, axis=-1, keepdims=True)
    return scale * (weighted - scaled * inner), jnp.sum(grad * scaled, axis=0)


def mlp_core(gate_in, up_in):
    return jax.nn.gelu(gate_in, approximate=True) * up_in


def masked_squares(values_in, row_mask):
    return jnp.sum(row_mask * jnp.sum(values_in * values_in, axis=-1))


def body(n_img, n_seq, patches, counts, norm_gain_one, w_query, w_key, w_value, w_out,
         norm_gain_two, w_gate, w_up, w_down, cotangent):
    charts, block_len, width = patches.shape
    members = n_seq // GROUPS
    head_count = HEADS // members
    pairs = -(-head_count // 2)
    pad_cols = pairs * 128 - head_count * 64
    mine_cols = head_count * 64
    main_own = GROUPS * block_len
    seq_len = n_seq * block_len
    here = lax.axis_index("seq")
    group, member = here // members, here % members

    def shift_perm(step):
        return [(g * members + r, ((g + step) % GROUPS) * members + r)
                for g in range(GROUPS) for r in range(members)]

    def member_perm(step):
        return [(g * members + r, g * members + (r ^ step))
                for g in range(GROUPS) for r in range(members)]

    def to_groups(array):
        pieces = []
        for step in range(GROUPS):
            part = lax.dynamic_index_in_dim(array, (group + step) % GROUPS, 0, keepdims=False)
            pieces.append(part if step == 0 else lax.ppermute(part, "seq", shift_perm(step)))
        return pieces

    def from_groups(rows):
        pieces = []
        for step in range(GROUPS):
            part = rows[step * block_len:(step + 1) * block_len]
            pieces.append(part if step == 0 else lax.ppermute(part, "seq", shift_perm(-step)))
        ring = jnp.stack(pieces + pieces)
        return lax.dynamic_slice_in_dim(ring, (GROUPS - group) % GROUPS, GROUPS, 0)

    def to_members(own):
        return [own] + [lax.ppermute(own, "seq", member_perm(step)) for step in range(1, members)]

    def columns_of(weight, who):
        part = lax.dynamic_slice_in_dim(weight, who * mine_cols, mine_cols, 1)
        return jnp.pad(part, ((0, 0), (0, pad_cols))) if pad_cols else part

    gain_one = norm_gain_one.astype(F32)
    gain_two = norm_gain_two.astype(F32)
    steps = jnp.arange(GROUPS, dtype=jnp.int32)
    block_of = ((group - steps) % GROUPS) * members
    inside = jnp.arange(block_len, dtype=jnp.int32)

    def main_positions(who):
        return ((block_of + who) * block_len)[:, None] + inside[None, :]

    count_main = lax.dynamic_index_in_dim(counts, group, 0, keepdims=False)
    count_rest = counts[GROUPS]
    rest_positions = here * block_len + inside
    row_valid = jnp.concatenate([
        (main_positions(member) < count_main).reshape(-1), rest_positions < count_rest])
    row_mask = row_valid.astype(F32)
    key_positions = jnp.concatenate(
        [main_positions(member ^ step).reshape(-1) for step in range(members)])
    bias_main = jnp.where(key_positions < count_main, 0.0, NEG).astype(F32)[:, None]
    bias_rest = jnp.where(jnp.arange(seq_len) < count_rest, 0.0, NEG).astype(F32)[:, None]

    rest_rows = patches[GROUPS]
    rest_f32 = rest_rows.astype(F32)
    first_rest = (rest_f32 * norm_scale(rest_f32) * gain_one).astype(BF)
    moved = to_groups(patches)
    first_rest_all = lax.all_gather(first_rest, "seq", axis=0, tiled=True)
    main_rows = jnp.concatenate(moved, axis=0).astype(F32)
    first_main = (main_rows * norm_scale(main_rows) * gain_one).astype(BF)
    first_all = jnp.concatenate(to_members(first_main), axis=0)
    grad_moved = to_groups(cotangent)

    place = jnp.reshape(member, (1,)).astype(jnp.int32)
    zero_place = jnp.zeros((1,), jnp.int32)
    if pad_cols:
        main_weights = [columns_of(w, member) for w in (w_query, w_key, w_value)]
        main_place = zero_place
    else:
        main_weights = [w_query, w_key, w_value]
        main_place = place
    q_rows = 256
    qx_main, kx_main, vx_main, attn_main = attend(
        main_place, first_all, first_all, *main_weights, bias_main, pairs, q_rows)
    qx_rest, kx_rest, vx_rest, attn_rest = attend(
        zero_place, first_rest, first_rest_all, w_query, w_key, w_value, bias_rest,
        HEADS // 2, min(q_rows, block_len))

    def swap_in(array):
        pieces = []
        for step in range(members):
            part = array[step * main_own:(step + 1) * main_own, :mine_cols]
            pieces.append(part if step == 0 else lax.ppermute(part, "seq", member_perm(step)))
        out = jnp.zeros((main_own, width), array.dtype)
        for step in range(members):
            out = lax.dynamic_update_slice_in_dim(out, pieces[step], (member ^ step) * mine_cols, 1)
        return out

    attn_in = jnp.concatenate([swap_in(attn_main), attn_rest], axis=0)
    resid = jnp.concatenate([main_rows, rest_f32], axis=0)
    branch_one = dot(attn_in, w_out)
    middle = resid + branch_one
    second_in = (middle * norm_scale(middle) * gain_two).astype(BF)
    gate_rows = dot(second_in, w_gate)
    up_rows = dot(second_in, w_up)
    inner = mlp_core(gate_rows, up_rows).astype(BF)
    branch_two = dot(inner, w_down)
    result = middle + branch_two
    squares = jnp.stack([masked_squares(v, row_mask) for v in (resid, branch_one, branch_two, result)])
    valid_count = jnp.sum(row_mask)
    result_low = result.astype(BF)
    layer_out = jnp.concatenate(
        [from_groups(result_low[:main_own]), result_low[main_own:][None]], axis=0)

    grad_low = jnp.concatenate(grad_moved + [cotangent[GROUPS]], axis=0)
    grad_out = grad_low.astype(F32)

    def total(*arrays):
        return lax.psum(tuple(a.astype(BF) for a in arrays), ("img", "seq"))

    (sum_down,) = total(dot_tn(inner, grad_low))
    grad_inner = dot_nt(grad_low, w_down)
    _, mlp_back = jax.vjp(mlp_core, gate_rows, up_rows)
    grad_gate, grad_up = mlp_back(grad_inner)
    grad_gate = grad_gate.astype(BF)
    grad_up = grad_up.astype(BF)
    sum_gate, sum_up = total(dot_tn(second_in, grad_gate), dot_tn(second_in, grad_up))
    grad_second = dot_nt(grad_gate, w_gate) + dot_nt(grad_up, w_up)
    grad_mid_norm, grad_gain_two = norm_back(middle, gain_two, grad_second)
    grad_mid = grad_out + grad_mid_norm
    grad_mid_low = grad_mid.astype(BF)
    part_out = dot_tn(attn_in, grad_mid_low)

    main_grads = []
    for step in range(members):
        rows_of = lax.dynamic_slice_in_dim(w_out, (member ^ step) * mine_cols, mine_cols, 0)
        part = dot_nt(grad_mid_low[:main_own], rows_of).astype(BF)
        if pad_cols:
            part = jnp.pad(part, ((0, 0), (0, pad_cols)))
        main_grads.append(part if step == 0 else lax.ppermute(part, "seq", member_perm(step)))
    grad_attn_main = jnp.concatenate(main_grads, axis=0)
    grad_attn_rest = dot_nt(grad_mid_low[main_own:], w_out).astype(BF)

    dq_rest, dk_rest, dv_rest = attend_back(
        qx_rest, kx_rest, vx_rest, attn_rest, grad_attn_rest, min(q_rows, block_len))
    first_part_rest = (dot_nt(dk_rest, w_key) + dot_nt(dv_rest, w_value)).astype(BF)
    first_sum_rest = lax.psum_scatter(first_part_rest, "seq", scatter_dimension=0, tiled=True)
    dq_main, dk_main, dv_main = attend_back(
        qx_main, kx_main, vx_main, attn_main, grad_attn_main, q_rows)

    main_parts = [(dq_main, w_query), (dk_main, w_key), (dv_main, w_value)]
    first_part_main = sum(
        dot_nt(part[:, :mine_cols], lax.dynamic_slice_in_dim(w, member * mine_cols, mine_cols, 1))
        for part, w in main_parts)
    grad_first_main = first_part_main[:main_own]
    for step in range(1, members):
        part = first_part_main[step * main_own:(step + 1) * main_own].astype(BF)
        grad_first_main = grad_first_main + lax.ppermute(part, "seq", member_perm(step)).astype(F32)
    grad_first_rest = dot_nt(dq_rest, w_query) + first_sum_rest.astype(F32)
    grad_first = jnp.concatenate([grad_first_main, grad_first_rest], axis=0)

    qkv_parts = []
    rest_parts = [(first_rest, dq_rest), (first_rest_all, dk_rest), (first_rest_all, dv_rest)]
    for (part, _), (fi_rest, part_rest) in zip(main_parts, rest_parts):
        whole = dot_tn(fi_rest, part_rest)
        local = dot_tn(first_all, part[:, :mine_cols])
        spot = lax.dynamic_slice_in_dim(whole, member * mine_cols, mine_cols, 1)
        qkv_parts.append(lax.dynamic_update_slice_in_dim(whole, spot + local, member * mine_cols, 1))
    sum_query, sum_key, sum_value, sum_out = total(*qkv_parts, part_out)

    grad_resid_norm, grad_gain_one = norm_back(resid, gain_one, grad_first)
    grad_input_rows = (grad_mid + grad_resid_norm).astype(BF)
    grad_input = jnp.concatenate(
        [from_groups(grad_input_rows[:main_own]), grad_input_rows[main_own:][None]], axis=0)
    sum_gain_one, sum_gain_two, sum_squares, sum_count = lax.psum(
        (grad_gain_one, grad_gain_two, squares, valid_count), ("img", "seq"))
    rms_stats = jnp.sqrt(sum_squares / (sum_count * width))
    wide = lambda a: a.astype(F32)
    return (layer_out, grad_input, sum_gain_one, wide(sum_query), wide(sum_key), wide(sum_value),
            wide(sum_out), sum_gain_two, wide(sum_gate), wide(sum_up), wide(sum_down), rms_stats)


def solution(mesh):
    rows = P("img", "seq", None)
    return jax.shard_map(
        functools.partial(body, mesh.shape["img"], mesh.shape["seq"]),
        mesh=mesh,
        in_specs=(rows, P("img"), P(), P(), P(), P(), P(), P(), P(), P(), P(), rows),
        out_specs=(rows, rows, P(), P(), P(), P(), P(), P(), P(), P(), P(), P()),
        check_vma=False,
    )
```

```python
import functools
import math

import jax
import jax.numpy as jnp
from jax import lax
from jax.experimental import pallas as pl
from jax.experimental.pallas import tpu as pltpu
from jax.sharding import PartitionSpec as P

HEADS = 12
GROUPS = 4
SHARDS = 16
EPS = 1e-06
NEG = -1000000000.0
LOG2E = 1.4426950408889634
LN2 = 0.6931471805599453
GELU_C = 0.7978845608028654
GELU_A = 0.044715
BF = jnp.bfloat16
F32 = jnp.float32
VMEM_LIMIT = 56 * 1024 * 1024
ANY = pl.BlockSpec(memory_space=pl.ANY)


def dot(left, right):
    return jnp.dot(left, right, preferred_element_type=F32)


def dot_nt(left, right):
    return lax.dot_general(left, right, (((1,), (1,)), ((), ())), preferred_element_type=F32)


def dot_tn(left, right):
    return lax.dot_general(left, right, (((0,), (0,)), ((), ())), preferred_element_type=F32)


def split_three(column):
    hi = column.astype(BF).astype(F32)
    rest = column - hi
    mid = rest.astype(BF).astype(F32)
    return hi, mid, rest - mid


def extras(rows, columns):
    lane = lax.broadcasted_iota(jnp.int32, (rows, 128), 1)
    out = jnp.zeros((rows, 128), F32)
    for index, column in enumerate(columns):
        if column is not None:
            out = jnp.where(lane == index, column, out)
    return out.astype(BF)


def head_lanes(values, half):
    lane = lax.broadcasted_iota(jnp.int32, values.shape, 1)
    return jnp.where((lane < 64) if half == 0 else (lane >= 64), values, jnp.zeros_like(values))


def stack_heads(values):
    return jnp.concatenate([head_lanes(values, 0), head_lanes(values, 1)], axis=0)


def attend_kernel(q_rows, place_ref, fiq_ref, fik_ref, wq_ref, wk_ref, wv_ref, ext_ref, *refs):
    q_ref, k_ref, v_ref, log_ref, out_ref = refs[-5:]
    scale = LOG2E / math.sqrt(64.0)
    both = dot(fik_ref[...], jnp.concatenate([wk_ref[...], wv_ref[...]], axis=1)).astype(BF)
    k_ref[0] = both[:, :128]
    v_ref[0] = both[:, 128:]
    query = (dot(fiq_ref[...], wq_ref[...]) * scale).astype(BF)
    q_ref[0] = query
    ext = ext_ref[...]
    keys = jnp.concatenate([both[:, :128], ext], axis=1)
    values = jnp.concatenate([both[:, 128:], ext], axis=1)
    one = extras(2 * q_rows, (None, None, None, 1.0))
    for start in range(0, fiq_ref.shape[0], q_rows):
        rows = slice(start, start + q_rows)
        scores = dot_nt(jnp.concatenate([stack_heads(query[rows]), one], axis=1), keys)
        top = jnp.max(scores, axis=1, keepdims=True)
        weights = jnp.exp2(scores - top).astype(BF)
        mixed = dot(weights, values)
        norm = mixed[:, 128:129]
        logs = extras(2 * q_rows, split_three(-(top + jnp.log2(norm))) + (1.0,))
        log_ref[0, rows, :] = logs[:q_rows]
        log_ref[1, rows, :] = logs[q_rows:]
        scaled = mixed[:, :128] / norm
        lane = lax.broadcasted_iota(jnp.int32, (q_rows, 128), 1)
        out_ref[rows, :] = jnp.where(lane < 64, scaled[:q_rows], scaled[q_rows:]).astype(BF)


def attend(place, fi_q, fi_k, w_query, w_key, w_value, ext, pairs, q_rows, after=()):
    q_total, width = fi_q.shape
    k_total = fi_k.shape[0]
    column = lambda i, p: (0, p[0] * pairs + i)
    whole = lambda i, p: (0, 0)
    stacked = lambda i, p: (i, 0, 0)
    return pl.pallas_call(
        functools.partial(attend_kernel, q_rows),
        grid_spec=pltpu.PrefetchScalarGridSpec(
            num_scalar_prefetch=1,
            grid=(pairs,),
            in_specs=[
                pl.BlockSpec((q_total, width), whole),
                pl.BlockSpec((k_total, width), whole),
                pl.BlockSpec((width, 128), column),
                pl.BlockSpec((width, 128), column),
                pl.BlockSpec((width, 128), column),
                pl.BlockSpec((k_total, 128), whole),
            ] + [ANY] * len(after),
            out_specs=[
                pl.BlockSpec((1, q_total, 128), stacked),
                pl.BlockSpec((1, k_total, 128), stacked),
                pl.BlockSpec((1, k_total, 128), stacked),
                pl.BlockSpec((2, q_total, 128), stacked),
                pl.BlockSpec((q_total, 128), lambda i, p: (0, i)),
            ],
        ),
        out_shape=[
            jax.ShapeDtypeStruct((pairs, q_total, 128), BF),
            jax.ShapeDtypeStruct((pairs, k_total, 128), BF),
            jax.ShapeDtypeStruct((pairs, k_total, 128), BF),
            jax.ShapeDtypeStruct((2 * pairs, q_total, 128), BF),
            jax.ShapeDtypeStruct((q_total, pairs * 128), BF),
        ],
        compiler_params=pltpu.CompilerParams(vmem_limit_bytes=VMEM_LIMIT),
        cost_estimate=pl.CostEstimate(
            flops=4 * 128 * pairs * (4 * q_total * k_total + width * (q_total + 2 * k_total)),
            bytes_accessed=2 * (q_total + k_total) * width * 4,
            transcendentals=2 * pairs * q_total * k_total,
        ),
    )(place, fi_q, fi_k, w_query, w_key, w_value, ext, *after)


def attend_back_kernel(q_rows, q_ref, k_ref, v_ref, ext_ref, log_ref, out_ref, grad_ref, *refs):
    dq_ref, dk_ref, dv_ref = refs[-3:]
    ext = ext_ref[...]
    key_pair = k_ref[0]
    keys = jnp.concatenate([key_pair, ext], axis=1)
    values = jnp.concatenate([v_ref[0], ext], axis=1)
    keys_trans = jnp.transpose(key_pair.astype(F32)).astype(BF)
    dk_sum = jnp.zeros(key_pair.shape, F32)
    dv_sum = jnp.zeros(key_pair.shape, F32)
    for start in range(0, q_ref.shape[1], q_rows):
        rows = slice(start, start + q_rows)
        grad = grad_ref[rows, :]
        product = grad.astype(F32) * out_ref[rows, :].astype(F32)
        delta = jnp.sum(stack_heads(product), axis=1, keepdims=True)
        grad_h = stack_heads(grad)
        query_h = stack_heads(q_ref[0, rows, :])
        logs = jnp.concatenate([log_ref[0, rows, :], log_ref[1, rows, :]], axis=0)
        probs = jnp.exp2(dot_nt(keys, jnp.concatenate([query_h, logs], axis=1)))
        centred = dot_nt(values, jnp.concatenate([grad_h, extras(2 * q_rows, split_three(-delta))], axis=1))
        grad_scores = (probs * centred).astype(BF)
        dv_sum = dv_sum + dot(probs.astype(BF), grad_h)
        dk_sum = dk_sum + dot(grad_scores, query_h)
        first = dot(keys_trans[:64], grad_scores[:, :q_rows])
        second = dot(keys_trans[64:], grad_scores[:, q_rows:])
        dq_ref[rows, :] = (jnp.transpose(jnp.concatenate([first, second], axis=0)) * 0.125).astype(BF)
    dk_ref[...] = (dk_sum * LN2).astype(BF)
    dv_ref[...] = dv_sum.astype(BF)


def attend_back(query, key, value, ext, logs, out, grad, q_rows, after=()):
    _, q_total, _ = query.shape
    pairs = query.shape[0]
    k_total = key.shape[1]
    stacked = lambda i: (i, 0, 0)
    flat = lambda i: (0, i)
    return pl.pallas_call(
        functools.partial(attend_back_kernel, q_rows),
        grid=(pairs,),
        in_specs=[
            pl.BlockSpec((1, q_total, 128), stacked),
            pl.BlockSpec((1, k_total, 128), stacked),
            pl.BlockSpec((1, k_total, 128), stacked),
            pl.BlockSpec((k_total, 128), lambda i: (0, 0)),
            pl.BlockSpec((2, q_total, 128), stacked),
            pl.BlockSpec((q_total, 128), flat),
            pl.BlockSpec((q_total, 128), flat),
        ] + [ANY] * len(after),
        out_specs=[
            pl.BlockSpec((q_total, 128), lambda i: (0, i)),
            pl.BlockSpec((k_total, 128), lambda i: (0, i)),
            pl.BlockSpec((k_total, 128), lambda i: (0, i)),
        ],
        out_shape=[
            jax.ShapeDtypeStruct((q_total, pairs * 128), BF),
            jax.ShapeDtypeStruct((k_total, pairs * 128), BF),
            jax.ShapeDtypeStruct((k_total, pairs * 128), BF),
        ],
        compiler_params=pltpu.CompilerParams(vmem_limit_bytes=VMEM_LIMIT),
        cost_estimate=pl.CostEstimate(
            flops=2 * 256 * pairs * 5 * q_total * k_total,
            bytes_accessed=2 * 128 * pairs * (4 * q_total + 4 * k_total),
            transcendentals=2 * pairs * q_total * k_total,
        ),
    )(query, key, value, ext, logs, out, grad, *after)


FF_TILE = 256


def ff_kernel(first, place_ref, second_ref, grad_ref, wg_ref, wu_ref, wd_ref, *refs):
    two_ref, gs_ref, part_ref, second_t_ref = refs[-4:]
    step = pl.program_id(0)

    @pl.when(step == 0)
    def _():
        second_t_ref[...] = jnp.transpose(second_ref[...])
        if first:
            two_ref[...] = jnp.zeros_like(two_ref)
            gs_ref[...] = jnp.zeros_like(gs_ref)
        else:
            two_ref[...] = refs[0][...]
            gs_ref[...] = refs[1][...]

    second, grad = second_ref[...], grad_ref[...]
    gate = dot(second, wg_ref[...])
    up = dot(second, wu_ref[...])
    grad_inner = dot_nt(grad, wd_ref[...])
    square = gate * gate
    bend = jnp.tanh(GELU_C * gate * (1.0 + GELU_A * square))
    half_plus = 0.5 + 0.5 * bend
    gelu = gate * half_plus
    slope = half_plus + 0.5 * gate * (1.0 - bend * bend) * (GELU_C * (1.0 + 3.0 * GELU_A * square))
    inner = (gelu * up).astype(BF)
    grad_gate = (grad_inner * up * slope).astype(BF)
    grad_up = (grad_inner * gelu).astype(BF)
    two_ref[...] += dot(inner, wd_ref[...])
    gs_ref[...] += dot_nt(grad_gate, wg_ref[...]) + dot_nt(grad_up, wu_ref[...])
    width = second.shape[1]
    shard, shard_down = width // SHARDS, 2 * FF_TILE // SHARDS
    shape = (4, 4, shard, FF_TILE)
    part_gate = dot(second_t_ref[...], grad_gate).astype(BF).reshape(shape)
    part_up = dot(second_t_ref[...], grad_up).astype(BF).reshape(shape)
    part_down = dot_tn(inner, grad).astype(BF)
    for odd in range(2):
        @pl.when(step % 2 == odd)
        def _():
            part_ref[:, :, shard * odd:shard * (odd + 1), :] = part_gate
            part_ref[:, :, shard * (2 + odd):shard * (3 + odd), :] = part_up
            for tile in range(width // FF_TILE):
                at = 4 * shard + shard_down * tile
                part_ref[2 * odd:2 * odd + 2, :, at:at + shard_down, :] = (
                    part_down[:, FF_TILE * tile:FF_TILE * (tile + 1)].reshape(2, 4, shard_down, FF_TILE))


def ff_half(place, second, grad, w_gate, w_up, w_down, sums, after=()):
    rows, width = second.shape
    tiles = w_gate.shape[1] // FF_TILE // 2
    tile_at = lambda j, p: (j // 2) * 4 + p[0] * 2 + j % 2
    whole = lambda j, p: (0, 0)
    sum_spec = pl.BlockSpec((rows, width), whole)
    columns = pl.BlockSpec((width, FF_TILE), lambda j, p: (0, tile_at(j, p)))
    shard_rows = 4 * (width // SHARDS) + (2 * FF_TILE // SHARDS) * (width // FF_TILE)
    return pl.pallas_call(
        functools.partial(ff_kernel, sums is None),
        grid_spec=pltpu.PrefetchScalarGridSpec(
            num_scalar_prefetch=1,
            grid=(tiles,),
            in_specs=[
                pl.BlockSpec((rows, width), whole), pl.BlockSpec((rows, width), whole),
                columns, columns, pl.BlockSpec((FF_TILE, width), lambda j, p: (tile_at(j, p), 0)),
            ] + [sum_spec] * (0 if sums is None else 2) + [ANY] * len(after),
            out_specs=[sum_spec, sum_spec,
                       pl.BlockSpec((4, 4, shard_rows, FF_TILE), lambda j, p: (0, 0, j // 2, 0))],
            scratch_shapes=[pltpu.VMEM((width, rows), BF)],
        ),
        out_shape=[jax.ShapeDtypeStruct((rows, width), F32)] * 2
        + [jax.ShapeDtypeStruct((4, 4, 2 * shard_rows, FF_TILE), BF)],
        compiler_params=pltpu.CompilerParams(vmem_limit_bytes=VMEM_LIMIT),
        cost_estimate=pl.CostEstimate(
            flops=18 * rows * width * tiles * FF_TILE,
            bytes_accessed=12 * width * tiles * FF_TILE + 16 * rows * width,
            transcendentals=rows * tiles * FF_TILE),
    )(place, second, grad, w_gate, w_up, w_down, *(sums or ()), *after)


def split_kernel(place_ref, *refs):
    ins, outs = refs[:8], refs[-4:]
    for index, out in enumerate(outs):
        for step in range(4):
            at = jnp.bitwise_xor(place_ref[3], step)
            out[0, step] = (ins[index][0, 0, at].astype(F32) + ins[4 + index][0, 0, at].astype(F32)).astype(BF)


def split_cores(place, kept, got, after=()):
    tail = kept.shape[3:]

    def spec(order, away):
        def at(b, p):
            first, second = p[1 + order] ^ away, p[2 - order] ^ b
            return (order, first + 2 * second if order == 0 else second + 2 * first, 0, 0, 0)
        return pl.BlockSpec((1, 1, 4) + tail, at)

    specs = [spec(order, away) for order in range(2) for away in range(2)]
    out = pl.BlockSpec((1, 4) + tail, lambda b, p: (b, 0, 0, 0))
    return pl.pallas_call(
        split_kernel,
        grid_spec=pltpu.PrefetchScalarGridSpec(
            num_scalar_prefetch=1, grid=(2,), in_specs=specs * 2 + [ANY] * len(after), out_specs=[out] * 4),
        out_shape=[jax.ShapeDtypeStruct((2, 4) + tail, BF)] * 4,
        compiler_params=pltpu.CompilerParams(vmem_limit_bytes=VMEM_LIMIT),
        cost_estimate=pl.CostEstimate(flops=0, bytes_accessed=6 * kept.size, transcendentals=0),
    )(place, *([kept] * 4), *([got] * 4), *after)


def hold(array, after):
    return pl.pallas_call(
        lambda *refs: None,
        in_specs=[ANY] * (1 + len(after)),
        out_specs=ANY,
        out_shape=jax.ShapeDtypeStruct(array.shape, array.dtype),
        input_output_aliases={0: 0},
        cost_estimate=pl.CostEstimate(flops=0, bytes_accessed=0, transcendentals=0),
    )(array, *after)


def place_rows_kernel(place_ref, *refs):
    pieces, out_ref = refs[:-1], refs[-1]
    for step in range(GROUPS):
        out_ref[(place_ref[3] + step) % GROUPS] = pieces[step][...]
    for index in range(GROUPS, len(pieces)):
        out_ref[index] = pieces[index][...]


def place_rows(place, pieces):
    block = pl.BlockSpec(pieces[0].shape, lambda j, p: (0, 0))
    shape = (len(pieces),) + pieces[0].shape
    return pl.pallas_call(
        place_rows_kernel,
        grid_spec=pltpu.PrefetchScalarGridSpec(
            num_scalar_prefetch=1, grid=(1,), in_specs=[block] * len(pieces),
            out_specs=pl.BlockSpec(shape, lambda j, p: (0, 0, 0))),
        out_shape=jax.ShapeDtypeStruct(shape, pieces[0].dtype),
        cost_estimate=pl.CostEstimate(flops=0, bytes_accessed=0, transcendentals=0),
    )(place, *pieces)


def add_kernel(x_ref, rx_ref, y_ref, ry_ref, *refs):
    outs = refs[-4:]
    for index in range(2):
        outs[index][...] = add_low(x_ref[index], rx_ref[index])
        outs[2 + index][...] = add_low(y_ref[index], ry_ref[index])


def add_pairs(x, rx, y, ry, after=()):
    tail = x.shape[2:]
    return pl.pallas_call(
        add_kernel,
        grid=(4,),
        in_specs=[pl.BlockSpec((2, 1) + tail, lambda j: (0, j, 0, 0))] * 4 + [ANY] * len(after),
        out_specs=[pl.BlockSpec((1,) + tail, lambda j: (j, 0, 0))] * 4,
        out_shape=[jax.ShapeDtypeStruct((4,) + tail, BF)] * 4,
        compiler_params=pltpu.CompilerParams(vmem_limit_bytes=VMEM_LIMIT),
        cost_estimate=pl.CostEstimate(flops=0, bytes_accessed=12 * x.size, transcendentals=0),
    )(x, rx, y, ry, *after)


def add_four_kernel(x_ref, rx_ref, y_ref, ry_ref, *refs):
    outs = refs[-4:]
    for index in range(4):
        outs[index][0] = add_low(x_ref[index], rx_ref[index])
        outs[index][1] = add_low(y_ref[index], ry_ref[index])


def add_fours(x, rx, y, ry, after=()):
    tail = x.shape[1:]
    whole = pl.BlockSpec(x.shape, lambda j: (0, 0, 0))
    return pl.pallas_call(
        add_four_kernel,
        grid=(1,),
        in_specs=[whole] * 4 + [ANY] * len(after),
        out_specs=[pl.BlockSpec((2,) + tail, lambda j: (0, 0, 0))] * 4,
        out_shape=[jax.ShapeDtypeStruct((2,) + tail, BF)] * 4,
        compiler_params=pltpu.CompilerParams(vmem_limit_bytes=VMEM_LIMIT),
        cost_estimate=pl.CostEstimate(flops=0, bytes_accessed=12 * x.size, transcendentals=0),
    )(x, rx, y, ry, *after)


def sum_kernel(*refs):
    total = refs[0][...].astype(F32)
    for ref in refs[1:GROUPS]:
        total = total + ref[...].astype(F32)
    refs[-1][...] = total.astype(BF)


def sum_shards(shards, after=()):
    whole = pl.BlockSpec(shards[0].shape, lambda: (0, 0, 0))
    return pl.pallas_call(
        sum_kernel,
        in_specs=[whole] * GROUPS + [ANY] * len(after),
        out_specs=whole,
        out_shape=jax.ShapeDtypeStruct(shards[0].shape, BF),
        cost_estimate=pl.CostEstimate(flops=0, bytes_accessed=0, transcendentals=0),
    )(*shards, *after)


def stack_orders_kernel(*refs):
    for order in range(2):
        for index in range(GROUPS):
            refs[order - 2][index] = refs[index][order]


def stack_orders(pieces, after=()):
    tail = pieces[0].shape[1:]
    return pl.pallas_call(
        stack_orders_kernel,
        in_specs=[pl.BlockSpec((2,) + tail, lambda: (0, 0, 0))] * GROUPS + [ANY] * len(after),
        out_specs=[pl.BlockSpec((GROUPS,) + tail, lambda: (0, 0, 0))] * 2,
        out_shape=[jax.ShapeDtypeStruct((GROUPS,) + tail, BF)] * 2,
        cost_estimate=pl.CostEstimate(flops=0, bytes_accessed=0, transcendentals=0),
    )(*pieces, *after)


def stack_pairs_kernel(x_ref, rx_ref, y_ref, ry_ref, *refs):
    refs[-2][0] = x_ref[...]
    refs[-2][1] = rx_ref[...]
    refs[-1][0] = y_ref[...]
    refs[-1][1] = ry_ref[...]


def stack_pairs(x, rx, y, ry, after=()):
    tail = x.shape[1:]
    block = pl.BlockSpec((1,) + tail, lambda j: (j, 0, 0))
    return pl.pallas_call(
        stack_pairs_kernel,
        grid=(GROUPS,),
        in_specs=[block] * 4 + [ANY] * len(after),
        out_specs=[pl.BlockSpec((2, 1) + tail, lambda j: (0, j, 0, 0))] * 2,
        out_shape=[jax.ShapeDtypeStruct((2,) + x.shape, BF)] * 2,
        cost_estimate=pl.CostEstimate(flops=0, bytes_accessed=0, transcendentals=0),
    )(x, rx, y, ry, *after)


def grad_kernel(columns, place_ref, *refs):
    ins, part_ref = refs[:-1], refs[-1]
    for order, at, terms in columns:
        total = None
        for left, right in terms:
            term = dot_tn(ins[left][...], ins[right][...])
            total = term if total is None else total + term
        rows, cols = total.shape
        part_ref[order, :, :, :, at:at + cols] = total.astype(BF).reshape(4, 4, rows // SHARDS, cols)


def grad_part(place, ins, columns, after=()):
    specs = []
    for array, halved in ins:
        depth, cols = array.shape
        if halved:
            specs.append(pl.BlockSpec((depth, cols // 2), lambda j, p: (0, p[0])))
        else:
            specs.append(pl.BlockSpec((depth, cols), lambda j, p: (0, 0)))
    rows = ins[0][0].shape[1]
    shape = (2, 4, 4, rows // SHARDS, rows)
    return pl.pallas_call(
        functools.partial(grad_kernel, columns),
        grid_spec=pltpu.PrefetchScalarGridSpec(
            num_scalar_prefetch=1,
            grid=(1,),
            in_specs=specs + [ANY] * len(after),
            out_specs=pl.BlockSpec(shape, lambda j, p: (0, 0, 0, 0, 0)),
        ),
        out_shape=jax.ShapeDtypeStruct(shape, BF),
        compiler_params=pltpu.CompilerParams(vmem_limit_bytes=VMEM_LIMIT),
        cost_estimate=pl.CostEstimate(
            flops=sum(2 * rows * (rows // 2) * ins[left][0].shape[0]
                      for _, _, terms in columns for left, _ in terms),
            bytes_accessed=sum(2 * a.size for a, _ in ins), transcendentals=0),
    )(place, *[a for a, _ in ins], *after)


def from_pieces(place_ref, refs, order, group):
    here_ref, away_ref, other_here_ref, other_away_ref = refs[4 * order:4 * order + 4]
    quarter = pl.program_id(0)
    bit = quarter % 2 if order == 0 else quarter // 2
    near = place_ref[1 + order] == bit
    at = jnp.bitwise_xor(place_ref[3], group)
    own = jnp.where(near, here_ref[0, at], away_ref[0, at]).astype(F32)
    other = jnp.where(near, other_here_ref[0, at], other_away_ref[0, at]).astype(F32)
    lower = place_ref[0] == 0
    return jnp.where(lower, own, other), jnp.where(lower, other, own)


def assemble_ff_kernel(place_ref, own_ref, other_ref, gate_ref, up_ref, down_ref):
    shard, down = gate_ref.shape[0] // 4, down_ref.shape[2] // 4
    shard_rows = own_ref.shape[2] // 2

    def write(halves):
        for group in range(4):
            rows = slice(shard * group, shard * (group + 1))
            for half, source in enumerate(halves):
                for order in range(2):
                    base = order * shard_rows
                    for tile in range(2):
                        at = ((order * 2 + half) * 2 + tile) * FF_TILE
                        gate_ref[rows, at:at + FF_TILE] = source[
                            0, group, base + shard * tile:base + shard * (tile + 1)].astype(F32)
                        up_ref[rows, at:at + FF_TILE] = source[
                            0, group, base + shard * (2 + tile):base + shard * (3 + tile)].astype(F32)
                    for tile in range(down_ref.shape[3] // FF_TILE):
                        at = base + 4 * shard + down * tile
                        down_ref[order * 2 + half, 0, down * group:down * (group + 1),
                                 FF_TILE * tile:FF_TILE * (tile + 1)] = source[
                                     0, group, at:at + down].astype(F32)

    pl.when(place_ref[0] == 0)(lambda: write((own_ref, other_ref)))
    pl.when(place_ref[0] != 0)(lambda: write((other_ref, own_ref)))


def assemble_ff(place, own, other, hidden):
    quarter = lambda rows: pl.BlockSpec((rows, hidden), lambda q, p: (q, 0))
    part = pl.BlockSpec((1,) + own.shape[1:], lambda q, p: (q, 0, 0, 0))
    rows = own.shape[2] // 2
    width = (rows * FF_TILE * SHARDS * 4) // (3 * hidden)
    gate, up, down = pl.pallas_call(
        assemble_ff_kernel,
        grid_spec=pltpu.PrefetchScalarGridSpec(
            num_scalar_prefetch=1, grid=(4,), in_specs=[part, part],
            out_specs=[quarter(width // 4), quarter(width // 4),
                       pl.BlockSpec((4, 1, hidden // 16, width), lambda q, p: (0, q, 0, 0))]),
        out_shape=[jax.ShapeDtypeStruct((width, hidden), F32)] * 2
        + [jax.ShapeDtypeStruct((4, 4, hidden // 16, width), F32)],
        compiler_params=pltpu.CompilerParams(vmem_limit_bytes=VMEM_LIMIT),
        cost_estimate=pl.CostEstimate(flops=0, bytes_accessed=12 * own.size, transcendentals=0),
    )(place, own, other)
    return gate, up, down.reshape(hidden, width)


def assemble_kernel(place_ref, *refs):
    outs = refs[-4:]
    shard = outs[0].shape[0] // 4
    for order in range(2):
        for group in range(4):
            rows = slice(shard * group, shard * (group + 1))
            for half, value in enumerate(from_pieces(place_ref, refs, order, group)):
                width = value.shape[1] // 2
                for which in range(2):
                    outs[2 * order + which][rows, half * width:(half + 1) * width] = (
                        value[:, which * width:(which + 1) * width])


def assemble(kernel, place, pieces, out_shapes, out_specs, after=()):
    tail = pieces[0].shape[1:]
    near = pl.BlockSpec((1,) + tail, lambda q, p: (p[2] ^ (q // 2), 0, 0, 0))
    far = pl.BlockSpec((1,) + tail, lambda q, p: (p[1] ^ (q % 2), 0, 0, 0))
    return pl.pallas_call(
        kernel,
        grid_spec=pltpu.PrefetchScalarGridSpec(
            num_scalar_prefetch=1, grid=(4,), in_specs=[near] * 4 + [far] * 4 + [ANY] * len(after),
            out_specs=out_specs),
        out_shape=[jax.ShapeDtypeStruct(shape, F32) for shape in out_shapes],
        compiler_params=pltpu.CompilerParams(vmem_limit_bytes=VMEM_LIMIT),
        cost_estimate=pl.CostEstimate(
            flops=0, bytes_accessed=16 * 8 * pieces[0].size // 4, transcendentals=0),
    )(place, *pieces, *after)


def add_low(left, right):
    return (left.astype(F32) + right.astype(F32)).astype(BF)


def norm_scale(values):
    return lax.rsqrt(jnp.mean(values * values, axis=-1, keepdims=True) + EPS)


def norm_back(values, gain, grad):
    scale = norm_scale(values)
    scaled = values * scale
    weighted = grad * gain
    inner = jnp.mean(weighted * scaled, axis=-1, keepdims=True)
    return scale * (weighted - scaled * inner), jnp.sum(grad * scaled, axis=0)


def masked_squares(values_in, row_mask):
    return jnp.sum(row_mask * jnp.sum(values_in * values_in, axis=-1))


def body(n_img, n_seq, patches, counts, norm_gain_one, w_query, w_key, w_value, w_out,
         norm_gain_two, w_gate, w_up, w_down, cotangent):
    charts, block_len, width = patches.shape
    members = n_seq // GROUPS
    head_count = HEADS // members
    pairs = -(-head_count // 2)
    pad_cols = pairs * 128 - head_count * 64
    mine_cols = head_count * 64
    main_own = GROUPS * block_len
    seq_len = n_seq * block_len
    here = lax.axis_index("seq")
    group, member = here // members, here % members
    img_here = lax.axis_index("img")

    def slot_of(who):
        return (who % 2) * (members // 2) + who // 2

    def bit_exchange(axis, bit):
        def move(array):
            if axis == "img":
                perm = [(i, i ^ (1 << bit)) for i in range(n_img)]
            elif axis == "group":
                perm = [(g * members + r, (g ^ (1 << bit)) * members + r)
                        for g in range(GROUPS) for r in range(members)]
            else:
                perm = [(g * members + r, g * members + (r ^ (1 << bit)))
                        for g in range(GROUPS) for r in range(members)]
            return lax.ppermute(array, "img" if axis == "img" else "seq", perm)
        return move

    img_moves = [bit_exchange("img", 0), bit_exchange("img", 1)]
    z_moves = [bit_exchange("group", 0), bit_exchange("group", 1)]

    def z_move(array, step):
        perm = [(g * members + r, (g ^ step) * members + r) for g in range(GROUPS) for r in range(members)]
        return lax.ppermute(array, "seq", perm)

    core_move = bit_exchange("member", 0)
    more_moves = [bit_exchange("img", b) for b in range(2, n_img.bit_length() - 1)]
    more_moves += [bit_exchange("member", b) for b in range(1, members.bit_length() - 1)]
    img_bits = [img_here % 2, (img_here // 2) % 2]
    half_here = member % 2

    def place_of(half):
        return jnp.stack([half] + img_bits + [group]).astype(jnp.int32)

    there, here_place = place_of(1 - half_here), place_of(half_here)

    def sum_img_first(kx, sx, ky, sy, after=()):
        return add_pairs(kx, img_moves[0](sx), ky, img_moves[1](sy), after)

    def sum_img_second(kx, sx, ky, sy, after=()):
        return add_fours(kx, img_moves[1](sx), ky, img_moves[0](sy), after)

    def sum_groups(shards, after=()):
        total = sum_shards(
            [shards[0]] + [z_move(shards[step], step) for step in range(1, GROUPS)], after)
        for move in more_moves:
            total = add_low(total, move(total))
        return total

    def quarters(total, after):
        return stack_orders([total] + [z_move(total, step) for step in range(1, GROUPS)], after)

    def halves(parts, after):
        return stack_pairs(parts[0], img_moves[1](parts[0]), parts[1], img_moves[0](parts[1]), after)

    def far_halves(near, after):
        far = [img_moves[order](near[order]) for order in range(2)]
        return [hold(f, after) for f in far] if after else far

    def every_piece(near, far):
        return [a for n, f in zip(near, far) for a in (n, f, core_move(n), core_move(f))]

    def shift_perm(step):
        return [(g * members + r, ((g + step) % GROUPS) * members + r)
                for g in range(GROUPS) for r in range(members)]

    def member_perm(step):
        return [(g * members + r, g * members + (r ^ step))
                for g in range(GROUPS) for r in range(members)]

    def to_groups(array, after=()):
        pieces = []
        for step in range(GROUPS):
            part = lax.dynamic_index_in_dim(array, (group + step) % GROUPS, 0, keepdims=False)
            if step:
                part = lax.ppermute(hold(part, after) if after else part, "seq", shift_perm(step))
            pieces.append(part)
        return pieces

    def from_groups(rows):
        pieces = []
        for step in range(GROUPS):
            part = rows[step * block_len:(step + 1) * block_len]
            pieces.append(part if step == 0 else lax.ppermute(part, "seq", shift_perm(-step)))
        return place_rows(here_place, pieces + [rows[main_own:]])

    def to_members(own):
        return [own] + [lax.ppermute(own, "seq", member_perm(step)) for step in range(1, members)]

    def columns_of(weight, who):
        part = lax.dynamic_slice_in_dim(weight, who * mine_cols, mine_cols, 1)
        return jnp.pad(part, ((0, 0), (0, pad_cols))) if pad_cols else part

    gain_one = norm_gain_one.astype(F32)
    gain_two = norm_gain_two.astype(F32)
    steps = jnp.arange(GROUPS, dtype=jnp.int32)
    block_of = ((group - steps) % GROUPS) * members
    inside = jnp.arange(block_len, dtype=jnp.int32)

    def main_positions(who):
        return ((block_of + who) * block_len)[:, None] + inside[None, :]

    count_main = lax.dynamic_index_in_dim(counts, group, 0, keepdims=False)
    count_rest = counts[GROUPS]
    rest_positions = here * block_len + inside
    row_valid = jnp.concatenate([
        (main_positions(member) < count_main).reshape(-1), rest_positions < count_rest])
    row_mask = row_valid.astype(F32)
    key_positions = jnp.concatenate(
        [main_positions(member ^ step).reshape(-1) for step in range(members)])

    def key_extras(valid):
        bias = jnp.where(valid, 0.0, NEG)[:, None]
        lane = jnp.arange(128)[None, :]
        return jnp.where(lane < 3, 1.0, jnp.where(lane == 3, bias, 0.0)).astype(BF)

    ext_main = key_extras(key_positions < count_main)
    ext_rest = key_extras(jnp.arange(seq_len) < count_rest)

    rest_rows = patches[GROUPS]
    rest_f32 = rest_rows.astype(F32)
    first_rest = (rest_f32 * norm_scale(rest_f32) * gain_one).astype(BF)
    moved = to_groups(patches)
    main_rows = jnp.concatenate(moved, axis=0).astype(F32)
    first_main = (main_rows * norm_scale(main_rows) * gain_one).astype(BF)
    first_all = jnp.concatenate(to_members(first_main), axis=0)
    first_rest_sent, _ = lax.optimization_barrier((first_rest, first_main))
    first_rest_all = lax.all_gather(first_rest_sent, "seq", axis=0, tiled=True)

    place = jnp.reshape(slot_of(member), (1,)).astype(jnp.int32)
    zero_place = jnp.zeros((1,), jnp.int32)
    if pad_cols:
        main_weights = [columns_of(w, slot_of(member)) for w in (w_query, w_key, w_value)]
        main_place = zero_place
    else:
        main_weights = [w_query, w_key, w_value]
        main_place = place
    q_rows = min(128, block_len)
    query_main, key_main, value_main, logs_main, attn_main = attend(
        main_place, first_all, first_all, *main_weights, ext_main, pairs, q_rows)
    query_rest, key_rest, value_rest, logs_rest, attn_rest = attend(
        zero_place, first_rest, first_rest_all, w_query, w_key, w_value, ext_rest,
        HEADS // 2, q_rows, (attn_main,))
    grad_moved = to_groups(cotangent, (attn_main,))
    grad_low = jnp.concatenate([hold(g, (attn_rest,)) for g in grad_moved] + [cotangent[GROUPS]], axis=0)

    def swap_in(array):
        pieces = []
        for step in range(members):
            part = array[step * main_own:(step + 1) * main_own, :mine_cols]
            pieces.append(part if step == 0 else lax.ppermute(part, "seq", member_perm(step)))
        out = jnp.zeros((main_own, width), array.dtype)
        for step in range(members):
            out = lax.dynamic_update_slice_in_dim(out, pieces[step], slot_of(member ^ step) * mine_cols, 1)
        return out

    attn_in = jnp.concatenate([swap_in(attn_main), attn_rest], axis=0)
    resid = jnp.concatenate([main_rows, rest_f32], axis=0)
    branch_one = dot(attn_in, w_out)
    middle = resid + branch_one
    second_in = (middle * norm_scale(middle) * gain_two).astype(BF)
    ff_ins = (second_in, grad_low, w_gate, w_up, w_down)
    sums_two, sums_gs, ff_sent = ff_half(there, *ff_ins, None)
    branch_two, grad_second, ff_kept = ff_half(here_place, *ff_ins, (sums_two, sums_gs))
    ff_now = add_low(ff_kept, core_move(ff_sent))
    img_fours = [list(range(i, i + 4)) for i in range(0, n_img, 4)]
    same_member = [[g * members + r for g in range(GROUPS)] for r in range(members)]
    ff_quarter = lax.psum_scatter(ff_now, "img", scatter_dimension=0, axis_index_groups=img_fours)
    branch_two = hold(branch_two, (ff_now,))
    result = middle + branch_two
    squares = jnp.stack([masked_squares(v, row_mask) for v in (resid, branch_one, branch_two, result)])
    valid_count = jnp.sum(row_mask)
    result_low = result.astype(BF)
    layer_out = from_groups(result_low)
    grad_out = grad_low.astype(F32)
    grad_second = hold(grad_second, (ff_now,))
    grad_mid_norm, grad_gain_two = norm_back(middle, gain_two, grad_second)
    grad_mid = grad_out + grad_mid_norm
    grad_mid_low = grad_mid.astype(BF)

    main_grads = []
    for step in range(members):
        rows_of = lax.dynamic_slice_in_dim(w_out, slot_of(member ^ step) * mine_cols, mine_cols, 0)
        part = dot_nt(grad_mid_low[:main_own], rows_of).astype(BF)
        if pad_cols:
            part = jnp.pad(part, ((0, 0), (0, pad_cols)))
        main_grads.append(part if step == 0 else lax.ppermute(part, "seq", member_perm(step)))
    grad_attn_main = jnp.concatenate(main_grads, axis=0)
    grad_attn_rest = dot_nt(grad_mid_low[main_own:], w_out).astype(BF)

    dq_rest, dk_rest, dv_rest = attend_back(
        query_rest, key_rest, value_rest, ext_rest, logs_rest, attn_rest, grad_attn_rest, q_rows)
    first_part_rest = (dot_nt(dk_rest, w_key) + dot_nt(dv_rest, w_value)).astype(BF)
    by_owner = first_part_rest.reshape(GROUPS, members, block_len, width)
    first_sum_rest = lax.dynamic_index_in_dim(by_owner, member, 1, keepdims=False).astype(F32)
    for step in range(1, members):
        part = lax.dynamic_index_in_dim(by_owner, member ^ step, 1, keepdims=False)
        first_sum_rest = first_sum_rest + lax.ppermute(part, "seq", member_perm(step)).astype(F32)
    by_owner = first_sum_rest.astype(BF)
    first_sum_rest = lax.dynamic_index_in_dim(by_owner, group, 0, keepdims=False).astype(F32)
    for step in range(1, GROUPS):
        part = lax.dynamic_index_in_dim(by_owner, group ^ step, 0, keepdims=False)
        first_sum_rest = first_sum_rest + z_move(part, step).astype(F32)
    half_width = width // 2
    rest_ins = [(first_rest, False), (dq_rest, True), (first_rest_all, False), (dk_rest, True),
                (dv_rest, True), (attn_in, False), (grad_mid_low, True)]
    qkv_sent = grad_part(there, rest_ins, [
        (0, 0, [(0, 1)]), (0, half_width, [(5, 6)]), (1, 0, [(2, 3)]), (1, half_width, [(2, 4)])],
        (first_part_rest,))
    dq_main, dk_main, dv_main = attend_back(
        query_main, key_main, value_main, ext_main, logs_main, attn_main, grad_attn_main,
        min(256, block_len * 2), (qkv_sent, layer_out))

    main_parts = [(dq_main, w_query), (dk_main, w_key), (dv_main, w_value)]
    def in_half(part):
        part = part[:, :mine_cols]
        if mine_cols == width // 2:
            return part
        empty = jnp.zeros((part.shape[0], width // 2), part.dtype)
        return lax.dynamic_update_slice_in_dim(empty, part, (member // 2) * mine_cols, 1)

    main_ins = [(first_all, False), (in_half(dq_main), False), (in_half(dk_main), False),
                (in_half(dv_main), False)]
    qkv_kept = grad_part(here_place, rest_ins + main_ins, [
        (0, 0, [(0, 1), (7, 8)]), (0, half_width, [(5, 6)]),
        (1, 0, [(2, 3), (7, 9)]), (1, half_width, [(2, 4), (7, 10)])])
    qkv_now = split_cores(here_place, qkv_kept, core_move(qkv_sent))
    main_parts = [(hold(part, qkv_now), w) for part, w in main_parts]
    first_part_main = sum(
        dot_nt(part[:, :mine_cols], lax.dynamic_slice_in_dim(w, slot_of(member) * mine_cols, mine_cols, 1))
        for part, w in main_parts)
    grad_first_main = first_part_main[:main_own]
    for step in range(1, members):
        part = first_part_main[step * main_own:(step + 1) * main_own].astype(BF)
        grad_first_main = grad_first_main + lax.ppermute(part, "seq", member_perm(step)).astype(F32)
    grad_first_rest = dot_nt(dq_rest, w_query) + first_sum_rest
    grad_first = jnp.concatenate([grad_first_main, grad_first_rest], axis=0)

    qkv_now = sum_img_first(*qkv_now)
    ff_quarter = hold(ff_quarter, (dq_main,))
    ff_shard = lax.psum_scatter(ff_quarter, "seq", scatter_dimension=0, axis_index_groups=same_member)
    for move in more_moves:
        ff_shard = add_low(ff_shard, move(ff_shard))
    ff_shard = hold(ff_shard, (first_part_main,))
    ff_groups = lax.all_gather(ff_shard, "seq", axis=0, axis_index_groups=same_member)
    grad_resid_norm, grad_gain_one = norm_back(resid, gain_one, grad_first)
    grad_input_rows = (grad_mid + grad_resid_norm).astype(BF)
    grad_input = from_groups(grad_input_rows)
    qkv_now = sum_img_second(*qkv_now)
    ff_groups = hold(ff_groups, qkv_now)
    ff_own = lax.all_gather(ff_groups, "img", axis=0, axis_index_groups=img_fours)
    qkv_near = halves(quarters(sum_groups(qkv_now), ()), (grad_input,))
    ff_own = hold(ff_own, qkv_near)
    sum_gate, sum_up, sum_down = assemble_ff(here_place, ff_own, core_move(ff_own), w_gate.shape[1])
    sum_query, sum_out, sum_key, sum_value = assemble(
        assemble_kernel, here_place, every_piece(qkv_near, far_halves(qkv_near, ())), [(width, width)] * 4,
        [pl.BlockSpec((width // 4, width), lambda q, p: (q, 0))] * 4)

    small = jnp.concatenate([grad_gain_one, grad_gain_two, squares, valid_count[None]])
    small = jnp.pad(small, (0, -small.size % 1024)).reshape(-1, 128)
    for move in z_moves + [core_move] + img_moves + more_moves:
        small = small + move(small)
    small = small.reshape(-1)
    sum_gain_one, sum_gain_two = small[:width], small[width:2 * width]
    sum_squares, sum_count = small[2 * width:2 * width + 4], small[2 * width + 4]
    rms_stats = jnp.sqrt(sum_squares / (sum_count * width))
    return (layer_out, grad_input, sum_gain_one, sum_query, sum_key, sum_value, sum_out,
            sum_gain_two, sum_gate, sum_up, sum_down, rms_stats)


def solution(mesh):
    rows = P("img", "seq", None)
    return jax.shard_map(
        functools.partial(body, mesh.shape["img"], mesh.shape["seq"]),
        mesh=mesh,
        in_specs=(rows, P("img"), P(), P(), P(), P(), P(), P(), P(), P(), P(), rows),
        out_specs=(rows, rows, P(), P(), P(), P(), P(), P(), P(), P(), P(), P()),
        check_vma=False,
    )
```

```python
import functools
import math

import jax
import jax.numpy as jnp
from jax import lax
from jax.experimental import pallas as pl
from jax.experimental.pallas import tpu as pltpu
from jax.sharding import PartitionSpec as P

HEADS = 12
GROUPS = 4
SHARDS = 16
EPS = 1e-06
NEG = -1000000000.0
LOG2E = 1.4426950408889634
LN2 = 0.6931471805599453
GELU_C = 0.7978845608028654
GELU_A = 0.044715
BF = jnp.bfloat16
F32 = jnp.float32
VMEM_LIMIT = 56 * 1024 * 1024
ANY = pl.BlockSpec(memory_space=pl.ANY)


def dot(left, right):
    return jnp.dot(left, right, preferred_element_type=F32)


def dot_nt(left, right):
    return lax.dot_general(left, right, (((1,), (1,)), ((), ())), preferred_element_type=F32)


def dot_tn(left, right):
    return lax.dot_general(left, right, (((0,), (0,)), ((), ())), preferred_element_type=F32)


def split_three(column):
    hi = column.astype(BF).astype(F32)
    rest = column - hi
    mid = rest.astype(BF).astype(F32)
    return hi, mid, rest - mid


def extras(rows, columns):
    lane = lax.broadcasted_iota(jnp.int32, (rows, 128), 1)
    out = jnp.zeros((rows, 128), F32)
    for index, column in enumerate(columns):
        if column is not None:
            out = jnp.where(lane == index, column, out)
    return out.astype(BF)


def head_lanes(values, half):
    lane = lax.broadcasted_iota(jnp.int32, values.shape, 1)
    return jnp.where((lane < 64) if half == 0 else (lane >= 64), values, jnp.zeros_like(values))


def stack_heads(values):
    return jnp.concatenate([head_lanes(values, 0), head_lanes(values, 1)], axis=0)


def attend_kernel(q_rows, place_ref, fiq_ref, fik_ref, wq_ref, wk_ref, wv_ref, ext_ref, *refs):
    q_ref, k_ref, v_ref, log_ref, out_ref = refs[-5:]
    scale = LOG2E / math.sqrt(64.0)
    both = dot(fik_ref[...], jnp.concatenate([wk_ref[...], wv_ref[...]], axis=1)).astype(BF)
    k_ref[0] = both[:, :128]
    v_ref[0] = both[:, 128:]
    query = (dot(fiq_ref[...], wq_ref[...]) * scale).astype(BF)
    q_ref[0] = query
    ext = ext_ref[...]
    keys = jnp.concatenate([both[:, :128], ext], axis=1)
    values = jnp.concatenate([both[:, 128:], ext], axis=1)
    one = extras(2 * q_rows, (None, None, None, 1.0))
    for start in range(0, fiq_ref.shape[0], q_rows):
        rows = slice(start, start + q_rows)
        scores = dot_nt(jnp.concatenate([stack_heads(query[rows]), one], axis=1), keys)
        top = jnp.max(scores, axis=1, keepdims=True)
        weights = jnp.exp2(scores - top).astype(BF)
        mixed = dot(weights, values)
        norm = mixed[:, 128:129]
        logs = extras(2 * q_rows, split_three(-(top + jnp.log2(norm))) + (1.0,))
        log_ref[0, rows, :] = logs[:q_rows]
        log_ref[1, rows, :] = logs[q_rows:]
        scaled = mixed[:, :128] / norm
        lane = lax.broadcasted_iota(jnp.int32, (q_rows, 128), 1)
        out_ref[rows, :] = jnp.where(lane < 64, scaled[:q_rows], scaled[q_rows:]).astype(BF)


def attend(place, fi_q, fi_k, w_query, w_key, w_value, ext, pairs, q_rows, after=()):
    q_total, width = fi_q.shape
    k_total = fi_k.shape[0]
    column = lambda i, p: (0, p[0] * pairs + i)
    whole = lambda i, p: (0, 0)
    stacked = lambda i, p: (i, 0, 0)
    return pl.pallas_call(
        functools.partial(attend_kernel, q_rows),
        grid_spec=pltpu.PrefetchScalarGridSpec(
            num_scalar_prefetch=1,
            grid=(pairs,),
            in_specs=[
                pl.BlockSpec((q_total, width), whole),
                pl.BlockSpec((k_total, width), whole),
                pl.BlockSpec((width, 128), column),
                pl.BlockSpec((width, 128), column),
                pl.BlockSpec((width, 128), column),
                pl.BlockSpec((k_total, 128), whole),
            ] + [ANY] * len(after),
            out_specs=[
                pl.BlockSpec((1, q_total, 128), stacked),
                pl.BlockSpec((1, k_total, 128), stacked),
                pl.BlockSpec((1, k_total, 128), stacked),
                pl.BlockSpec((2, q_total, 128), stacked),
                pl.BlockSpec((q_total, 128), lambda i, p: (0, i)),
            ],
        ),
        out_shape=[
            jax.ShapeDtypeStruct((pairs, q_total, 128), BF),
            jax.ShapeDtypeStruct((pairs, k_total, 128), BF),
            jax.ShapeDtypeStruct((pairs, k_total, 128), BF),
            jax.ShapeDtypeStruct((2 * pairs, q_total, 128), BF),
            jax.ShapeDtypeStruct((q_total, pairs * 128), BF),
        ],
        compiler_params=pltpu.CompilerParams(vmem_limit_bytes=VMEM_LIMIT),
        cost_estimate=pl.CostEstimate(
            flops=4 * 128 * pairs * (4 * q_total * k_total + width * (q_total + 2 * k_total)),
            bytes_accessed=2 * (q_total + k_total) * width * 4,
            transcendentals=2 * pairs * q_total * k_total,
        ),
    )(place, fi_q, fi_k, w_query, w_key, w_value, ext, *after)


def attend_back_kernel(q_rows, own_rows, place_ref, q_ref, k_ref, v_ref, ext_ref, log_ref, out_ref,
                       grad_ref, wq_ref, wk_ref, wv_ref, *refs):
    dq_ref, dk_ref, dv_ref, own_ref, far_ref, sum_q, sum_k = refs[-7:]
    del place_ref
    step = pl.program_id(0)

    @pl.when(step == 0)
    def _():
        if not own_rows:
            sum_q[...] = jnp.zeros_like(sum_q)
        sum_k[...] = jnp.zeros_like(sum_k)

    ext = ext_ref[...]
    key_pair = k_ref[0]
    keys = jnp.concatenate([key_pair, ext], axis=1)
    values = jnp.concatenate([v_ref[0], ext], axis=1)
    keys_trans = jnp.transpose(key_pair.astype(F32)).astype(BF)
    dk_sum = jnp.zeros(key_pair.shape, F32)
    dv_sum = jnp.zeros(key_pair.shape, F32)
    for start in range(0, q_ref.shape[1], q_rows):
        rows = slice(start, start + q_rows)
        grad = grad_ref[rows, :]
        product = grad.astype(F32) * out_ref[rows, :].astype(F32)
        delta = jnp.sum(stack_heads(product), axis=1, keepdims=True)
        grad_h = stack_heads(grad)
        query_h = stack_heads(q_ref[0, rows, :])
        logs = jnp.concatenate([log_ref[0, rows, :], log_ref[1, rows, :]], axis=0)
        probs = jnp.exp2(dot_nt(keys, jnp.concatenate([query_h, logs], axis=1)))
        centred = dot_nt(values, jnp.concatenate([grad_h, extras(2 * q_rows, split_three(-delta))], axis=1))
        grad_scores = (probs * centred).astype(BF)
        dv_sum = dv_sum + dot(probs.astype(BF), grad_h)
        dk_sum = dk_sum + dot(grad_scores, query_h)
        first = dot(keys_trans[:64], grad_scores[:, :q_rows])
        second = dot(keys_trans[64:], grad_scores[:, q_rows:])
        dq_ref[rows, :] = (jnp.transpose(jnp.concatenate([first, second], axis=0)) * 0.125).astype(BF)
    dk = (dk_sum * LN2).astype(BF)
    dv = dv_sum.astype(BF)
    dk_ref[...] = dk
    dv_ref[...] = dv
    if own_rows:
        sum_k[...] += dot_nt(
            jnp.concatenate([dq_ref[...], dk, dv], axis=1),
            jnp.concatenate([wq_ref[...], wk_ref[...], wv_ref[...]], axis=1))
    else:
        sum_q[...] += dot_nt(dq_ref[...], wq_ref[...])
        sum_k[...] += dot_nt(
            jnp.concatenate([dk, dv], axis=1), jnp.concatenate([wk_ref[...], wv_ref[...]], axis=1))

    @pl.when(step == pl.num_programs(0) - 1)
    def _():
        if own_rows:
            own_ref[...] = sum_k[:own_rows]
            far_ref[...] = sum_k[own_rows:].astype(BF)
        else:
            own_ref[...] = sum_q[...]
            far_ref[...] = sum_k[...].astype(BF)


def attend_back(place, query, key, value, ext, logs, out, grad, weights, q_rows, own_rows, after=()):
    pairs, q_total, _ = query.shape
    k_total = key.shape[1]
    width = weights[0].shape[0]
    stacked = lambda i, p: (i, 0, 0)
    flat = lambda i, p: (0, i)
    whole = lambda i, p: (0, 0)
    column = pl.BlockSpec((width, 128), lambda i, p: (0, p[0] * pairs + i))
    shapes = [(own_rows, width), (k_total - own_rows, width)] if own_rows else [(q_total, width), (k_total, width)]
    return pl.pallas_call(
        functools.partial(attend_back_kernel, q_rows, own_rows),
        grid_spec=pltpu.PrefetchScalarGridSpec(
            num_scalar_prefetch=1,
            grid=(pairs,),
            in_specs=[
                pl.BlockSpec((1, q_total, 128), stacked),
                pl.BlockSpec((1, k_total, 128), stacked),
                pl.BlockSpec((1, k_total, 128), stacked),
                pl.BlockSpec((k_total, 128), whole),
                pl.BlockSpec((2, q_total, 128), stacked),
                pl.BlockSpec((q_total, 128), flat),
                pl.BlockSpec((q_total, 128), flat),
                column, column, column,
            ] + [ANY] * len(after),
            out_specs=[
                pl.BlockSpec((q_total, 128), flat),
                pl.BlockSpec((k_total, 128), flat),
                pl.BlockSpec((k_total, 128), flat),
                pl.BlockSpec(shapes[0], whole),
                pl.BlockSpec(shapes[1], whole),
            ],
            scratch_shapes=[
                pltpu.VMEM((8 if own_rows else q_total, width), F32), pltpu.VMEM((k_total, width), F32)],
        ),
        out_shape=[
            jax.ShapeDtypeStruct((q_total, pairs * 128), BF),
            jax.ShapeDtypeStruct((k_total, pairs * 128), BF),
            jax.ShapeDtypeStruct((k_total, pairs * 128), BF),
            jax.ShapeDtypeStruct(shapes[0], F32),
            jax.ShapeDtypeStruct(shapes[1], BF),
        ],
        compiler_params=pltpu.CompilerParams(vmem_limit_bytes=VMEM_LIMIT),
        cost_estimate=pl.CostEstimate(
            flops=2 * 256 * pairs * 5 * q_total * k_total,
            bytes_accessed=2 * 128 * pairs * (4 * q_total + 4 * k_total),
            transcendentals=2 * pairs * q_total * k_total,
        ),
    )(place, query, key, value, ext, logs, out, grad, *weights, *after)


FF_TILE = 256
FF_STEP = 512


def ff_kernel(first, place_ref, second_ref, grad_ref, wg_ref, wu_ref, wd_ref, *refs):
    two_ref, gs_ref, part_ref, second_t_ref = refs[-4:]
    step = pl.program_id(0)

    @pl.when(step == 0)
    def _():
        second_t_ref[...] = jnp.transpose(second_ref[...])
        if first:
            two_ref[...] = jnp.zeros_like(two_ref)
            gs_ref[...] = jnp.zeros_like(gs_ref)
        else:
            two_ref[...] = refs[0][...]
            gs_ref[...] = refs[1][...]

    second, grad = second_ref[...], grad_ref[...]
    gate = dot(second, wg_ref[...])
    up = dot(second, wu_ref[...])
    grad_inner = dot_nt(grad, wd_ref[...])
    square = gate * gate
    half_plus = 0.5 + 0.5 * jnp.tanh(gate * (GELU_C + (GELU_C * GELU_A) * square))
    gelu = gate * half_plus
    slope = half_plus + gelu * (1.0 - half_plus) * (2.0 * GELU_C + (6.0 * GELU_C * GELU_A) * square)
    inner = (gelu * up).astype(BF)
    grad_gate = (grad_inner * up * slope).astype(BF)
    grad_up = (grad_inner * gelu).astype(BF)
    two_ref[...] += dot(inner, wd_ref[...])
    gs_ref[...] += dot_nt(grad_gate, wg_ref[...]) + dot_nt(grad_up, wu_ref[...])
    width = second.shape[1]
    shard, shard_down = width // SHARDS, 2 * FF_TILE // SHARDS
    part_gate = dot(second_t_ref[...], grad_gate).astype(BF)
    part_up = dot(second_t_ref[...], grad_up).astype(BF)
    part_down = dot_tn(inner, grad).astype(BF)
    shape = (4, 4, shard, FF_TILE)
    for odd in range(FF_STEP // FF_TILE):
        here = slice(FF_TILE * odd, FF_TILE * (odd + 1))
        part_ref[:, :, shard * odd:shard * (odd + 1), :] = part_gate[:, here].reshape(shape)
        part_ref[:, :, shard * (2 + odd):shard * (3 + odd), :] = part_up[:, here].reshape(shape)
        for tile in range(width // FF_TILE):
            at = 4 * shard + shard_down * tile
            part_ref[2 * odd:2 * odd + 2, :, at:at + shard_down, :] = (
                part_down[here, FF_TILE * tile:FF_TILE * (tile + 1)].reshape(2, 4, shard_down, FF_TILE))


def ff_half(place, second, grad, w_gate, w_up, w_down, sums, after=()):
    rows, width = second.shape
    tiles = w_gate.shape[1] // FF_STEP // 2
    tile_at = lambda j, p: j * 2 + p[0]
    whole = lambda j, p: (0, 0)
    sum_spec = pl.BlockSpec((rows, width), whole)
    columns = pl.BlockSpec((width, FF_STEP), lambda j, p: (0, tile_at(j, p)))
    shard_rows = 4 * (width // SHARDS) + (2 * FF_TILE // SHARDS) * (width // FF_TILE)
    return pl.pallas_call(
        functools.partial(ff_kernel, sums is None),
        grid_spec=pltpu.PrefetchScalarGridSpec(
            num_scalar_prefetch=1,
            grid=(tiles,),
            in_specs=[
                pl.BlockSpec((rows, width), whole), pl.BlockSpec((rows, width), whole),
                columns, columns, pl.BlockSpec((FF_STEP, width), lambda j, p: (tile_at(j, p), 0)),
            ] + [sum_spec] * (0 if sums is None else 2) + [ANY] * len(after),
            out_specs=[sum_spec, sum_spec,
                       pl.BlockSpec((4, 4, shard_rows, FF_TILE), lambda j, p: (0, 0, j, 0))],
            scratch_shapes=[pltpu.VMEM((width, rows), BF)],
        ),
        out_shape=[jax.ShapeDtypeStruct((rows, width), F32)] * 2
        + [jax.ShapeDtypeStruct((4, 4, 2 * shard_rows, FF_TILE), BF)],
        compiler_params=pltpu.CompilerParams(vmem_limit_bytes=VMEM_LIMIT),
        cost_estimate=pl.CostEstimate(
            flops=18 * rows * width * tiles * FF_STEP,
            bytes_accessed=12 * width * tiles * FF_STEP + 16 * rows * width,
            transcendentals=rows * tiles * FF_STEP),
    )(place, second, grad, w_gate, w_up, w_down, *(sums or ()), *after)


def split_kernel(place_ref, *refs):
    ins, outs = refs[:8], refs[-4:]
    for index, out in enumerate(outs):
        for step in range(4):
            at = jnp.bitwise_xor(place_ref[3], step)
            out[0, step] = (ins[index][0, 0, at].astype(F32) + ins[4 + index][0, 0, at].astype(F32)).astype(BF)


def split_cores(place, kept, got, after=()):
    tail = kept.shape[3:]

    def spec(order, away):
        def at(b, p):
            first, second = p[1 + order] ^ away, p[2 - order] ^ b
            return (order, first + 2 * second if order == 0 else second + 2 * first, 0, 0, 0)
        return pl.BlockSpec((1, 1, 4) + tail, at)

    specs = [spec(order, away) for order in range(2) for away in range(2)]
    out = pl.BlockSpec((1, 4) + tail, lambda b, p: (b, 0, 0, 0))
    return pl.pallas_call(
        split_kernel,
        grid_spec=pltpu.PrefetchScalarGridSpec(
            num_scalar_prefetch=1, grid=(2,), in_specs=specs * 2 + [ANY] * len(after), out_specs=[out] * 4),
        out_shape=[jax.ShapeDtypeStruct((2, 4) + tail, BF)] * 4,
        compiler_params=pltpu.CompilerParams(vmem_limit_bytes=VMEM_LIMIT),
        cost_estimate=pl.CostEstimate(flops=0, bytes_accessed=6 * kept.size, transcendentals=0),
    )(place, *([kept] * 4), *([got] * 4), *after)


def hold(array, after):
    return pl.pallas_call(
        lambda *refs: None,
        in_specs=[ANY] * (1 + len(after)),
        out_specs=ANY,
        out_shape=jax.ShapeDtypeStruct(array.shape, array.dtype),
        input_output_aliases={0: 0},
        cost_estimate=pl.CostEstimate(flops=0, bytes_accessed=0, transcendentals=0),
    )(array, *after)


def hold_all(arrays, after=()):
    return pl.pallas_call(
        lambda *refs: None,
        in_specs=[ANY] * (len(arrays) + len(after)),
        out_specs=[ANY] * len(arrays),
        out_shape=[jax.ShapeDtypeStruct(a.shape, a.dtype) for a in arrays],
        input_output_aliases={i: i for i in range(len(arrays))},
        cost_estimate=pl.CostEstimate(flops=0, bytes_accessed=0, transcendentals=0),
    )(*arrays, *after)


def pack_rows_kernel(count, *refs):
    at = 0
    for ref in refs[:count]:
        rows = ref.shape[0]
        refs[-1][at:at + rows, :] = ref[...]
        at += rows


def pack_rows(pieces, after=()):
    rows = sum(p.shape[0] for p in pieces)
    shape = (rows, pieces[0].shape[1])
    return pl.pallas_call(
        functools.partial(pack_rows_kernel, len(pieces)),
        in_specs=[pl.BlockSpec(p.shape, lambda: (0, 0)) for p in pieces] + [ANY] * len(after),
        out_specs=pl.BlockSpec(shape, lambda: (0, 0)),
        out_shape=jax.ShapeDtypeStruct(shape, pieces[0].dtype),
        cost_estimate=pl.CostEstimate(flops=0, bytes_accessed=0, transcendentals=0),
    )(*pieces, *after)


def join_heads_kernel(members, slots_ref, *refs):
    pieces, rest_ref, out_ref = refs[:members], refs[members], refs[members + 1]
    rows, cols = pieces[0].shape
    for index in range(members):
        for slot in range(members):
            @pl.when(slots_ref[index] == slot)
            def _():
                out_ref[0:rows, slot * cols:(slot + 1) * cols] = pieces[index][...]
    out_ref[rows:, :] = rest_ref[...]


def join_heads(slots, pieces, rest):
    rows, cols = pieces[0].shape
    members = len(pieces)
    shape = (rows + rest.shape[0], members * cols)
    block = lambda a: pl.BlockSpec(a.shape, lambda j, p: (0, 0))
    return pl.pallas_call(
        functools.partial(join_heads_kernel, members),
        grid_spec=pltpu.PrefetchScalarGridSpec(
            num_scalar_prefetch=1, grid=(1,), in_specs=[block(p) for p in pieces] + [block(rest)],
            out_specs=pl.BlockSpec(shape, lambda j, p: (0, 0))),
        out_shape=jax.ShapeDtypeStruct(shape, rest.dtype),
        cost_estimate=pl.CostEstimate(flops=0, bytes_accessed=0, transcendentals=0),
    )(slots, *pieces, rest)


def place_rows_kernel(place_ref, *refs):
    pieces, out_ref = refs[:-1], refs[-1]
    for step in range(GROUPS):
        out_ref[(place_ref[3] + step) % GROUPS] = pieces[step][...]
    for index in range(GROUPS, len(pieces)):
        out_ref[index] = pieces[index][...]


def place_rows(place, pieces):
    block = pl.BlockSpec(pieces[0].shape, lambda j, p: (0, 0))
    shape = (len(pieces),) + pieces[0].shape
    return pl.pallas_call(
        place_rows_kernel,
        grid_spec=pltpu.PrefetchScalarGridSpec(
            num_scalar_prefetch=1, grid=(1,), in_specs=[block] * len(pieces),
            out_specs=pl.BlockSpec(shape, lambda j, p: (0, 0, 0))),
        out_shape=jax.ShapeDtypeStruct(shape, pieces[0].dtype),
        cost_estimate=pl.CostEstimate(flops=0, bytes_accessed=0, transcendentals=0),
    )(place, *pieces)


def add_kernel(x_ref, rx_ref, y_ref, ry_ref, *refs):
    outs = refs[-4:]
    for index in range(2):
        outs[index][...] = add_low(x_ref[index], rx_ref[index])
        outs[2 + index][...] = add_low(y_ref[index], ry_ref[index])


def add_pairs(x, rx, y, ry, after=()):
    tail = x.shape[2:]
    return pl.pallas_call(
        add_kernel,
        grid=(4,),
        in_specs=[pl.BlockSpec((2, 1) + tail, lambda j: (0, j, 0, 0))] * 4 + [ANY] * len(after),
        out_specs=[pl.BlockSpec((1,) + tail, lambda j: (j, 0, 0))] * 4,
        out_shape=[jax.ShapeDtypeStruct((4,) + tail, BF)] * 4,
        compiler_params=pltpu.CompilerParams(vmem_limit_bytes=VMEM_LIMIT),
        cost_estimate=pl.CostEstimate(flops=0, bytes_accessed=12 * x.size, transcendentals=0),
    )(x, rx, y, ry, *after)


def add_four_kernel(x_ref, rx_ref, y_ref, ry_ref, *refs):
    outs = refs[-4:]
    for index in range(4):
        outs[index][0] = add_low(x_ref[index], rx_ref[index])
        outs[index][1] = add_low(y_ref[index], ry_ref[index])


def add_fours(x, rx, y, ry, after=()):
    tail = x.shape[1:]
    whole = pl.BlockSpec(x.shape, lambda j: (0, 0, 0))
    return pl.pallas_call(
        add_four_kernel,
        grid=(1,),
        in_specs=[whole] * 4 + [ANY] * len(after),
        out_specs=[pl.BlockSpec((2,) + tail, lambda j: (0, 0, 0))] * 4,
        out_shape=[jax.ShapeDtypeStruct((2,) + tail, BF)] * 4,
        compiler_params=pltpu.CompilerParams(vmem_limit_bytes=VMEM_LIMIT),
        cost_estimate=pl.CostEstimate(flops=0, bytes_accessed=12 * x.size, transcendentals=0),
    )(x, rx, y, ry, *after)


def sum_kernel(*refs):
    total = refs[0][...].astype(F32)
    for ref in refs[1:GROUPS]:
        total = total + ref[...].astype(F32)
    refs[-1][...] = total.astype(BF)


def sum_shards(shards, after=()):
    whole = pl.BlockSpec(shards[0].shape, lambda: (0, 0, 0))
    return pl.pallas_call(
        sum_kernel,
        in_specs=[whole] * GROUPS + [ANY] * len(after),
        out_specs=whole,
        out_shape=jax.ShapeDtypeStruct(shards[0].shape, BF),
        cost_estimate=pl.CostEstimate(flops=0, bytes_accessed=0, transcendentals=0),
    )(*shards, *after)


def stack_orders_kernel(*refs):
    for order in range(2):
        for index in range(GROUPS):
            refs[order - 2][index] = refs[index][order]


def stack_orders(pieces, after=()):
    tail = pieces[0].shape[1:]
    return pl.pallas_call(
        stack_orders_kernel,
        in_specs=[pl.BlockSpec((2,) + tail, lambda: (0, 0, 0))] * GROUPS + [ANY] * len(after),
        out_specs=[pl.BlockSpec((GROUPS,) + tail, lambda: (0, 0, 0))] * 2,
        out_shape=[jax.ShapeDtypeStruct((GROUPS,) + tail, BF)] * 2,
        cost_estimate=pl.CostEstimate(flops=0, bytes_accessed=0, transcendentals=0),
    )(*pieces, *after)


def stack_pairs_kernel(x_ref, rx_ref, y_ref, ry_ref, *refs):
    refs[-2][0] = x_ref[...]
    refs[-2][1] = rx_ref[...]
    refs[-1][0] = y_ref[...]
    refs[-1][1] = ry_ref[...]


def stack_pairs(x, rx, y, ry, after=()):
    tail = x.shape[1:]
    block = pl.BlockSpec((1,) + tail, lambda j: (j, 0, 0))
    return pl.pallas_call(
        stack_pairs_kernel,
        grid=(GROUPS,),
        in_specs=[block] * 4 + [ANY] * len(after),
        out_specs=[pl.BlockSpec((2, 1) + tail, lambda j: (0, j, 0, 0))] * 2,
        out_shape=[jax.ShapeDtypeStruct((2,) + x.shape, BF)] * 2,
        cost_estimate=pl.CostEstimate(flops=0, bytes_accessed=0, transcendentals=0),
    )(x, rx, y, ry, *after)


def grad_kernel(columns, place_ref, *refs):
    ins, part_ref = refs[:-1], refs[-1]
    for order, at, terms in columns:
        total = None
        for left, right in terms:
            term = dot_tn(ins[left][...], ins[right][...])
            total = term if total is None else total + term
        rows, cols = total.shape
        part_ref[order, :, :, :, at:at + cols] = total.astype(BF).reshape(4, 4, rows // SHARDS, cols)


def grad_part(place, ins, columns, after=()):
    specs = []
    for array, halved in ins:
        depth, cols = array.shape
        if halved:
            specs.append(pl.BlockSpec((depth, cols // 2), lambda j, p: (0, p[0])))
        else:
            specs.append(pl.BlockSpec((depth, cols), lambda j, p: (0, 0)))
    rows = ins[0][0].shape[1]
    shape = (2, 4, 4, rows // SHARDS, rows)
    return pl.pallas_call(
        functools.partial(grad_kernel, columns),
        grid_spec=pltpu.PrefetchScalarGridSpec(
            num_scalar_prefetch=1,
            grid=(1,),
            in_specs=specs + [ANY] * len(after),
            out_specs=pl.BlockSpec(shape, lambda j, p: (0, 0, 0, 0, 0)),
        ),
        out_shape=jax.ShapeDtypeStruct(shape, BF),
        compiler_params=pltpu.CompilerParams(vmem_limit_bytes=VMEM_LIMIT),
        cost_estimate=pl.CostEstimate(
            flops=sum(2 * rows * (rows // 2) * ins[left][0].shape[0]
                      for _, _, terms in columns for left, _ in terms),
            bytes_accessed=sum(2 * a.size for a, _ in ins), transcendentals=0),
    )(place, *[a for a, _ in ins], *after)


def from_pieces(place_ref, refs, order, group):
    here_ref, away_ref, other_here_ref, other_away_ref = refs[4 * order:4 * order + 4]
    quarter = pl.program_id(0)
    bit = quarter % 2 if order == 0 else quarter // 2
    near = place_ref[1 + order] == bit
    at = jnp.bitwise_xor(place_ref[3], group)
    own = jnp.where(near, here_ref[0, at], away_ref[0, at]).astype(F32)
    other = jnp.where(near, other_here_ref[0, at], other_away_ref[0, at]).astype(F32)
    lower = place_ref[0] == 0
    return jnp.where(lower, own, other), jnp.where(lower, other, own)


def assemble_ff_kernel(place_ref, own_ref, other_ref, gate_ref, up_ref, down_ref):
    shard, down = gate_ref.shape[0] // 4, down_ref.shape[2] // 4
    shard_rows = own_ref.shape[2] // 2

    def write(halves):
        for group in range(4):
            rows = slice(shard * group, shard * (group + 1))
            for half, source in enumerate(halves):
                for order in range(2):
                    base = order * shard_rows
                    for tile in range(2):
                        at = ((order * 2 + half) * 2 + tile) * FF_TILE
                        gate_ref[rows, at:at + FF_TILE] = source[
                            0, group, base + shard * tile:base + shard * (tile + 1)].astype(F32)
                        up_ref[rows, at:at + FF_TILE] = source[
                            0, group, base + shard * (2 + tile):base + shard * (3 + tile)].astype(F32)
                    for tile in range(down_ref.shape[3] // FF_TILE):
                        at = base + 4 * shard + down * tile
                        down_ref[order * 2 + half, 0, down * group:down * (group + 1),
                                 FF_TILE * tile:FF_TILE * (tile + 1)] = source[
                                     0, group, at:at + down].astype(F32)

    pl.when(place_ref[0] == 0)(lambda: write((own_ref, other_ref)))
    pl.when(place_ref[0] != 0)(lambda: write((other_ref, own_ref)))


def assemble_ff(place, own, other, hidden):
    quarter = lambda rows: pl.BlockSpec((rows, hidden), lambda q, p: (q, 0))
    part = pl.BlockSpec((1,) + own.shape[1:], lambda q, p: (q, 0, 0, 0))
    rows = own.shape[2] // 2
    width = (rows * FF_TILE * SHARDS * 4) // (3 * hidden)
    gate, up, down = pl.pallas_call(
        assemble_ff_kernel,
        grid_spec=pltpu.PrefetchScalarGridSpec(
            num_scalar_prefetch=1, grid=(4,), in_specs=[part, part],
            out_specs=[quarter(width // 4), quarter(width // 4),
                       pl.BlockSpec((4, 1, hidden // 16, width), lambda q, p: (0, q, 0, 0))]),
        out_shape=[jax.ShapeDtypeStruct((width, hidden), F32)] * 2
        + [jax.ShapeDtypeStruct((4, 4, hidden // 16, width), F32)],
        compiler_params=pltpu.CompilerParams(vmem_limit_bytes=VMEM_LIMIT),
        cost_estimate=pl.CostEstimate(flops=0, bytes_accessed=12 * own.size, transcendentals=0),
    )(place, own, other)
    return gate, up, down.reshape(hidden, width)


def assemble_kernel(place_ref, *refs):
    wq_ref, wk_ref, wv_ref, gain_ref = refs[8:12]
    outs = refs[-5:-1]
    shard = outs[0].shape[0] // 4
    for order in range(2):
        for group in range(4):
            rows = slice(shard * group, shard * (group + 1))
            for half, value in enumerate(from_pieces(place_ref, refs, order, group)):
                width = value.shape[1] // 2
                for which in range(2):
                    outs[2 * order + which][rows, half * width:(half + 1) * width] = (
                        value[:, which * width:(which + 1) * width])
    products = (outs[0][...] * wq_ref[...].astype(F32) + outs[2][...] * wk_ref[...].astype(F32)
                + outs[3][...] * wv_ref[...].astype(F32))
    refs[-1][...] = jnp.sum(products, axis=1, keepdims=True) / gain_ref[...]


def assemble(place, pieces, weights, gain, after=()):
    tail = pieces[0].shape[1:]
    width = gain.shape[0]
    near = pl.BlockSpec((1,) + tail, lambda q, p: (p[2] ^ (q // 2), 0, 0, 0))
    far = pl.BlockSpec((1,) + tail, lambda q, p: (p[1] ^ (q % 2), 0, 0, 0))
    rows = pl.BlockSpec((width // 4, width), lambda q, p: (q, 0))
    column = pl.BlockSpec((width // 4, 1), lambda q, p: (q, 0))
    return pl.pallas_call(
        assemble_kernel,
        grid_spec=pltpu.PrefetchScalarGridSpec(
            num_scalar_prefetch=1, grid=(4,),
            in_specs=[near] * 4 + [far] * 4 + [rows] * 3 + [column] + [ANY] * len(after),
            out_specs=[rows] * 4 + [column]),
        out_shape=[jax.ShapeDtypeStruct((width, width), F32)] * 4 + [jax.ShapeDtypeStruct((width, 1), F32)],
        compiler_params=pltpu.CompilerParams(vmem_limit_bytes=VMEM_LIMIT),
        cost_estimate=pl.CostEstimate(
            flops=0, bytes_accessed=16 * 8 * pieces[0].size // 4, transcendentals=0),
    )(place, *pieces, *weights, gain, *after)


def add_low(left, right):
    return (left.astype(F32) + right.astype(F32)).astype(BF)


def norm_scale(values):
    return lax.rsqrt(jnp.mean(values * values, axis=-1, keepdims=True) + EPS)


def norm_back(values, gain, grad):
    scale = norm_scale(values)
    scaled = values * scale
    weighted = grad * gain
    inner = jnp.mean(weighted * scaled, axis=-1, keepdims=True)
    return scale * (weighted - scaled * inner), jnp.sum(grad * scaled, axis=0)


def masked_squares(values_in, row_mask):
    return jnp.sum(row_mask * jnp.sum(values_in * values_in, axis=-1))


def body(n_img, n_seq, patches, counts, norm_gain_one, w_query, w_key, w_value, w_out,
         norm_gain_two, w_gate, w_up, w_down, cotangent):
    charts, block_len, width = patches.shape
    members = n_seq // GROUPS
    head_count = HEADS // members
    pairs = -(-head_count // 2)
    pad_cols = pairs * 128 - head_count * 64
    mine_cols = head_count * 64
    main_own = GROUPS * block_len
    seq_len = n_seq * block_len
    here = lax.axis_index("seq")
    group, member = here // members, here % members
    img_here = lax.axis_index("img")

    def slot_of(who):
        return (who % 2) * (members // 2) + who // 2

    def bit_exchange(axis, bit):
        def move(array):
            if axis == "img":
                perm = [(i, i ^ (1 << bit)) for i in range(n_img)]
            elif axis == "group":
                perm = [(g * members + r, (g ^ (1 << bit)) * members + r)
                        for g in range(GROUPS) for r in range(members)]
            else:
                perm = [(g * members + r, g * members + (r ^ (1 << bit)))
                        for g in range(GROUPS) for r in range(members)]
            return lax.ppermute(array, "img" if axis == "img" else "seq", perm)
        return move

    img_moves = [bit_exchange("img", 0), bit_exchange("img", 1)]
    z_moves = [bit_exchange("group", 0), bit_exchange("group", 1)]

    def z_move(array, step):
        perm = [(g * members + r, (g ^ step) * members + r) for g in range(GROUPS) for r in range(members)]
        return lax.ppermute(array, "seq", perm)

    core_move = bit_exchange("member", 0)
    more_moves = [bit_exchange("img", b) for b in range(2, n_img.bit_length() - 1)]
    more_moves += [bit_exchange("member", b) for b in range(1, members.bit_length() - 1)]
    img_bits = [img_here % 2, (img_here // 2) % 2]
    half_here = member % 2

    def place_of(half):
        return jnp.stack([half] + img_bits + [group]).astype(jnp.int32)

    there, here_place = place_of(1 - half_here), place_of(half_here)

    def sum_img_first(kx, sx, ky, sy, after=()):
        return add_pairs(kx, img_moves[0](sx), ky, img_moves[1](sy), after)

    def sum_img_second(kx, sx, ky, sy, after=()):
        return add_fours(kx, img_moves[1](sx), ky, img_moves[0](sy), after)

    def sum_groups(shards, after=()):
        total = sum_shards(
            [shards[0]] + [z_move(shards[step], step) for step in range(1, GROUPS)], after)
        for move in more_moves:
            total = add_low(total, move(total))
        return total

    def quarters(total, after):
        return stack_orders([total] + [z_move(total, step) for step in range(1, GROUPS)], after)

    def halves(parts, after):
        return stack_pairs(parts[0], img_moves[1](parts[0]), parts[1], img_moves[0](parts[1]), after)

    def shift_perm(step):
        return [(g * members + r, ((g + step) % GROUPS) * members + r)
                for g in range(GROUPS) for r in range(members)]

    def member_perm(step):
        return [(g * members + r, g * members + (r ^ step))
                for g in range(GROUPS) for r in range(members)]

    def to_groups(array, after=()):
        pieces = []
        for step in range(GROUPS):
            part = lax.dynamic_index_in_dim(array, (group + step) % GROUPS, 0, keepdims=False)
            if step:
                part = lax.ppermute(hold(part, after) if after else part, "seq", shift_perm(step))
            pieces.append(part)
        return pieces

    def from_groups(rows):
        pieces = []
        for step in range(GROUPS):
            part = rows[step * block_len:(step + 1) * block_len]
            pieces.append(part if step == 0 else lax.ppermute(part, "seq", shift_perm(-step)))
        return place_rows(here_place, pieces + [rows[main_own:]])

    def to_members(own):
        return [own] + [lax.ppermute(own, "seq", member_perm(step)) for step in range(1, members)]

    def columns_of(weight, who):
        part = lax.dynamic_slice_in_dim(weight, who * mine_cols, mine_cols, 1)
        return jnp.pad(part, ((0, 0), (0, pad_cols))) if pad_cols else part

    gain_one = norm_gain_one.astype(F32)
    gain_two = norm_gain_two.astype(F32)
    steps = jnp.arange(GROUPS, dtype=jnp.int32)
    block_of = ((group - steps) % GROUPS) * members
    inside = jnp.arange(block_len, dtype=jnp.int32)

    def main_positions(who):
        return ((block_of + who) * block_len)[:, None] + inside[None, :]

    count_main = lax.dynamic_index_in_dim(counts, group, 0, keepdims=False)
    count_rest = counts[GROUPS]
    rest_positions = here * block_len + inside
    row_valid = jnp.concatenate([
        (main_positions(member) < count_main).reshape(-1), rest_positions < count_rest])
    row_mask = row_valid.astype(F32)
    key_positions = jnp.concatenate(
        [main_positions(member ^ step).reshape(-1) for step in range(members)])

    def key_extras(valid):
        bias = jnp.where(valid, 0.0, NEG)[:, None]
        lane = jnp.arange(128)[None, :]
        return jnp.where(lane < 3, 1.0, jnp.where(lane == 3, bias, 0.0)).astype(BF)

    ext_main = key_extras(key_positions < count_main)
    ext_rest = key_extras(jnp.arange(seq_len) < count_rest)

    rest_rows = patches[GROUPS]
    rest_f32 = rest_rows.astype(F32)
    first_rest = (rest_f32 * norm_scale(rest_f32) * gain_one).astype(BF)
    moved = to_groups(patches)
    main_rows = jnp.concatenate(moved, axis=0).astype(F32)
    first_main = (main_rows * norm_scale(main_rows) * gain_one).astype(BF)
    first_all = jnp.concatenate(to_members(first_main), axis=0)
    first_rest_sent, _ = lax.optimization_barrier((first_rest, first_main))
    first_rest_all = lax.all_gather(first_rest_sent, "seq", axis=0, tiled=True)

    place = jnp.reshape(slot_of(member), (1,)).astype(jnp.int32)
    zero_place = jnp.zeros((1,), jnp.int32)
    if pad_cols:
        main_weights = [columns_of(w, slot_of(member)) for w in (w_query, w_key, w_value)]
        main_place = zero_place
    else:
        main_weights = [w_query, w_key, w_value]
        main_place = place
    q_rows = min(128, block_len)
    query_main, key_main, value_main, logs_main, attn_main = attend(
        main_place, first_all, first_all, *main_weights, ext_main, pairs, q_rows)
    query_rest, key_rest, value_rest, logs_rest, attn_rest = attend(
        zero_place, first_rest, first_rest_all, w_query, w_key, w_value, ext_rest,
        HEADS // 2, q_rows, (attn_main,))
    grad_moved = to_groups(cotangent, (attn_main,))
    grad_low = pack_rows(grad_moved + [cotangent[GROUPS]], (attn_rest,))

    slots = jnp.stack([slot_of(member ^ step) for step in range(members)]).astype(jnp.int32)
    swapped = []
    for step in range(members):
        part = attn_main[step * main_own:(step + 1) * main_own, :mine_cols]
        swapped.append(part if step == 0 else lax.ppermute(part, "seq", member_perm(step)))
    attn_in = join_heads(slots, swapped, attn_rest)
    resid = jnp.concatenate([main_rows, rest_f32], axis=0)
    branch_one = dot(attn_in, w_out)
    middle = resid + branch_one
    second_in = (middle * norm_scale(middle) * gain_two).astype(BF)
    ff_ins = (second_in, grad_low, w_gate, w_up, w_down)
    sums_two, sums_gs, ff_sent = ff_half(there, *ff_ins, None)
    branch_two, grad_second, ff_kept = ff_half(here_place, *ff_ins, (sums_two, sums_gs))
    ff_now = add_low(ff_kept, core_move(ff_sent))
    img_fours = [list(range(i, i + 4)) for i in range(0, n_img, 4)]
    same_member = [[g * members + r for g in range(GROUPS)] for r in range(members)]
    ff_quarter = lax.psum_scatter(ff_now, "img", scatter_dimension=0, axis_index_groups=img_fours)
    branch_two = hold(branch_two, (ff_now,))
    result = middle + branch_two
    squares = jnp.stack([masked_squares(v, row_mask) for v in (resid, branch_one, branch_two, result)])
    valid_count = jnp.sum(row_mask)
    result_low = result.astype(BF)
    layer_out = from_groups(result_low)
    grad_out = grad_low.astype(F32)
    grad_second = hold(grad_second, (ff_now,))
    grad_mid_norm, grad_gain_two = norm_back(middle, gain_two, grad_second)
    grad_mid = grad_out + grad_mid_norm
    grad_mid_low = grad_mid.astype(BF)

    main_grads = []
    for step in range(members):
        rows_of = lax.dynamic_slice_in_dim(w_out, slot_of(member ^ step) * mine_cols, mine_cols, 0)
        part = dot_nt(grad_mid_low[:main_own], rows_of).astype(BF)
        if pad_cols:
            part = jnp.pad(part, ((0, 0), (0, pad_cols)))
        main_grads.append(part if step == 0 else lax.ppermute(part, "seq", member_perm(step)))
    grad_attn_main = pack_rows(main_grads)
    grad_attn_rest = dot_nt(grad_mid_low[main_own:], w_out).astype(BF)

    dq_rest, dk_rest, dv_rest, first_own_rest, first_part_rest = attend_back(
        zero_place, query_rest, key_rest, value_rest, ext_rest, logs_rest, attn_rest, grad_attn_rest,
        (w_query, w_key, w_value), q_rows, 0)
    by_owner = first_part_rest.reshape(GROUPS, members, block_len, width)
    by_group = lax.dynamic_index_in_dim(by_owner, member, 1, keepdims=False).astype(F32)
    for step in range(1, members):
        part = lax.dynamic_index_in_dim(by_owner, member ^ step, 1, keepdims=False)
        by_group = by_group + lax.ppermute(part, "seq", member_perm(step)).astype(F32)
    by_group = by_group.astype(BF)
    rest_parts = [lax.dynamic_index_in_dim(by_group, group ^ step, 0, keepdims=False) for step in range(GROUPS)]

    half_width = width // 2
    rest_ins = [(first_rest, False), (dq_rest, True), (first_rest_all, False), (dk_rest, True),
                (dv_rest, True), (attn_in, False), (grad_mid_low, True)]
    qkv_sent = grad_part(there, rest_ins, [
        (0, 0, [(0, 1)]), (0, half_width, [(5, 6)]), (1, 0, [(2, 3)]), (1, half_width, [(2, 4)])],
        (dq_rest,))
    ff_quarter = hold(ff_quarter, (qkv_sent, layer_out, grad_attn_main, *rest_parts))
    ff_shard = lax.psum_scatter(ff_quarter, "seq", scatter_dimension=0, axis_index_groups=same_member)
    for move in more_moves:
        ff_shard = add_low(ff_shard, move(ff_shard))
    dq_main, dk_main, dv_main, first_own_main, first_far_main = attend_back(
        main_place, query_main, key_main, value_main, ext_main, logs_main, attn_main, grad_attn_main,
        main_weights, min(256, block_len * 2), main_own, (ff_quarter, *rest_parts))

    def in_half(part):
        part = part[:, :mine_cols]
        if mine_cols == width // 2:
            return part
        empty = jnp.zeros((part.shape[0], width // 2), part.dtype)
        return lax.dynamic_update_slice_in_dim(empty, part, (member // 2) * mine_cols, 1)

    main_ins = [(first_all, False), (in_half(dq_main), False), (in_half(dk_main), False),
                (in_half(dv_main), False)]
    qkv_kept = grad_part(here_place, rest_ins + main_ins, [
        (0, 0, [(0, 1), (7, 8)]), (0, half_width, [(5, 6)]),
        (1, 0, [(2, 3), (7, 9)]), (1, half_width, [(2, 4), (7, 10)])])
    ff_shard = hold(ff_shard, (qkv_kept,))
    ff_groups = lax.all_gather(ff_shard, "seq", axis=0, axis_index_groups=same_member)
    rest_got = [z_move(rest_parts[step], step) for step in range(1, GROUPS)]
    kx, sx, ky, sy = split_cores(here_place, qkv_kept, core_move(qkv_sent), rest_got)

    small = jnp.concatenate([grad_gain_two, squares, valid_count[None]])
    small = jnp.pad(small, (0, -small.size % 1024)).reshape(-1, 128)
    for move in [core_move] + more_moves:
        small = small + move(small)

    got, sx, sy = hold_all([img_moves[0](small), img_moves[0](sx), img_moves[1](sy)])
    small = small + got
    kx, sx, ky, sy = add_pairs(kx, sx, ky, sy)

    far = [first_far_main[(step - 1) * main_own:step * main_own] for step in range(1, members)]
    got, sx, sy, *far = hold_all(
        [img_moves[1](small), img_moves[1](sx), img_moves[0](sy)]
        + [lax.ppermute(part, "seq", member_perm(step + 1)) for step, part in enumerate(far)])
    small = small + got
    shards = add_fours(kx, sx, ky, sy)
    grad_first_main = first_own_main + sum(part.astype(F32) for part in far)
    grad_first_rest = first_own_rest + rest_parts[0].astype(F32) + sum(part.astype(F32) for part in rest_got)
    grad_first = jnp.concatenate([grad_first_main, grad_first_rest], axis=0)
    grad_input_rows = (grad_mid + norm_back(resid, gain_one, grad_first)[0]).astype(BF)

    ff_groups = hold(ff_groups, shards)
    ff_own = lax.all_gather(ff_groups, "img", axis=0, axis_index_groups=img_fours)
    got, *pieces = hold_all([z_moves[0](small)] + [z_move(shards[step], step) for step in range(1, GROUPS)])
    small = small + got
    qkv_total = sum_shards([shards[0]] + pieces, (grad_input_rows,))
    for move in more_moves:
        qkv_total = add_low(qkv_total, move(qkv_total))

    got, *pieces = hold_all([z_moves[1](small)] + [z_move(qkv_total, step) for step in range(1, GROUPS)])
    small = (small + got).reshape(-1)
    x, y = stack_orders([qkv_total] + pieces)
    sent_rows = [lax.ppermute(grad_input_rows[step * block_len:(step + 1) * block_len], "seq", shift_perm(-step))
                 for step in range(1, GROUPS)]
    rx, ry, *got = hold_all([img_moves[1](x), img_moves[0](y)] + sent_rows)
    near = stack_pairs(x, rx, y, ry)
    grad_input = place_rows(
        here_place, [grad_input_rows[:block_len]] + got + [grad_input_rows[main_own:]])
    rx, ry, cx, cy = hold_all(
        [img_moves[0](near[0]), img_moves[1](near[1]), core_move(near[0]), core_move(near[1])], (grad_input,))
    pieces = [near[0], rx, cx, core_move(rx), near[1], ry, cy, core_move(ry)]
    ff_own = hold(ff_own, (pieces[3], pieces[7]))
    ff_other = core_move(ff_own)
    sum_query, sum_out, sum_key, sum_value, sum_gain_one = assemble(
        here_place, pieces, (w_query, w_key, w_value), gain_one[:, None], (ff_own,))
    sum_gate, sum_up, sum_down = assemble_ff(
        here_place, ff_own, hold(ff_other, (sum_query,)), w_gate.shape[1])
    sum_gain_one = sum_gain_one.reshape(width)
    sum_gain_two, sum_squares, sum_count = small[:width], small[width:width + 4], small[width + 4]
    rms_stats = jnp.sqrt(sum_squares / (sum_count * width))
    return (layer_out, grad_input, sum_gain_one, sum_query, sum_key, sum_value, sum_out,
            sum_gain_two, sum_gate, sum_up, sum_down, rms_stats)


def solution(mesh):
    rows = P("img", "seq", None)
    return jax.shard_map(
        functools.partial(body, mesh.shape["img"], mesh.shape["seq"]),
        mesh=mesh,
        in_specs=(rows, P("img"), P(), P(), P(), P(), P(), P(), P(), P(), P(), rows),
        out_specs=(rows, rows, P(), P(), P(), P(), P(), P(), P(), P(), P(), P()),
        check_vma=False,
    )
```

```python
import functools
import math

import jax
import jax.numpy as jnp
from jax import lax
from jax.experimental import pallas as pl
from jax.experimental.pallas import tpu as pltpu
from jax.sharding import PartitionSpec as P

HEADS = 12
GROUPS = 4
SHARDS = 16
EPS = 1e-06
NEG = -1000000000.0
LOG2E = 1.4426950408889634
LN2 = 0.6931471805599453
GELU_C = 0.7978845608028654
GELU_A = 0.044715
BF = jnp.bfloat16
F32 = jnp.float32
VMEM_LIMIT = 56 * 1024 * 1024
ANY = pl.BlockSpec(memory_space=pl.ANY)


def dot(left, right):
    return jnp.dot(left, right, preferred_element_type=F32)


def dot_nt(left, right):
    return lax.dot_general(left, right, (((1,), (1,)), ((), ())), preferred_element_type=F32)


def dot_tn(left, right):
    return lax.dot_general(left, right, (((0,), (0,)), ((), ())), preferred_element_type=F32)


def split_three(column):
    hi = column.astype(BF).astype(F32)
    rest = column - hi
    mid = rest.astype(BF).astype(F32)
    return hi, mid, rest - mid


def extras(rows, columns):
    lane = lax.broadcasted_iota(jnp.int32, (rows, 128), 1)
    out = jnp.zeros((rows, 128), F32)
    for index, column in enumerate(columns):
        if column is not None:
            out = jnp.where(lane == index, column, out)
    return out.astype(BF)


def head_lanes(values, half):
    lane = lax.broadcasted_iota(jnp.int32, values.shape, 1)
    return jnp.where((lane < 64) if half == 0 else (lane >= 64), values, jnp.zeros_like(values))


def stack_heads(values):
    return jnp.concatenate([head_lanes(values, 0), head_lanes(values, 1)], axis=0)


def attend_kernel(q_rows, place_ref, fiq_ref, fik_ref, wq_ref, wk_ref, wv_ref, ext_ref, *refs):
    q_ref, k_ref, v_ref, log_ref, out_ref = refs[-5:]
    scale = LOG2E / math.sqrt(64.0)
    both = dot(fik_ref[...], jnp.concatenate([wk_ref[...], wv_ref[...]], axis=1)).astype(BF)
    k_ref[0] = both[:, :128]
    v_ref[0] = both[:, 128:]
    query = (dot(fiq_ref[...], wq_ref[...]) * scale).astype(BF)
    q_ref[0] = query
    ext = ext_ref[...]
    keys = jnp.concatenate([both[:, :128], ext], axis=1)
    values = jnp.concatenate([both[:, 128:], ext], axis=1)
    one = extras(2 * q_rows, (None, None, None, 1.0))
    for start in range(0, fiq_ref.shape[0], q_rows):
        rows = slice(start, start + q_rows)
        scores = dot_nt(jnp.concatenate([stack_heads(query[rows]), one], axis=1), keys)
        top = jnp.max(scores, axis=1, keepdims=True)
        weights = jnp.exp2(scores - top).astype(BF)
        mixed = dot(weights, values)
        norm = mixed[:, 128:129]
        logs = extras(2 * q_rows, split_three(-(top + jnp.log2(norm))) + (1.0,))
        log_ref[0, rows, :] = logs[:q_rows]
        log_ref[1, rows, :] = logs[q_rows:]
        scaled = mixed[:, :128] / norm
        lane = lax.broadcasted_iota(jnp.int32, (q_rows, 128), 1)
        out_ref[rows, :] = jnp.where(lane < 64, scaled[:q_rows], scaled[q_rows:]).astype(BF)


def attend(place, fi_q, fi_k, w_query, w_key, w_value, ext, pairs, q_rows, after=()):
    q_total, width = fi_q.shape
    k_total = fi_k.shape[0]
    column = lambda i, p: (0, p[0] * pairs + i)
    whole = lambda i, p: (0, 0)
    stacked = lambda i, p: (i, 0, 0)
    return pl.pallas_call(
        functools.partial(attend_kernel, q_rows),
        grid_spec=pltpu.PrefetchScalarGridSpec(
            num_scalar_prefetch=1,
            grid=(pairs,),
            in_specs=[
                pl.BlockSpec((q_total, width), whole),
                pl.BlockSpec((k_total, width), whole),
                pl.BlockSpec((width, 128), column),
                pl.BlockSpec((width, 128), column),
                pl.BlockSpec((width, 128), column),
                pl.BlockSpec((k_total, 128), whole),
            ] + [ANY] * len(after),
            out_specs=[
                pl.BlockSpec((1, q_total, 128), stacked),
                pl.BlockSpec((1, k_total, 128), stacked),
                pl.BlockSpec((1, k_total, 128), stacked),
                pl.BlockSpec((2, q_total, 128), stacked),
                pl.BlockSpec((q_total, 128), lambda i, p: (0, i)),
            ],
        ),
        out_shape=[
            jax.ShapeDtypeStruct((pairs, q_total, 128), BF),
            jax.ShapeDtypeStruct((pairs, k_total, 128), BF),
            jax.ShapeDtypeStruct((pairs, k_total, 128), BF),
            jax.ShapeDtypeStruct((2 * pairs, q_total, 128), BF),
            jax.ShapeDtypeStruct((q_total, pairs * 128), BF),
        ],
        compiler_params=pltpu.CompilerParams(vmem_limit_bytes=VMEM_LIMIT),
        cost_estimate=pl.CostEstimate(
            flops=4 * 128 * pairs * (4 * q_total * k_total + width * (q_total + 2 * k_total)),
            bytes_accessed=2 * (q_total + k_total) * width * 4,
            transcendentals=2 * pairs * q_total * k_total,
        ),
    )(place, fi_q, fi_k, w_query, w_key, w_value, ext, *after)


def attend_back_kernel(q_rows, own_rows, place_ref, q_ref, k_ref, v_ref, ext_ref, log_ref, out_ref,
                       grad_ref, wq_ref, wk_ref, wv_ref, *refs):
    dq_ref, dk_ref, dv_ref, own_ref, far_ref, sum_q, sum_k = refs[-7:]
    del place_ref
    step = pl.program_id(0)

    @pl.when(step == 0)
    def _():
        if not own_rows:
            sum_q[...] = jnp.zeros_like(sum_q)
        sum_k[...] = jnp.zeros_like(sum_k)

    ext = ext_ref[...]
    key_pair = k_ref[0]
    keys = jnp.concatenate([key_pair, ext], axis=1)
    values = jnp.concatenate([v_ref[0], ext], axis=1)
    keys_trans = jnp.transpose(key_pair.astype(F32)).astype(BF)
    dk_sum = jnp.zeros(key_pair.shape, F32)
    dv_sum = jnp.zeros(key_pair.shape, F32)
    for start in range(0, q_ref.shape[1], q_rows):
        rows = slice(start, start + q_rows)
        grad = grad_ref[rows, :]
        product = grad.astype(F32) * out_ref[rows, :].astype(F32)
        delta = jnp.sum(stack_heads(product), axis=1, keepdims=True)
        grad_h = stack_heads(grad)
        query_h = stack_heads(q_ref[0, rows, :])
        logs = jnp.concatenate([log_ref[0, rows, :], log_ref[1, rows, :]], axis=0)
        probs = jnp.exp2(dot_nt(keys, jnp.concatenate([query_h, logs], axis=1)))
        centred = dot_nt(values, jnp.concatenate([grad_h, extras(2 * q_rows, split_three(-delta))], axis=1))
        grad_scores = (probs * centred).astype(BF)
        dv_sum = dv_sum + dot(probs.astype(BF), grad_h)
        dk_sum = dk_sum + dot(grad_scores, query_h)
        first = dot(keys_trans[:64], grad_scores[:, :q_rows])
        second = dot(keys_trans[64:], grad_scores[:, q_rows:])
        dq_ref[rows, :] = (jnp.transpose(jnp.concatenate([first, second], axis=0)) * 0.125).astype(BF)
    dk = (dk_sum * LN2).astype(BF)
    dv = dv_sum.astype(BF)
    dk_ref[...] = dk
    dv_ref[...] = dv
    if own_rows:
        sum_k[...] += dot_nt(
            jnp.concatenate([dq_ref[...], dk, dv], axis=1),
            jnp.concatenate([wq_ref[...], wk_ref[...], wv_ref[...]], axis=1))
    else:
        sum_q[...] += dot_nt(dq_ref[...], wq_ref[...])
        sum_k[...] += dot_nt(
            jnp.concatenate([dk, dv], axis=1), jnp.concatenate([wk_ref[...], wv_ref[...]], axis=1))

    @pl.when(step == pl.num_programs(0) - 1)
    def _():
        if own_rows:
            own_ref[...] = sum_k[:own_rows]
            far_ref[...] = sum_k[own_rows:].astype(BF)
        else:
            own_ref[...] = sum_q[...]
            far_ref[...] = sum_k[...].astype(BF)


def attend_back(place, query, key, value, ext, logs, out, grad, weights, q_rows, own_rows, after=()):
    pairs, q_total, _ = query.shape
    k_total = key.shape[1]
    width = weights[0].shape[0]
    stacked = lambda i, p: (i, 0, 0)
    flat = lambda i, p: (0, i)
    whole = lambda i, p: (0, 0)
    column = pl.BlockSpec((width, 128), lambda i, p: (0, p[0] * pairs + i))
    shapes = [(own_rows, width), (k_total - own_rows, width)] if own_rows else [(q_total, width), (k_total, width)]
    return pl.pallas_call(
        functools.partial(attend_back_kernel, q_rows, own_rows),
        grid_spec=pltpu.PrefetchScalarGridSpec(
            num_scalar_prefetch=1,
            grid=(pairs,),
            in_specs=[
                pl.BlockSpec((1, q_total, 128), stacked),
                pl.BlockSpec((1, k_total, 128), stacked),
                pl.BlockSpec((1, k_total, 128), stacked),
                pl.BlockSpec((k_total, 128), whole),
                pl.BlockSpec((2, q_total, 128), stacked),
                pl.BlockSpec((q_total, 128), flat),
                pl.BlockSpec((q_total, 128), flat),
                column, column, column,
            ] + [ANY] * len(after),
            out_specs=[
                pl.BlockSpec((q_total, 128), flat),
                pl.BlockSpec((k_total, 128), flat),
                pl.BlockSpec((k_total, 128), flat),
                pl.BlockSpec(shapes[0], whole),
                pl.BlockSpec(shapes[1], whole),
            ],
            scratch_shapes=[
                pltpu.VMEM((8 if own_rows else q_total, width), F32), pltpu.VMEM((k_total, width), F32)],
        ),
        out_shape=[
            jax.ShapeDtypeStruct((q_total, pairs * 128), BF),
            jax.ShapeDtypeStruct((k_total, pairs * 128), BF),
            jax.ShapeDtypeStruct((k_total, pairs * 128), BF),
            jax.ShapeDtypeStruct(shapes[0], F32),
            jax.ShapeDtypeStruct(shapes[1], BF),
        ],
        compiler_params=pltpu.CompilerParams(vmem_limit_bytes=VMEM_LIMIT),
        cost_estimate=pl.CostEstimate(
            flops=2 * 256 * pairs * 5 * q_total * k_total,
            bytes_accessed=2 * 128 * pairs * (4 * q_total + 4 * k_total),
            transcendentals=2 * pairs * q_total * k_total,
        ),
    )(place, query, key, value, ext, logs, out, grad, *weights, *after)


FF_TILE = 256
FF_STEP = 512


def ff_kernel(first, place_ref, second_ref, grad_ref, wg_ref, wu_ref, wd_ref, *refs):
    two_ref, gs_ref, part_ref, second_t_ref = refs[-4:]
    step = pl.program_id(0)

    @pl.when(step == 0)
    def _():
        second_t_ref[...] = jnp.transpose(second_ref[...])
        if first:
            two_ref[...] = jnp.zeros_like(two_ref)
            gs_ref[...] = jnp.zeros_like(gs_ref)
        else:
            two_ref[...] = refs[0][...]
            gs_ref[...] = refs[1][...]

    second, grad = second_ref[...], grad_ref[...]
    gate = dot(second, wg_ref[...])
    up = dot(second, wu_ref[...])
    grad_inner = dot_nt(grad, wd_ref[...])
    square = gate * gate
    half_plus = 0.5 + 0.5 * jnp.tanh(gate * (GELU_C + (GELU_C * GELU_A) * square))
    gelu = gate * half_plus
    slope = half_plus + gelu * (1.0 - half_plus) * (2.0 * GELU_C + (6.0 * GELU_C * GELU_A) * square)
    inner = (gelu * up).astype(BF)
    grad_gate = (grad_inner * up * slope).astype(BF)
    grad_up = (grad_inner * gelu).astype(BF)
    two_ref[...] += dot(inner, wd_ref[...])
    gs_ref[...] += dot_nt(grad_gate, wg_ref[...]) + dot_nt(grad_up, wu_ref[...])
    width = second.shape[1]
    shard, shard_down = width // SHARDS, 2 * FF_TILE // SHARDS
    part_gate = dot(second_t_ref[...], grad_gate).astype(BF)
    part_up = dot(second_t_ref[...], grad_up).astype(BF)
    part_down = dot_tn(inner, grad).astype(BF)
    shape = (4, 4, shard, FF_TILE)
    for odd in range(FF_STEP // FF_TILE):
        here = slice(FF_TILE * odd, FF_TILE * (odd + 1))
        part_ref[:, :, shard * odd:shard * (odd + 1), :] = part_gate[:, here].reshape(shape)
        part_ref[:, :, shard * (2 + odd):shard * (3 + odd), :] = part_up[:, here].reshape(shape)
        for tile in range(width // FF_TILE):
            at = 4 * shard + shard_down * tile
            part_ref[2 * odd:2 * odd + 2, :, at:at + shard_down, :] = (
                part_down[here, FF_TILE * tile:FF_TILE * (tile + 1)].reshape(2, 4, shard_down, FF_TILE))


def ff_half(place, second, grad, w_gate, w_up, w_down, sums, after=()):
    rows, width = second.shape
    tiles = w_gate.shape[1] // FF_STEP // 2
    tile_at = lambda j, p: j * 2 + p[0]
    whole = lambda j, p: (0, 0)
    sum_spec = pl.BlockSpec((rows, width), whole)
    columns = pl.BlockSpec((width, FF_STEP), lambda j, p: (0, tile_at(j, p)))
    shard_rows = 4 * (width // SHARDS) + (2 * FF_TILE // SHARDS) * (width // FF_TILE)
    return pl.pallas_call(
        functools.partial(ff_kernel, sums is None),
        grid_spec=pltpu.PrefetchScalarGridSpec(
            num_scalar_prefetch=1,
            grid=(tiles,),
            in_specs=[
                pl.BlockSpec((rows, width), whole), pl.BlockSpec((rows, width), whole),
                columns, columns, pl.BlockSpec((FF_STEP, width), lambda j, p: (tile_at(j, p), 0)),
            ] + [sum_spec] * (0 if sums is None else 2) + [ANY] * len(after),
            out_specs=[sum_spec, sum_spec,
                       pl.BlockSpec((4, 4, shard_rows, FF_TILE), lambda j, p: (0, 0, j, 0))],
            scratch_shapes=[pltpu.VMEM((width, rows), BF)],
        ),
        out_shape=[jax.ShapeDtypeStruct((rows, width), F32)] * 2
        + [jax.ShapeDtypeStruct((4, 4, 2 * shard_rows, FF_TILE), BF)],
        compiler_params=pltpu.CompilerParams(vmem_limit_bytes=VMEM_LIMIT),
        cost_estimate=pl.CostEstimate(
            flops=18 * rows * width * tiles * FF_STEP,
            bytes_accessed=12 * width * tiles * FF_STEP + 16 * rows * width,
            transcendentals=rows * tiles * FF_STEP),
    )(place, second, grad, w_gate, w_up, w_down, *(sums or ()), *after)


def split_kernel(place_ref, *refs):
    ins, outs = refs[:8], refs[-4:]
    for index, out in enumerate(outs):
        for step in range(4):
            at = jnp.bitwise_xor(place_ref[3], step)
            out[0, step] = (ins[index][0, 0, at].astype(F32) + ins[4 + index][0, 0, at].astype(F32)).astype(BF)


def split_cores(place, kept, got, after=()):
    tail = kept.shape[3:]

    def spec(order, away):
        def at(b, p):
            first, second = p[1 + order] ^ away, p[2 - order] ^ b
            return (order, first + 2 * second if order == 0 else second + 2 * first, 0, 0, 0)
        return pl.BlockSpec((1, 1, 4) + tail, at)

    specs = [spec(order, away) for order in range(2) for away in range(2)]
    out = pl.BlockSpec((1, 4) + tail, lambda b, p: (b, 0, 0, 0))
    return pl.pallas_call(
        split_kernel,
        grid_spec=pltpu.PrefetchScalarGridSpec(
            num_scalar_prefetch=1, grid=(2,), in_specs=specs * 2 + [ANY] * len(after), out_specs=[out] * 4),
        out_shape=[jax.ShapeDtypeStruct((2, 4) + tail, BF)] * 4,
        compiler_params=pltpu.CompilerParams(vmem_limit_bytes=VMEM_LIMIT),
        cost_estimate=pl.CostEstimate(flops=0, bytes_accessed=6 * kept.size, transcendentals=0),
    )(place, *([kept] * 4), *([got] * 4), *after)


def hold(array, after):
    return pl.pallas_call(
        lambda *refs: None,
        in_specs=[ANY] * (1 + len(after)),
        out_specs=ANY,
        out_shape=jax.ShapeDtypeStruct(array.shape, array.dtype),
        input_output_aliases={0: 0},
        cost_estimate=pl.CostEstimate(flops=0, bytes_accessed=0, transcendentals=0),
    )(array, *after)


def hold_all(arrays, after=()):
    return pl.pallas_call(
        lambda *refs: None,
        in_specs=[ANY] * (len(arrays) + len(after)),
        out_specs=[ANY] * len(arrays),
        out_shape=[jax.ShapeDtypeStruct(a.shape, a.dtype) for a in arrays],
        input_output_aliases={i: i for i in range(len(arrays))},
        cost_estimate=pl.CostEstimate(flops=0, bytes_accessed=0, transcendentals=0),
    )(*arrays, *after)


def pack_rows_kernel(count, *refs):
    at = 0
    for ref in refs[:count]:
        rows = ref.shape[0]
        refs[-1][at:at + rows, :] = ref[...]
        at += rows


def pack_rows(pieces, after=()):
    rows = sum(p.shape[0] for p in pieces)
    shape = (rows, pieces[0].shape[1])
    return pl.pallas_call(
        functools.partial(pack_rows_kernel, len(pieces)),
        in_specs=[pl.BlockSpec(p.shape, lambda: (0, 0)) for p in pieces] + [ANY] * len(after),
        out_specs=pl.BlockSpec(shape, lambda: (0, 0)),
        out_shape=jax.ShapeDtypeStruct(shape, pieces[0].dtype),
        cost_estimate=pl.CostEstimate(flops=0, bytes_accessed=0, transcendentals=0),
    )(*pieces, *after)


def join_heads_kernel(members, slots_ref, *refs):
    pieces, rest_ref, out_ref = refs[:members], refs[members], refs[members + 1]
    rows, cols = pieces[0].shape
    for index in range(members):
        for slot in range(members):
            @pl.when(slots_ref[index] == slot)
            def _():
                out_ref[0:rows, slot * cols:(slot + 1) * cols] = pieces[index][...]
    out_ref[rows:, :] = rest_ref[...]


def join_heads(slots, pieces, rest):
    rows, cols = pieces[0].shape
    members = len(pieces)
    shape = (rows + rest.shape[0], members * cols)
    block = lambda a: pl.BlockSpec(a.shape, lambda j, p: (0, 0))
    return pl.pallas_call(
        functools.partial(join_heads_kernel, members),
        grid_spec=pltpu.PrefetchScalarGridSpec(
            num_scalar_prefetch=1, grid=(1,), in_specs=[block(p) for p in pieces] + [block(rest)],
            out_specs=pl.BlockSpec(shape, lambda j, p: (0, 0))),
        out_shape=jax.ShapeDtypeStruct(shape, rest.dtype),
        cost_estimate=pl.CostEstimate(flops=0, bytes_accessed=0, transcendentals=0),
    )(slots, *pieces, rest)


def place_rows_kernel(place_ref, *refs):
    pieces, out_ref = refs[:-1], refs[-1]
    for step in range(GROUPS):
        out_ref[(place_ref[3] + step) % GROUPS] = pieces[step][...]
    for index in range(GROUPS, len(pieces)):
        out_ref[index] = pieces[index][...]


def place_rows(place, pieces):
    block = pl.BlockSpec(pieces[0].shape, lambda j, p: (0, 0))
    shape = (len(pieces),) + pieces[0].shape
    return pl.pallas_call(
        place_rows_kernel,
        grid_spec=pltpu.PrefetchScalarGridSpec(
            num_scalar_prefetch=1, grid=(1,), in_specs=[block] * len(pieces),
            out_specs=pl.BlockSpec(shape, lambda j, p: (0, 0, 0))),
        out_shape=jax.ShapeDtypeStruct(shape, pieces[0].dtype),
        cost_estimate=pl.CostEstimate(flops=0, bytes_accessed=0, transcendentals=0),
    )(place, *pieces)


def add_kernel(x_ref, rx_ref, y_ref, ry_ref, *refs):
    outs = refs[-4:]
    for index in range(2):
        outs[index][...] = add_low(x_ref[index], rx_ref[index])
        outs[2 + index][...] = add_low(y_ref[index], ry_ref[index])


def add_pairs(x, rx, y, ry, after=()):
    tail = x.shape[2:]
    return pl.pallas_call(
        add_kernel,
        grid=(4,),
        in_specs=[pl.BlockSpec((2, 1) + tail, lambda j: (0, j, 0, 0))] * 4 + [ANY] * len(after),
        out_specs=[pl.BlockSpec((1,) + tail, lambda j: (j, 0, 0))] * 4,
        out_shape=[jax.ShapeDtypeStruct((4,) + tail, BF)] * 4,
        compiler_params=pltpu.CompilerParams(vmem_limit_bytes=VMEM_LIMIT),
        cost_estimate=pl.CostEstimate(flops=0, bytes_accessed=12 * x.size, transcendentals=0),
    )(x, rx, y, ry, *after)


def add_four_kernel(x_ref, rx_ref, y_ref, ry_ref, *refs):
    outs = refs[-4:]
    for index in range(4):
        outs[index][0] = add_low(x_ref[index], rx_ref[index])
        outs[index][1] = add_low(y_ref[index], ry_ref[index])


def add_fours(x, rx, y, ry, after=()):
    tail = x.shape[1:]
    whole = pl.BlockSpec(x.shape, lambda j: (0, 0, 0))
    return pl.pallas_call(
        add_four_kernel,
        grid=(1,),
        in_specs=[whole] * 4 + [ANY] * len(after),
        out_specs=[pl.BlockSpec((2,) + tail, lambda j: (0, 0, 0))] * 4,
        out_shape=[jax.ShapeDtypeStruct((2,) + tail, BF)] * 4,
        compiler_params=pltpu.CompilerParams(vmem_limit_bytes=VMEM_LIMIT),
        cost_estimate=pl.CostEstimate(flops=0, bytes_accessed=12 * x.size, transcendentals=0),
    )(x, rx, y, ry, *after)


def sum_kernel(*refs):
    total = refs[0][...].astype(F32)
    for ref in refs[1:GROUPS]:
        total = total + ref[...].astype(F32)
    refs[-1][...] = total.astype(BF)


def sum_shards(shards, after=()):
    whole = pl.BlockSpec(shards[0].shape, lambda: (0, 0, 0))
    return pl.pallas_call(
        sum_kernel,
        in_specs=[whole] * GROUPS + [ANY] * len(after),
        out_specs=whole,
        out_shape=jax.ShapeDtypeStruct(shards[0].shape, BF),
        cost_estimate=pl.CostEstimate(flops=0, bytes_accessed=0, transcendentals=0),
    )(*shards, *after)


def stack_orders_kernel(*refs):
    for order in range(2):
        for index in range(GROUPS):
            refs[order - 2][index] = refs[index][order]


def stack_orders(pieces, after=()):
    tail = pieces[0].shape[1:]
    return pl.pallas_call(
        stack_orders_kernel,
        in_specs=[pl.BlockSpec((2,) + tail, lambda: (0, 0, 0))] * GROUPS + [ANY] * len(after),
        out_specs=[pl.BlockSpec((GROUPS,) + tail, lambda: (0, 0, 0))] * 2,
        out_shape=[jax.ShapeDtypeStruct((GROUPS,) + tail, BF)] * 2,
        cost_estimate=pl.CostEstimate(flops=0, bytes_accessed=0, transcendentals=0),
    )(*pieces, *after)


def stack_pairs_kernel(x_ref, rx_ref, y_ref, ry_ref, *refs):
    refs[-2][0] = x_ref[...]
    refs[-2][1] = rx_ref[...]
    refs[-1][0] = y_ref[...]
    refs[-1][1] = ry_ref[...]


def stack_pairs(x, rx, y, ry, after=()):
    tail = x.shape[1:]
    block = pl.BlockSpec((1,) + tail, lambda j: (j, 0, 0))
    return pl.pallas_call(
        stack_pairs_kernel,
        grid=(GROUPS,),
        in_specs=[block] * 4 + [ANY] * len(after),
        out_specs=[pl.BlockSpec((2, 1) + tail, lambda j: (0, j, 0, 0))] * 2,
        out_shape=[jax.ShapeDtypeStruct((2,) + x.shape, BF)] * 2,
        cost_estimate=pl.CostEstimate(flops=0, bytes_accessed=0, transcendentals=0),
    )(x, rx, y, ry, *after)


def grad_kernel(columns, place_ref, *refs):
    ins, part_ref = refs[:-1], refs[-1]
    for order, at, terms in columns:
        total = None
        for left, right in terms:
            term = dot_tn(ins[left][...], ins[right][...])
            total = term if total is None else total + term
        rows, cols = total.shape
        part_ref[order, :, :, :, at:at + cols] = total.astype(BF).reshape(4, 4, rows // SHARDS, cols)


def grad_part(place, ins, columns, after=()):
    specs = []
    for array, halved in ins:
        depth, cols = array.shape
        if halved:
            specs.append(pl.BlockSpec((depth, cols // 2), lambda j, p: (0, p[0])))
        else:
            specs.append(pl.BlockSpec((depth, cols), lambda j, p: (0, 0)))
    rows = ins[0][0].shape[1]
    shape = (2, 4, 4, rows // SHARDS, rows)
    return pl.pallas_call(
        functools.partial(grad_kernel, columns),
        grid_spec=pltpu.PrefetchScalarGridSpec(
            num_scalar_prefetch=1,
            grid=(1,),
            in_specs=specs + [ANY] * len(after),
            out_specs=pl.BlockSpec(shape, lambda j, p: (0, 0, 0, 0, 0)),
        ),
        out_shape=jax.ShapeDtypeStruct(shape, BF),
        compiler_params=pltpu.CompilerParams(vmem_limit_bytes=VMEM_LIMIT),
        cost_estimate=pl.CostEstimate(
            flops=sum(2 * rows * (rows // 2) * ins[left][0].shape[0]
                      for _, _, terms in columns for left, _ in terms),
            bytes_accessed=sum(2 * a.size for a, _ in ins), transcendentals=0),
    )(place, *[a for a, _ in ins], *after)


def from_pieces(place_ref, refs, order, group):
    here_ref, away_ref, other_here_ref, other_away_ref = refs[4 * order:4 * order + 4]
    quarter = pl.program_id(0)
    bit = quarter % 2 if order == 0 else quarter // 2
    near = place_ref[1 + order] == bit
    at = jnp.bitwise_xor(place_ref[3], group)
    own = jnp.where(near, here_ref[0, at], away_ref[0, at]).astype(F32)
    other = jnp.where(near, other_here_ref[0, at], other_away_ref[0, at]).astype(F32)
    lower = place_ref[0] == 0
    return jnp.where(lower, own, other), jnp.where(lower, other, own)


def assemble_ff_kernel(place_ref, own_ref, other_ref, gate_ref, up_ref, down_ref):
    shard, down = gate_ref.shape[0] // 4, down_ref.shape[2] // 4
    shard_rows = own_ref.shape[2] // 2

    def write(halves):
        for group in range(4):
            rows = slice(shard * group, shard * (group + 1))
            for half, source in enumerate(halves):
                for order in range(2):
                    base = order * shard_rows
                    for tile in range(2):
                        at = ((order * 2 + half) * 2 + tile) * FF_TILE
                        gate_ref[rows, at:at + FF_TILE] = source[
                            0, group, base + shard * tile:base + shard * (tile + 1)].astype(F32)
                        up_ref[rows, at:at + FF_TILE] = source[
                            0, group, base + shard * (2 + tile):base + shard * (3 + tile)].astype(F32)
                    for tile in range(down_ref.shape[3] // FF_TILE):
                        at = base + 4 * shard + down * tile
                        down_ref[order * 2 + half, 0, down * group:down * (group + 1),
                                 FF_TILE * tile:FF_TILE * (tile + 1)] = source[
                                     0, group, at:at + down].astype(F32)

    pl.when(place_ref[0] == 0)(lambda: write((own_ref, other_ref)))
    pl.when(place_ref[0] != 0)(lambda: write((other_ref, own_ref)))


def assemble_ff(place, own, other, hidden):
    quarter = lambda rows: pl.BlockSpec((rows, hidden), lambda q, p: (q, 0))
    part = pl.BlockSpec((1,) + own.shape[1:], lambda q, p: (q, 0, 0, 0))
    rows = own.shape[2] // 2
    width = (rows * FF_TILE * SHARDS * 4) // (3 * hidden)
    gate, up, down = pl.pallas_call(
        assemble_ff_kernel,
        grid_spec=pltpu.PrefetchScalarGridSpec(
            num_scalar_prefetch=1, grid=(4,), in_specs=[part, part],
            out_specs=[quarter(width // 4), quarter(width // 4),
                       pl.BlockSpec((4, 1, hidden // 16, width), lambda q, p: (0, q, 0, 0))]),
        out_shape=[jax.ShapeDtypeStruct((width, hidden), F32)] * 2
        + [jax.ShapeDtypeStruct((4, 4, hidden // 16, width), F32)],
        compiler_params=pltpu.CompilerParams(vmem_limit_bytes=VMEM_LIMIT),
        cost_estimate=pl.CostEstimate(flops=0, bytes_accessed=12 * own.size, transcendentals=0),
    )(place, own, other)
    return gate, up, down.reshape(hidden, width)


def assemble_kernel(place_ref, *refs):
    wq_ref, wk_ref, wv_ref, gain_ref = refs[8:12]
    outs = refs[-5:-1]
    shard = outs[0].shape[0] // 4
    for order in range(2):
        for group in range(4):
            rows = slice(shard * group, shard * (group + 1))
            for half, value in enumerate(from_pieces(place_ref, refs, order, group)):
                width = value.shape[1] // 2
                for which in range(2):
                    outs[2 * order + which][rows, half * width:(half + 1) * width] = (
                        value[:, which * width:(which + 1) * width])
    products = (outs[0][...] * wq_ref[...].astype(F32) + outs[2][...] * wk_ref[...].astype(F32)
                + outs[3][...] * wv_ref[...].astype(F32))
    refs[-1][...] = jnp.sum(products, axis=1, keepdims=True) / gain_ref[...]


def assemble(place, pieces, weights, gain, after=()):
    tail = pieces[0].shape[1:]
    width = gain.shape[0]
    near = pl.BlockSpec((1,) + tail, lambda q, p: (p[2] ^ (q // 2), 0, 0, 0))
    far = pl.BlockSpec((1,) + tail, lambda q, p: (p[1] ^ (q % 2), 0, 0, 0))
    rows = pl.BlockSpec((width // 4, width), lambda q, p: (q, 0))
    column = pl.BlockSpec((width // 4, 1), lambda q, p: (q, 0))
    return pl.pallas_call(
        assemble_kernel,
        grid_spec=pltpu.PrefetchScalarGridSpec(
            num_scalar_prefetch=1, grid=(4,),
            in_specs=[near] * 4 + [far] * 4 + [rows] * 3 + [column] + [ANY] * len(after),
            out_specs=[rows] * 4 + [column]),
        out_shape=[jax.ShapeDtypeStruct((width, width), F32)] * 4 + [jax.ShapeDtypeStruct((width, 1), F32)],
        compiler_params=pltpu.CompilerParams(vmem_limit_bytes=VMEM_LIMIT),
        cost_estimate=pl.CostEstimate(
            flops=0, bytes_accessed=16 * 8 * pieces[0].size // 4, transcendentals=0),
    )(place, *pieces, *weights, gain, *after)


def add_low(left, right):
    return (left.astype(F32) + right.astype(F32)).astype(BF)


def norm_scale(values):
    return lax.rsqrt(jnp.mean(values * values, axis=-1, keepdims=True) + EPS)


def norm_back(values, gain, grad):
    scale = norm_scale(values)
    scaled = values * scale
    weighted = grad * gain
    inner = jnp.mean(weighted * scaled, axis=-1, keepdims=True)
    return scale * (weighted - scaled * inner), jnp.sum(grad * scaled, axis=0)


def masked_squares(values_in, row_mask):
    return jnp.sum(row_mask * jnp.sum(values_in * values_in, axis=-1))


def body(n_img, n_seq, patches, counts, norm_gain_one, w_query, w_key, w_value, w_out,
         norm_gain_two, w_gate, w_up, w_down, cotangent):
    charts, block_len, width = patches.shape
    members = n_seq // GROUPS
    head_count = HEADS // members
    pairs = -(-head_count // 2)
    pad_cols = pairs * 128 - head_count * 64
    mine_cols = head_count * 64
    main_own = GROUPS * block_len
    seq_len = n_seq * block_len
    here = lax.axis_index("seq")
    group, member = here // members, here % members
    img_here = lax.axis_index("img")

    def slot_of(who):
        return (who % 2) * (members // 2) + who // 2

    def bit_exchange(axis, bit):
        def move(array):
            if axis == "img":
                perm = [(i, i ^ (1 << bit)) for i in range(n_img)]
            elif axis == "group":
                perm = [(g * members + r, (g ^ (1 << bit)) * members + r)
                        for g in range(GROUPS) for r in range(members)]
            else:
                perm = [(g * members + r, g * members + (r ^ (1 << bit)))
                        for g in range(GROUPS) for r in range(members)]
            return lax.ppermute(array, "img" if axis == "img" else "seq", perm)
        return move

    img_moves = [bit_exchange("img", 0), bit_exchange("img", 1)]
    z_moves = [bit_exchange("group", 0), bit_exchange("group", 1)]

    def z_move(array, step):
        perm = [(g * members + r, (g ^ step) * members + r) for g in range(GROUPS) for r in range(members)]
        return lax.ppermute(array, "seq", perm)

    core_move = bit_exchange("member", 0)
    more_moves = [bit_exchange("img", b) for b in range(2, n_img.bit_length() - 1)]
    more_moves += [bit_exchange("member", b) for b in range(1, members.bit_length() - 1)]
    img_bits = [img_here % 2, (img_here // 2) % 2]
    half_here = member % 2

    def place_of(half):
        return jnp.stack([half] + img_bits + [group]).astype(jnp.int32)

    there, here_place = place_of(1 - half_here), place_of(half_here)

    def sum_img_first(kx, sx, ky, sy, after=()):
        return add_pairs(kx, img_moves[0](sx), ky, img_moves[1](sy), after)

    def sum_img_second(kx, sx, ky, sy, after=()):
        return add_fours(kx, img_moves[1](sx), ky, img_moves[0](sy), after)

    def sum_groups(shards, after=()):
        total = sum_shards(
            [shards[0]] + [z_move(shards[step], step) for step in range(1, GROUPS)], after)
        for move in more_moves:
            total = add_low(total, move(total))
        return total

    def quarters(total, after):
        return stack_orders([total] + [z_move(total, step) for step in range(1, GROUPS)], after)

    def halves(parts, after):
        return stack_pairs(parts[0], img_moves[1](parts[0]), parts[1], img_moves[0](parts[1]), after)

    def shift_perm(step):
        return [(g * members + r, ((g + step) % GROUPS) * members + r)
                for g in range(GROUPS) for r in range(members)]

    def member_perm(step):
        return [(g * members + r, g * members + (r ^ step))
                for g in range(GROUPS) for r in range(members)]

    def to_groups(array, after=()):
        pieces = []
        for step in range(GROUPS):
            part = lax.dynamic_index_in_dim(array, (group + step) % GROUPS, 0, keepdims=False)
            if step:
                part = lax.ppermute(hold(part, after) if after else part, "seq", shift_perm(step))
            pieces.append(part)
        return pieces

    def sent_home(rows):
        return [lax.ppermute(rows[step * block_len:(step + 1) * block_len], "seq", shift_perm(-step))
                for step in range(1, GROUPS)]

    def placed(rows, got):
        return place_rows(here_place, [rows[:block_len], *got, rows[main_own:]])

    def to_members(own):
        return [own] + [lax.ppermute(own, "seq", member_perm(step)) for step in range(1, members)]

    def columns_of(weight, who):
        part = lax.dynamic_slice_in_dim(weight, who * mine_cols, mine_cols, 1)
        return jnp.pad(part, ((0, 0), (0, pad_cols))) if pad_cols else part

    gain_one = norm_gain_one.astype(F32)
    gain_two = norm_gain_two.astype(F32)
    steps = jnp.arange(GROUPS, dtype=jnp.int32)
    block_of = ((group - steps) % GROUPS) * members
    inside = jnp.arange(block_len, dtype=jnp.int32)

    def main_positions(who):
        return ((block_of + who) * block_len)[:, None] + inside[None, :]

    count_main = lax.dynamic_index_in_dim(counts, group, 0, keepdims=False)
    count_rest = counts[GROUPS]
    rest_positions = here * block_len + inside
    row_valid = jnp.concatenate([
        (main_positions(member) < count_main).reshape(-1), rest_positions < count_rest])
    row_mask = row_valid.astype(F32)
    key_positions = jnp.concatenate(
        [main_positions(member ^ step).reshape(-1) for step in range(members)])

    def key_extras(valid):
        bias = jnp.where(valid, 0.0, NEG)[:, None]
        lane = jnp.arange(128)[None, :]
        return jnp.where(lane < 3, 1.0, jnp.where(lane == 3, bias, 0.0)).astype(BF)

    ext_main = key_extras(key_positions < count_main)
    ext_rest = key_extras(jnp.arange(seq_len) < count_rest)

    rest_rows = patches[GROUPS]
    rest_f32 = rest_rows.astype(F32)
    first_rest = (rest_f32 * norm_scale(rest_f32) * gain_one).astype(BF)
    moved = to_groups(patches)
    main_rows = jnp.concatenate(moved, axis=0).astype(F32)
    first_main = (main_rows * norm_scale(main_rows) * gain_one).astype(BF)
    first_all = jnp.concatenate(to_members(first_main), axis=0)
    first_rest_sent, _ = lax.optimization_barrier((first_rest, first_main))
    first_rest_all = lax.all_gather(first_rest_sent, "seq", axis=0, tiled=True)

    place = jnp.reshape(slot_of(member), (1,)).astype(jnp.int32)
    zero_place = jnp.zeros((1,), jnp.int32)
    if pad_cols:
        main_weights = [columns_of(w, slot_of(member)) for w in (w_query, w_key, w_value)]
        main_place = zero_place
    else:
        main_weights = [w_query, w_key, w_value]
        main_place = place
    q_rows = min(128, block_len)
    query_main, key_main, value_main, logs_main, attn_main = attend(
        main_place, first_all, first_all, *main_weights, ext_main, pairs, q_rows)
    query_rest, key_rest, value_rest, logs_rest, attn_rest = attend(
        zero_place, first_rest, first_rest_all, w_query, w_key, w_value, ext_rest,
        HEADS // 2, q_rows, (attn_main,))
    grad_moved = to_groups(cotangent, (attn_main,))
    grad_low = pack_rows(grad_moved + [cotangent[GROUPS]], (attn_rest,))

    slots = jnp.stack([slot_of(member ^ step) for step in range(members)]).astype(jnp.int32)
    swapped = []
    for step in range(members):
        part = attn_main[step * main_own:(step + 1) * main_own, :mine_cols]
        swapped.append(part if step == 0 else lax.ppermute(part, "seq", member_perm(step)))
    attn_in = join_heads(slots, swapped, attn_rest)
    resid = jnp.concatenate([main_rows, rest_f32], axis=0)
    branch_one = dot(attn_in, w_out)
    middle = resid + branch_one
    second_in = (middle * norm_scale(middle) * gain_two).astype(BF)
    ff_ins = (second_in, grad_low, w_gate, w_up, w_down)
    sums_two, sums_gs, ff_sent = ff_half(there, *ff_ins, None)
    branch_two, grad_second, ff_kept = ff_half(here_place, *ff_ins, (sums_two, sums_gs))
    ff_now = add_low(ff_kept, core_move(ff_sent))
    img_fours = [list(range(i, i + 4)) for i in range(0, n_img, 4)]
    same_member = [[g * members + r for g in range(GROUPS)] for r in range(members)]
    ff_quarter = lax.psum_scatter(ff_now, "img", scatter_dimension=0, axis_index_groups=img_fours)
    branch_two = hold(branch_two, (ff_now,))
    result = middle + branch_two
    squares = jnp.stack([masked_squares(v, row_mask) for v in (resid, branch_one, branch_two, result)])
    valid_count = jnp.sum(row_mask)
    result_low = result.astype(BF)
    grad_out = grad_low.astype(F32)
    grad_second = hold(grad_second, (ff_now,))
    grad_mid_norm, grad_gain_two = norm_back(middle, gain_two, grad_second)
    grad_mid = grad_out + grad_mid_norm
    grad_mid_low = grad_mid.astype(BF)

    main_grads = []
    for step in range(members):
        rows_of = lax.dynamic_slice_in_dim(w_out, slot_of(member ^ step) * mine_cols, mine_cols, 0)
        part = dot_nt(grad_mid_low[:main_own], rows_of).astype(BF)
        if pad_cols:
            part = jnp.pad(part, ((0, 0), (0, pad_cols)))
        main_grads.append(part if step == 0 else lax.ppermute(part, "seq", member_perm(step)))
    grad_attn_main = pack_rows(main_grads)
    grad_attn_rest = dot_nt(grad_mid_low[main_own:], w_out).astype(BF)

    dq_rest, dk_rest, dv_rest, first_own_rest, first_part_rest = attend_back(
        zero_place, query_rest, key_rest, value_rest, ext_rest, logs_rest, attn_rest, grad_attn_rest,
        (w_query, w_key, w_value), q_rows, 0)
    layer_got = hold_all(sent_home(result_low), (dq_rest,))
    layer_out = placed(result_low, layer_got)
    by_owner = hold(first_part_rest, (layer_out,)).reshape(GROUPS, members, block_len, width)
    by_group = lax.dynamic_index_in_dim(by_owner, member, 1, keepdims=False).astype(F32)
    for step in range(1, members):
        part = lax.dynamic_index_in_dim(by_owner, member ^ step, 1, keepdims=False)
        by_group = by_group + lax.ppermute(part, "seq", member_perm(step)).astype(F32)
    by_group = by_group.astype(BF)
    rest_parts = [lax.dynamic_index_in_dim(by_group, group ^ step, 0, keepdims=False) for step in range(GROUPS)]

    half_width = width // 2
    rest_ins = [(first_rest, False), (dq_rest, True), (first_rest_all, False), (dk_rest, True),
                (dv_rest, True), (attn_in, False), (grad_mid_low, True)]
    qkv_sent = grad_part(there, rest_ins, [
        (0, 0, [(0, 1)]), (0, half_width, [(5, 6)]), (1, 0, [(2, 3)]), (1, half_width, [(2, 4)])],
        (dq_rest,))
    rest_got = [z_move(rest_parts[step], step) for step in range(1, GROUPS)]
    rest_got = hold_all(rest_got, (qkv_sent, grad_attn_main))
    ff_quarter = hold(ff_quarter, rest_got)
    ff_shard = lax.psum_scatter(ff_quarter, "seq", scatter_dimension=0, axis_index_groups=same_member)
    for move in more_moves:
        ff_shard = add_low(ff_shard, move(ff_shard))
    dq_main, dk_main, dv_main, first_own_main, first_far_main = attend_back(
        main_place, query_main, key_main, value_main, ext_main, logs_main, attn_main, grad_attn_main,
        main_weights, min(256, block_len * 2), main_own, (ff_quarter,))

    def in_half(part):
        part = part[:, :mine_cols]
        if mine_cols == width // 2:
            return part
        empty = jnp.zeros((part.shape[0], width // 2), part.dtype)
        return lax.dynamic_update_slice_in_dim(empty, part, (member // 2) * mine_cols, 1)

    main_ins = [(first_all, False), (in_half(dq_main), False), (in_half(dk_main), False),
                (in_half(dv_main), False)]
    qkv_kept = grad_part(here_place, rest_ins + main_ins, [
        (0, 0, [(0, 1), (7, 8)]), (0, half_width, [(5, 6)]),
        (1, 0, [(2, 3), (7, 9)]), (1, half_width, [(2, 4), (7, 10)])])
    ff_shard = hold(ff_shard, (qkv_kept,))
    ff_groups = lax.all_gather(ff_shard, "seq", axis=0, axis_index_groups=same_member)
    kx, sx, ky, sy = split_cores(here_place, qkv_kept, core_move(qkv_sent))

    small = jnp.concatenate([grad_gain_two, squares, valid_count[None]])
    small = jnp.pad(small, (0, -small.size % 1024)).reshape(-1, 128)
    for move in [core_move] + more_moves:
        small = small + move(small)

    got, sx, sy = hold_all([img_moves[0](small), img_moves[0](sx), img_moves[1](sy)])
    small = small + got
    kx, sx, ky, sy = add_pairs(kx, sx, ky, sy)

    ff_groups = hold(ff_groups, (kx,))
    ff_own = lax.all_gather(ff_groups, "img", axis=0, axis_index_groups=img_fours)
    far = [first_far_main[(step - 1) * main_own:step * main_own] for step in range(1, members)]
    got, sx, sy, *far = hold_all(
        [img_moves[1](small), img_moves[1](sx), img_moves[0](sy)]
        + [lax.ppermute(part, "seq", member_perm(step + 1)) for step, part in enumerate(far)])
    small = small + got
    shards = add_fours(kx, sx, ky, sy)
    grad_first_main = first_own_main + sum(part.astype(F32) for part in far)
    grad_first_rest = first_own_rest + rest_parts[0].astype(F32) + sum(part.astype(F32) for part in rest_got)
    grad_first = jnp.concatenate([grad_first_main, grad_first_rest], axis=0)
    grad_input_rows = (grad_mid + norm_back(resid, gain_one, grad_first)[0]).astype(BF)

    got, *pieces = hold_all([z_moves[0](small)] + [z_move(shards[step], step) for step in range(1, GROUPS)])
    small = small + got
    qkv_total = sum_shards([shards[0]] + pieces, (grad_input_rows,))
    for move in more_moves:
        qkv_total = add_low(qkv_total, move(qkv_total))

    got, *pieces = hold_all([z_moves[1](small)] + [z_move(qkv_total, step) for step in range(1, GROUPS)])
    small = (small + got).reshape(-1)
    x, y = stack_orders([qkv_total] + pieces)
    rx, ry, *got = hold_all([img_moves[1](x), img_moves[0](y)] + sent_home(grad_input_rows))
    near = stack_pairs(x, rx, y, ry)
    grad_input = placed(grad_input_rows, got)
    ff_own = hold(ff_own, (rx, ry))
    sum_gate, sum_up, sum_down = assemble_ff(here_place, ff_own, core_move(ff_own), w_gate.shape[1])
    rx, ry, cx, cy = hold_all(
        [img_moves[0](near[0]), img_moves[1](near[1]), core_move(near[0]), core_move(near[1])],
        (grad_input, sum_gate))
    pieces = [near[0], rx, cx, core_move(rx), near[1], ry, cy, core_move(ry)]
    sum_query, sum_out, sum_key, sum_value, sum_gain_one = assemble(
        here_place, pieces, (w_query, w_key, w_value), gain_one[:, None])
    sum_gain_one = sum_gain_one.reshape(width)
    sum_gain_two, sum_squares, sum_count = small[:width], small[width:width + 4], small[width + 4]
    rms_stats = jnp.sqrt(sum_squares / (sum_count * width))
    return (layer_out, grad_input, sum_gain_one, sum_query, sum_key, sum_value, sum_out,
            sum_gain_two, sum_gate, sum_up, sum_down, rms_stats)


def solution(mesh):
    rows = P("img", "seq", None)
    return jax.shard_map(
        functools.partial(body, mesh.shape["img"], mesh.shape["seq"]),
        mesh=mesh,
        in_specs=(rows, P("img"), P(), P(), P(), P(), P(), P(), P(), P(), P(), rows),
        out_specs=(rows, rows, P(), P(), P(), P(), P(), P(), P(), P(), P(), P()),
        check_vma=False,
    )
```

```python
import functools
import math

import jax
import jax.numpy as jnp
from jax import lax
from jax.experimental import pallas as pl
from jax.experimental.pallas import tpu as pltpu
from jax.sharding import PartitionSpec as P

HEADS = 12
GROUPS = 4
REST_PER = 3
SHARDS = 16
EPS = 1e-06
NEG = -1000000000.0
LOG2E = 1.4426950408889634
LN2 = 0.6931471805599453
GELU_C = 0.7978845608028654
GELU_A = 0.044715
BF = jnp.bfloat16
F32 = jnp.float32
VMEM_LIMIT = 56 * 1024 * 1024
ANY = pl.BlockSpec(memory_space=pl.ANY)


def dot(left, right):
    return jnp.dot(left, right, preferred_element_type=F32)


def dot_nt(left, right):
    return lax.dot_general(left, right, (((1,), (1,)), ((), ())), preferred_element_type=F32)


def dot_tn(left, right):
    return lax.dot_general(left, right, (((0,), (0,)), ((), ())), preferred_element_type=F32)


def split_three(column):
    hi = column.astype(BF).astype(F32)
    rest = column - hi
    mid = rest.astype(BF).astype(F32)
    return hi, mid, rest - mid


def extras(rows, columns):
    lane = lax.broadcasted_iota(jnp.int32, (rows, 128), 1)
    out = jnp.zeros((rows, 128), F32)
    for index, column in enumerate(columns):
        if column is not None:
            out = jnp.where(lane == index, column, out)
    return out.astype(BF)


def head_lanes(values, half):
    lane = lax.broadcasted_iota(jnp.int32, values.shape, 1)
    return jnp.where((lane < 64) if half == 0 else (lane >= 64), values, jnp.zeros_like(values))


def stack_heads(values):
    return jnp.concatenate([head_lanes(values, 0), head_lanes(values, 1)], axis=0)


def attend_kernel(q_rows, per, place_ref, fiq_ref, fik_ref, wq_ref, wk_ref, wv_ref, ext_ref, *refs):
    q_ref, k_ref, v_ref, log_ref, out_ref = refs[-5:]
    scale = LOG2E / math.sqrt(64.0)
    both = dot(fik_ref[...], jnp.concatenate([wk_ref[...], wv_ref[...]], axis=1)).astype(BF)
    every_query = (dot(fiq_ref[...], wq_ref[...]) * scale).astype(BF)
    ext = ext_ref[...]
    one = extras(2 * q_rows, (None, None, None, 1.0))
    for pair in range(per):
        lanes = slice(128 * pair, 128 * (pair + 1))
        key_pair, value_pair = both[:, lanes], both[:, 128 * (per + pair):128 * (per + pair + 1)]
        query = every_query[:, lanes]
        k_ref[pair] = key_pair
        v_ref[pair] = value_pair
        q_ref[pair] = query
        keys = jnp.concatenate([key_pair, ext], axis=1)
        values = jnp.concatenate([value_pair, ext], axis=1)
        for start in range(0, fiq_ref.shape[0], q_rows):
            rows = slice(start, start + q_rows)
            scores = dot_nt(jnp.concatenate([stack_heads(query[rows]), one], axis=1), keys)
            top = jnp.max(scores, axis=1, keepdims=True)
            weights = jnp.exp2(scores - top).astype(BF)
            mixed = dot(weights, values)
            norm = mixed[:, 128:129]
            logs = extras(2 * q_rows, split_three(-(top + jnp.log2(norm))) + (1.0,))
            log_ref[2 * pair, rows, :] = logs[:q_rows]
            log_ref[2 * pair + 1, rows, :] = logs[q_rows:]
            scaled = mixed[:, :128] / norm
            lane = lax.broadcasted_iota(jnp.int32, (q_rows, 128), 1)
            out_ref[rows, lanes] = jnp.where(lane < 64, scaled[:q_rows], scaled[q_rows:]).astype(BF)


def attend(place, fi_q, fi_k, w_query, w_key, w_value, ext, pairs, q_rows, after=(), per=1):
    q_total, width = fi_q.shape
    k_total = fi_k.shape[0]
    column = lambda i, p: (0, p[0] * (pairs // per) + i)
    whole = lambda i, p: (0, 0)
    stacked = lambda i, p: (i, 0, 0)
    return pl.pallas_call(
        functools.partial(attend_kernel, q_rows, per),
        grid_spec=pltpu.PrefetchScalarGridSpec(
            num_scalar_prefetch=1,
            grid=(pairs // per,),
            in_specs=[
                pl.BlockSpec((q_total, width), whole),
                pl.BlockSpec((k_total, width), whole),
                pl.BlockSpec((width, 128 * per), column),
                pl.BlockSpec((width, 128 * per), column),
                pl.BlockSpec((width, 128 * per), column),
                pl.BlockSpec((k_total, 128), whole),
            ] + [ANY] * len(after),
            out_specs=[
                pl.BlockSpec((per, q_total, 128), stacked),
                pl.BlockSpec((per, k_total, 128), stacked),
                pl.BlockSpec((per, k_total, 128), stacked),
                pl.BlockSpec((2 * per, q_total, 128), stacked),
                pl.BlockSpec((q_total, 128 * per), lambda i, p: (0, i)),
            ],
        ),
        out_shape=[
            jax.ShapeDtypeStruct((pairs, q_total, 128), BF),
            jax.ShapeDtypeStruct((pairs, k_total, 128), BF),
            jax.ShapeDtypeStruct((pairs, k_total, 128), BF),
            jax.ShapeDtypeStruct((2 * pairs, q_total, 128), BF),
            jax.ShapeDtypeStruct((q_total, pairs * 128), BF),
        ],
        compiler_params=pltpu.CompilerParams(vmem_limit_bytes=VMEM_LIMIT),
        cost_estimate=pl.CostEstimate(
            flops=4 * 128 * pairs * (4 * q_total * k_total + width * (q_total + 2 * k_total)),
            bytes_accessed=2 * (q_total + k_total) * width * 4,
            transcendentals=2 * pairs * q_total * k_total,
        ),
    )(place, fi_q, fi_k, w_query, w_key, w_value, ext, *after)


def attend_back_kernel(q_rows, own_rows, per, place_ref, q_ref, k_ref, v_ref, ext_ref, log_ref, out_ref,
                       grad_ref, wq_ref, wk_ref, wv_ref, *refs):
    dq_ref, dk_ref, dv_ref, own_ref, far_ref, sum_q, sum_k = refs[-7:]
    del place_ref
    step = pl.program_id(0)

    @pl.when(step == 0)
    def _():
        if not own_rows:
            sum_q[...] = jnp.zeros_like(sum_q)
        sum_k[...] = jnp.zeros_like(sum_k)

    ext = ext_ref[...]
    for pair in range(per):
        lanes = slice(128 * pair, 128 * (pair + 1))
        key_pair = k_ref[pair]
        keys = jnp.concatenate([key_pair, ext], axis=1)
        values = jnp.concatenate([v_ref[pair], ext], axis=1)
        keys_trans = jnp.transpose(key_pair.astype(F32)).astype(BF)
        dk_sum = jnp.zeros(key_pair.shape, F32)
        dv_sum = jnp.zeros(key_pair.shape, F32)
        for start in range(0, q_ref.shape[1], q_rows):
            rows = slice(start, start + q_rows)
            grad = grad_ref[rows, lanes]
            product = grad.astype(F32) * out_ref[rows, lanes].astype(F32)
            delta = jnp.sum(stack_heads(product), axis=1, keepdims=True)
            grad_h = stack_heads(grad)
            query_h = stack_heads(q_ref[pair, rows, :])
            logs = jnp.concatenate([log_ref[2 * pair, rows, :], log_ref[2 * pair + 1, rows, :]], axis=0)
            probs = jnp.exp2(dot_nt(keys, jnp.concatenate([query_h, logs], axis=1)))
            centred = dot_nt(
                values, jnp.concatenate([grad_h, extras(2 * q_rows, split_three(-delta))], axis=1))
            grad_scores = (probs * centred).astype(BF)
            dv_sum = dv_sum + dot(probs.astype(BF), grad_h)
            dk_sum = dk_sum + dot(grad_scores, query_h)
            first = dot(keys_trans[:64], grad_scores[:, :q_rows])
            second = dot(keys_trans[64:], grad_scores[:, q_rows:])
            dq_ref[rows, lanes] = (
                jnp.transpose(jnp.concatenate([first, second], axis=0)) * 0.125).astype(BF)
        dk_ref[:, lanes] = (dk_sum * LN2).astype(BF)
        dv_ref[:, lanes] = dv_sum.astype(BF)
    dk, dv = dk_ref[...], dv_ref[...]
    if own_rows:
        sum_k[...] += dot_nt(
            jnp.concatenate([dq_ref[...], dk, dv], axis=1),
            jnp.concatenate([wq_ref[...], wk_ref[...], wv_ref[...]], axis=1))
    else:
        sum_q[...] += dot_nt(dq_ref[...], wq_ref[...])
        sum_k[...] += dot_nt(
            jnp.concatenate([dk, dv], axis=1), jnp.concatenate([wk_ref[...], wv_ref[...]], axis=1))

    @pl.when(step == pl.num_programs(0) - 1)
    def _():
        if own_rows:
            own_ref[...] = sum_k[:own_rows]
            far_ref[...] = sum_k[own_rows:].astype(BF)
        else:
            own_ref[...] = sum_q[...]
            far_ref[...] = sum_k[...].astype(BF)


def attend_back(place, query, key, value, ext, logs, out, grad, weights, q_rows, own_rows, after=(), per=1):
    pairs, q_total, _ = query.shape
    k_total = key.shape[1]
    width = weights[0].shape[0]
    stacked = lambda i, p: (i, 0, 0)
    flat = lambda i, p: (0, i)
    whole = lambda i, p: (0, 0)
    column = pl.BlockSpec((width, 128 * per), lambda i, p: (0, p[0] * (pairs // per) + i))
    shapes = [(own_rows, width), (k_total - own_rows, width)] if own_rows else [(q_total, width), (k_total, width)]
    return pl.pallas_call(
        functools.partial(attend_back_kernel, q_rows, own_rows, per),
        grid_spec=pltpu.PrefetchScalarGridSpec(
            num_scalar_prefetch=1,
            grid=(pairs // per,),
            in_specs=[
                pl.BlockSpec((per, q_total, 128), stacked),
                pl.BlockSpec((per, k_total, 128), stacked),
                pl.BlockSpec((per, k_total, 128), stacked),
                pl.BlockSpec((k_total, 128), whole),
                pl.BlockSpec((2 * per, q_total, 128), stacked),
                pl.BlockSpec((q_total, 128 * per), flat),
                pl.BlockSpec((q_total, 128 * per), flat),
                column, column, column,
            ] + [ANY] * len(after),
            out_specs=[
                pl.BlockSpec((q_total, 128 * per), flat),
                pl.BlockSpec((k_total, 128 * per), flat),
                pl.BlockSpec((k_total, 128 * per), flat),
                pl.BlockSpec(shapes[0], whole),
                pl.BlockSpec(shapes[1], whole),
            ],
            scratch_shapes=[
                pltpu.VMEM((8 if own_rows else q_total, width), F32), pltpu.VMEM((k_total, width), F32)],
        ),
        out_shape=[
            jax.ShapeDtypeStruct((q_total, pairs * 128), BF),
            jax.ShapeDtypeStruct((k_total, pairs * 128), BF),
            jax.ShapeDtypeStruct((k_total, pairs * 128), BF),
            jax.ShapeDtypeStruct(shapes[0], F32),
            jax.ShapeDtypeStruct(shapes[1], BF),
        ],
        compiler_params=pltpu.CompilerParams(vmem_limit_bytes=VMEM_LIMIT),
        cost_estimate=pl.CostEstimate(
            flops=2 * 256 * pairs * 5 * q_total * k_total,
            bytes_accessed=2 * 128 * pairs * (4 * q_total + 4 * k_total),
            transcendentals=2 * pairs * q_total * k_total,
        ),
    )(place, query, key, value, ext, logs, out, grad, *weights, *after)


FF_TILE = 256
FF_STEP = 512


def ff_kernel(first, place_ref, second_ref, grad_ref, wg_ref, wu_ref, wd_ref, *refs):
    two_ref, gs_ref, part_ref, second_t_ref = refs[-4:]
    step = pl.program_id(0)

    @pl.when(step == 0)
    def _():
        second_t_ref[...] = jnp.transpose(second_ref[...])
        if first:
            two_ref[...] = jnp.zeros_like(two_ref)
            gs_ref[...] = jnp.zeros_like(gs_ref)
        else:
            two_ref[...] = refs[0][...]
            gs_ref[...] = refs[1][...]

    second, grad = second_ref[...], grad_ref[...]
    gate = dot(second, wg_ref[...])
    up = dot(second, wu_ref[...])
    grad_inner = dot_nt(grad, wd_ref[...])
    square = gate * gate
    half_plus = 0.5 + 0.5 * jnp.tanh(gate * (GELU_C + (GELU_C * GELU_A) * square))
    gelu = gate * half_plus
    slope = half_plus + gelu * (1.0 - half_plus) * (2.0 * GELU_C + (6.0 * GELU_C * GELU_A) * square)
    inner = (gelu * up).astype(BF)
    grad_gate = (grad_inner * up * slope).astype(BF)
    grad_up = (grad_inner * gelu).astype(BF)
    two_ref[...] += dot(inner, wd_ref[...])
    gs_ref[...] += dot_nt(grad_gate, wg_ref[...]) + dot_nt(grad_up, wu_ref[...])
    width = second.shape[1]
    shard, shard_down = width // SHARDS, 2 * FF_TILE // SHARDS
    part_gate = dot(second_t_ref[...], grad_gate).astype(BF)
    part_up = dot(second_t_ref[...], grad_up).astype(BF)
    part_down = dot_tn(inner, grad).astype(BF)
    shape = (4, 4, shard, FF_TILE)
    for odd in range(FF_STEP // FF_TILE):
        here = slice(FF_TILE * odd, FF_TILE * (odd + 1))
        part_ref[:, :, shard * odd:shard * (odd + 1), :] = part_gate[:, here].reshape(shape)
        part_ref[:, :, shard * (2 + odd):shard * (3 + odd), :] = part_up[:, here].reshape(shape)
        for tile in range(width // FF_TILE):
            at = 4 * shard + shard_down * tile
            part_ref[2 * odd:2 * odd + 2, :, at:at + shard_down, :] = (
                part_down[here, FF_TILE * tile:FF_TILE * (tile + 1)].reshape(2, 4, shard_down, FF_TILE))


def ff_half(place, second, grad, w_gate, w_up, w_down, sums, after=()):
    rows, width = second.shape
    tiles = w_gate.shape[1] // FF_STEP // 2
    tile_at = lambda j, p: j * 2 + p[0]
    whole = lambda j, p: (0, 0)
    sum_spec = pl.BlockSpec((rows, width), whole)
    columns = pl.BlockSpec((width, FF_STEP), lambda j, p: (0, tile_at(j, p)))
    shard_rows = 4 * (width // SHARDS) + (2 * FF_TILE // SHARDS) * (width // FF_TILE)
    return pl.pallas_call(
        functools.partial(ff_kernel, sums is None),
        grid_spec=pltpu.PrefetchScalarGridSpec(
            num_scalar_prefetch=1,
            grid=(tiles,),
            in_specs=[
                pl.BlockSpec((rows, width), whole), pl.BlockSpec((rows, width), whole),
                columns, columns, pl.BlockSpec((FF_STEP, width), lambda j, p: (tile_at(j, p), 0)),
            ] + [sum_spec] * (0 if sums is None else 2) + [ANY] * len(after),
            out_specs=[sum_spec, sum_spec,
                       pl.BlockSpec((4, 4, shard_rows, FF_TILE), lambda j, p: (0, 0, j, 0))],
            scratch_shapes=[pltpu.VMEM((width, rows), BF)],
        ),
        out_shape=[jax.ShapeDtypeStruct((rows, width), F32)] * 2
        + [jax.ShapeDtypeStruct((4, 4, 2 * shard_rows, FF_TILE), BF)],
        compiler_params=pltpu.CompilerParams(vmem_limit_bytes=VMEM_LIMIT),
        cost_estimate=pl.CostEstimate(
            flops=18 * rows * width * tiles * FF_STEP,
            bytes_accessed=12 * width * tiles * FF_STEP + 16 * rows * width,
            transcendentals=rows * tiles * FF_STEP),
    )(place, second, grad, w_gate, w_up, w_down, *(sums or ()), *after)


def split_kernel(place_ref, *refs):
    ins, outs = refs[:8], refs[-4:]
    for index, out in enumerate(outs):
        for step in range(4):
            at = jnp.bitwise_xor(place_ref[3], step)
            out[0, step] = (ins[index][0, 0, at].astype(F32) + ins[4 + index][0, 0, at].astype(F32)).astype(BF)


def split_cores(place, kept, got, after=()):
    tail = kept.shape[3:]

    def spec(order, away):
        def at(b, p):
            first, second = p[1 + order] ^ away, p[2 - order] ^ b
            return (order, first + 2 * second if order == 0 else second + 2 * first, 0, 0, 0)
        return pl.BlockSpec((1, 1, 4) + tail, at)

    specs = [spec(order, away) for order in range(2) for away in range(2)]
    out = pl.BlockSpec((1, 4) + tail, lambda b, p: (b, 0, 0, 0))
    return pl.pallas_call(
        split_kernel,
        grid_spec=pltpu.PrefetchScalarGridSpec(
            num_scalar_prefetch=1, grid=(2,), in_specs=specs * 2 + [ANY] * len(after), out_specs=[out] * 4),
        out_shape=[jax.ShapeDtypeStruct((2, 4) + tail, BF)] * 4,
        compiler_params=pltpu.CompilerParams(vmem_limit_bytes=VMEM_LIMIT),
        cost_estimate=pl.CostEstimate(flops=0, bytes_accessed=6 * kept.size, transcendentals=0),
    )(place, *([kept] * 4), *([got] * 4), *after)


def hold(array, after):
    return pl.pallas_call(
        lambda *refs: None,
        in_specs=[ANY] * (1 + len(after)),
        out_specs=ANY,
        out_shape=jax.ShapeDtypeStruct(array.shape, array.dtype),
        input_output_aliases={0: 0},
        cost_estimate=pl.CostEstimate(flops=0, bytes_accessed=0, transcendentals=0),
    )(array, *after)


def hold_all(arrays, after=()):
    return pl.pallas_call(
        lambda *refs: None,
        in_specs=[ANY] * (len(arrays) + len(after)),
        out_specs=[ANY] * len(arrays),
        out_shape=[jax.ShapeDtypeStruct(a.shape, a.dtype) for a in arrays],
        input_output_aliases={i: i for i in range(len(arrays))},
        cost_estimate=pl.CostEstimate(flops=0, bytes_accessed=0, transcendentals=0),
    )(*arrays, *after)


def pack_rows_kernel(count, *refs):
    at = 0
    for ref in refs[:count]:
        rows = ref.shape[0]
        refs[-1][at:at + rows, :] = ref[...]
        at += rows


def pack_rows(pieces, after=()):
    rows = sum(p.shape[0] for p in pieces)
    shape = (rows, pieces[0].shape[1])
    return pl.pallas_call(
        functools.partial(pack_rows_kernel, len(pieces)),
        in_specs=[pl.BlockSpec(p.shape, lambda: (0, 0)) for p in pieces] + [ANY] * len(after),
        out_specs=pl.BlockSpec(shape, lambda: (0, 0)),
        out_shape=jax.ShapeDtypeStruct(shape, pieces[0].dtype),
        cost_estimate=pl.CostEstimate(flops=0, bytes_accessed=0, transcendentals=0),
    )(*pieces, *after)


def join_heads_kernel(members, slots_ref, *refs):
    pieces, rest_ref, out_ref = refs[:members], refs[members], refs[members + 1]
    rows, cols = pieces[0].shape
    for index in range(members):
        for slot in range(members):
            @pl.when(slots_ref[index] == slot)
            def _():
                out_ref[0:rows, slot * cols:(slot + 1) * cols] = pieces[index][...]
    out_ref[rows:, :] = rest_ref[...]


def join_heads(slots, pieces, rest):
    rows, cols = pieces[0].shape
    members = len(pieces)
    shape = (rows + rest.shape[0], members * cols)
    block = lambda a: pl.BlockSpec(a.shape, lambda j, p: (0, 0))
    return pl.pallas_call(
        functools.partial(join_heads_kernel, members),
        grid_spec=pltpu.PrefetchScalarGridSpec(
            num_scalar_prefetch=1, grid=(1,), in_specs=[block(p) for p in pieces] + [block(rest)],
            out_specs=pl.BlockSpec(shape, lambda j, p: (0, 0))),
        out_shape=jax.ShapeDtypeStruct(shape, rest.dtype),
        cost_estimate=pl.CostEstimate(flops=0, bytes_accessed=0, transcendentals=0),
    )(slots, *pieces, rest)


def place_rows_kernel(place_ref, *refs):
    pieces, out_ref = refs[:-1], refs[-1]
    for step in range(GROUPS):
        out_ref[(place_ref[3] + step) % GROUPS] = pieces[step][...]
    for index in range(GROUPS, len(pieces)):
        out_ref[index] = pieces[index][...]


def place_rows(place, pieces):
    block = pl.BlockSpec(pieces[0].shape, lambda j, p: (0, 0))
    shape = (len(pieces),) + pieces[0].shape
    return pl.pallas_call(
        place_rows_kernel,
        grid_spec=pltpu.PrefetchScalarGridSpec(
            num_scalar_prefetch=1, grid=(1,), in_specs=[block] * len(pieces),
            out_specs=pl.BlockSpec(shape, lambda j, p: (0, 0, 0))),
        out_shape=jax.ShapeDtypeStruct(shape, pieces[0].dtype),
        cost_estimate=pl.CostEstimate(flops=0, bytes_accessed=0, transcendentals=0),
    )(place, *pieces)


def add_kernel(x_ref, rx_ref, y_ref, ry_ref, *refs):
    outs = refs[-4:]
    for index in range(2):
        outs[index][...] = add_low(x_ref[index], rx_ref[index])
        outs[2 + index][...] = add_low(y_ref[index], ry_ref[index])


def add_pairs(x, rx, y, ry, after=()):
    tail = x.shape[2:]
    return pl.pallas_call(
        add_kernel,
        grid=(4,),
        in_specs=[pl.BlockSpec((2, 1) + tail, lambda j: (0, j, 0, 0))] * 4 + [ANY] * len(after),
        out_specs=[pl.BlockSpec((1,) + tail, lambda j: (j, 0, 0))] * 4,
        out_shape=[jax.ShapeDtypeStruct((4,) + tail, BF)] * 4,
        compiler_params=pltpu.CompilerParams(vmem_limit_bytes=VMEM_LIMIT),
        cost_estimate=pl.CostEstimate(flops=0, bytes_accessed=12 * x.size, transcendentals=0),
    )(x, rx, y, ry, *after)


def add_four_kernel(x_ref, rx_ref, y_ref, ry_ref, *refs):
    outs = refs[-4:]
    for index in range(4):
        outs[index][0] = add_low(x_ref[index], rx_ref[index])
        outs[index][1] = add_low(y_ref[index], ry_ref[index])


def add_fours(x, rx, y, ry, after=()):
    tail = x.shape[1:]
    whole = pl.BlockSpec(x.shape, lambda j: (0, 0, 0))
    return pl.pallas_call(
        add_four_kernel,
        grid=(1,),
        in_specs=[whole] * 4 + [ANY] * len(after),
        out_specs=[pl.BlockSpec((2,) + tail, lambda j: (0, 0, 0))] * 4,
        out_shape=[jax.ShapeDtypeStruct((2,) + tail, BF)] * 4,
        compiler_params=pltpu.CompilerParams(vmem_limit_bytes=VMEM_LIMIT),
        cost_estimate=pl.CostEstimate(flops=0, bytes_accessed=12 * x.size, transcendentals=0),
    )(x, rx, y, ry, *after)


def sum_kernel(*refs):
    total = refs[0][...].astype(F32)
    for ref in refs[1:GROUPS]:
        total = total + ref[...].astype(F32)
    refs[-1][...] = total.astype(BF)


def sum_shards(shards, after=()):
    whole = pl.BlockSpec(shards[0].shape, lambda: (0, 0, 0))
    return pl.pallas_call(
        sum_kernel,
        in_specs=[whole] * GROUPS + [ANY] * len(after),
        out_specs=whole,
        out_shape=jax.ShapeDtypeStruct(shards[0].shape, BF),
        cost_estimate=pl.CostEstimate(flops=0, bytes_accessed=0, transcendentals=0),
    )(*shards, *after)


def stack_orders_kernel(*refs):
    for order in range(2):
        for index in range(GROUPS):
            refs[order - 2][index] = refs[index][order]


def stack_orders(pieces, after=()):
    tail = pieces[0].shape[1:]
    return pl.pallas_call(
        stack_orders_kernel,
        in_specs=[pl.BlockSpec((2,) + tail, lambda: (0, 0, 0))] * GROUPS + [ANY] * len(after),
        out_specs=[pl.BlockSpec((GROUPS,) + tail, lambda: (0, 0, 0))] * 2,
        out_shape=[jax.ShapeDtypeStruct((GROUPS,) + tail, BF)] * 2,
        cost_estimate=pl.CostEstimate(flops=0, bytes_accessed=0, transcendentals=0),
    )(*pieces, *after)


def stack_pairs_kernel(x_ref, rx_ref, y_ref, ry_ref, *refs):
    refs[-2][0] = x_ref[...]
    refs[-2][1] = rx_ref[...]
    refs[-1][0] = y_ref[...]
    refs[-1][1] = ry_ref[...]


def stack_pairs(x, rx, y, ry, after=()):
    tail = x.shape[1:]
    block = pl.BlockSpec((1,) + tail, lambda j: (j, 0, 0))
    return pl.pallas_call(
        stack_pairs_kernel,
        grid=(GROUPS,),
        in_specs=[block] * 4 + [ANY] * len(after),
        out_specs=[pl.BlockSpec((2, 1) + tail, lambda j: (0, j, 0, 0))] * 2,
        out_shape=[jax.ShapeDtypeStruct((2,) + x.shape, BF)] * 2,
        cost_estimate=pl.CostEstimate(flops=0, bytes_accessed=0, transcendentals=0),
    )(x, rx, y, ry, *after)


def grad_kernel(columns, place_ref, *refs):
    ins, part_ref = refs[:-1], refs[-1]
    for order, at, terms in columns:
        total = None
        for left, right in terms:
            term = dot_tn(ins[left][...], ins[right][...])
            total = term if total is None else total + term
        rows, cols = total.shape
        part_ref[order, :, :, :, at:at + cols] = total.astype(BF).reshape(4, 4, rows // SHARDS, cols)


def grad_part(place, ins, columns, after=()):
    specs = []
    for array, halved in ins:
        depth, cols = array.shape
        if halved:
            specs.append(pl.BlockSpec((depth, cols // 2), lambda j, p: (0, p[0])))
        else:
            specs.append(pl.BlockSpec((depth, cols), lambda j, p: (0, 0)))
    rows = ins[0][0].shape[1]
    shape = (2, 4, 4, rows // SHARDS, rows)
    return pl.pallas_call(
        functools.partial(grad_kernel, columns),
        grid_spec=pltpu.PrefetchScalarGridSpec(
            num_scalar_prefetch=1,
            grid=(1,),
            in_specs=specs + [ANY] * len(after),
            out_specs=pl.BlockSpec(shape, lambda j, p: (0, 0, 0, 0, 0)),
        ),
        out_shape=jax.ShapeDtypeStruct(shape, BF),
        compiler_params=pltpu.CompilerParams(vmem_limit_bytes=VMEM_LIMIT),
        cost_estimate=pl.CostEstimate(
            flops=sum(2 * rows * (rows // 2) * ins[left][0].shape[0]
                      for _, _, terms in columns for left, _ in terms),
            bytes_accessed=sum(2 * a.size for a, _ in ins), transcendentals=0),
    )(place, *[a for a, _ in ins], *after)


def from_pieces(place_ref, refs, order, group):
    here_ref, away_ref, other_here_ref, other_away_ref = refs[4 * order:4 * order + 4]
    quarter = pl.program_id(0)
    bit = quarter % 2 if order == 0 else quarter // 2
    near = place_ref[1 + order] == bit
    at = jnp.bitwise_xor(place_ref[3], group)
    own = jnp.where(near, here_ref[0, at], away_ref[0, at]).astype(F32)
    other = jnp.where(near, other_here_ref[0, at], other_away_ref[0, at]).astype(F32)
    lower = place_ref[0] == 0
    return jnp.where(lower, own, other), jnp.where(lower, other, own)


def assemble_ff_kernel(place_ref, own_ref, other_ref, gate_ref, up_ref, down_ref):
    shard, down = gate_ref.shape[0] // 4, down_ref.shape[2] // 4
    shard_rows = own_ref.shape[2] // 2

    def write(halves):
        for group in range(4):
            rows = slice(shard * group, shard * (group + 1))
            for half, source in enumerate(halves):
                for order in range(2):
                    base = order * shard_rows
                    for tile in range(2):
                        at = ((order * 2 + half) * 2 + tile) * FF_TILE
                        gate_ref[rows, at:at + FF_TILE] = source[
                            0, group, base + shard * tile:base + shard * (tile + 1)].astype(F32)
                        up_ref[rows, at:at + FF_TILE] = source[
                            0, group, base + shard * (2 + tile):base + shard * (3 + tile)].astype(F32)
                    for tile in range(down_ref.shape[3] // FF_TILE):
                        at = base + 4 * shard + down * tile
                        down_ref[order * 2 + half, 0, down * group:down * (group + 1),
                                 FF_TILE * tile:FF_TILE * (tile + 1)] = source[
                                     0, group, at:at + down].astype(F32)

    pl.when(place_ref[0] == 0)(lambda: write((own_ref, other_ref)))
    pl.when(place_ref[0] != 0)(lambda: write((other_ref, own_ref)))


def assemble_ff(place, own, other, hidden):
    quarter = lambda rows: pl.BlockSpec((rows, hidden), lambda q, p: (q, 0))
    part = pl.BlockSpec((1,) + own.shape[1:], lambda q, p: (q, 0, 0, 0))
    rows = own.shape[2] // 2
    width = (rows * FF_TILE * SHARDS * 4) // (3 * hidden)
    gate, up, down = pl.pallas_call(
        assemble_ff_kernel,
        grid_spec=pltpu.PrefetchScalarGridSpec(
            num_scalar_prefetch=1, grid=(4,), in_specs=[part, part],
            out_specs=[quarter(width // 4), quarter(width // 4),
                       pl.BlockSpec((4, 1, hidden // 16, width), lambda q, p: (0, q, 0, 0))]),
        out_shape=[jax.ShapeDtypeStruct((width, hidden), F32)] * 2
        + [jax.ShapeDtypeStruct((4, 4, hidden // 16, width), F32)],
        compiler_params=pltpu.CompilerParams(vmem_limit_bytes=VMEM_LIMIT),
        cost_estimate=pl.CostEstimate(flops=0, bytes_accessed=12 * own.size, transcendentals=0),
    )(place, own, other)
    return gate, up, down.reshape(hidden, width)


def assemble_kernel(place_ref, *refs):
    wq_ref, wk_ref, wv_ref, gain_ref = refs[8:12]
    outs = refs[-5:-1]
    shard = outs[0].shape[0] // 4
    for order in range(2):
        for group in range(4):
            rows = slice(shard * group, shard * (group + 1))
            for half, value in enumerate(from_pieces(place_ref, refs, order, group)):
                width = value.shape[1] // 2
                for which in range(2):
                    outs[2 * order + which][rows, half * width:(half + 1) * width] = (
                        value[:, which * width:(which + 1) * width])
    products = (outs[0][...] * wq_ref[...].astype(F32) + outs[2][...] * wk_ref[...].astype(F32)
                + outs[3][...] * wv_ref[...].astype(F32))
    refs[-1][...] = jnp.sum(products, axis=1, keepdims=True) / gain_ref[...]


def assemble(place, pieces, weights, gain, after=()):
    tail = pieces[0].shape[1:]
    width = gain.shape[0]
    near = pl.BlockSpec((1,) + tail, lambda q, p: (p[2] ^ (q // 2), 0, 0, 0))
    far = pl.BlockSpec((1,) + tail, lambda q, p: (p[1] ^ (q % 2), 0, 0, 0))
    rows = pl.BlockSpec((width // 4, width), lambda q, p: (q, 0))
    column = pl.BlockSpec((width // 4, 1), lambda q, p: (q, 0))
    return pl.pallas_call(
        assemble_kernel,
        grid_spec=pltpu.PrefetchScalarGridSpec(
            num_scalar_prefetch=1, grid=(4,),
            in_specs=[near] * 4 + [far] * 4 + [rows] * 3 + [column] + [ANY] * len(after),
            out_specs=[rows] * 4 + [column]),
        out_shape=[jax.ShapeDtypeStruct((width, width), F32)] * 4 + [jax.ShapeDtypeStruct((width, 1), F32)],
        compiler_params=pltpu.CompilerParams(vmem_limit_bytes=VMEM_LIMIT),
        cost_estimate=pl.CostEstimate(
            flops=0, bytes_accessed=16 * 8 * pieces[0].size // 4, transcendentals=0),
    )(place, *pieces, *weights, gain, *after)


def add_low(left, right):
    return (left.astype(F32) + right.astype(F32)).astype(BF)


def norm_scale(values):
    return lax.rsqrt(jnp.mean(values * values, axis=-1, keepdims=True) + EPS)


def norm_back(values, gain, grad):
    scale = norm_scale(values)
    scaled = values * scale
    weighted = grad * gain
    inner = jnp.mean(weighted * scaled, axis=-1, keepdims=True)
    return scale * (weighted - scaled * inner), jnp.sum(grad * scaled, axis=0)


def masked_squares(values_in, row_mask):
    return jnp.sum(row_mask * jnp.sum(values_in * values_in, axis=-1))


def body(n_img, n_seq, patches, counts, norm_gain_one, w_query, w_key, w_value, w_out,
         norm_gain_two, w_gate, w_up, w_down, cotangent):
    charts, block_len, width = patches.shape
    members = n_seq // GROUPS
    head_count = HEADS // members
    pairs = -(-head_count // 2)
    pad_cols = pairs * 128 - head_count * 64
    mine_cols = head_count * 64
    main_own = GROUPS * block_len
    seq_len = n_seq * block_len
    here = lax.axis_index("seq")
    group, member = here // members, here % members
    img_here = lax.axis_index("img")

    def slot_of(who):
        return (who % 2) * (members // 2) + who // 2

    def bit_exchange(axis, bit):
        def move(array):
            if axis == "img":
                perm = [(i, i ^ (1 << bit)) for i in range(n_img)]
            elif axis == "group":
                perm = [(g * members + r, (g ^ (1 << bit)) * members + r)
                        for g in range(GROUPS) for r in range(members)]
            else:
                perm = [(g * members + r, g * members + (r ^ (1 << bit)))
                        for g in range(GROUPS) for r in range(members)]
            return lax.ppermute(array, "img" if axis == "img" else "seq", perm)
        return move

    img_moves = [bit_exchange("img", 0), bit_exchange("img", 1)]
    z_moves = [bit_exchange("group", 0), bit_exchange("group", 1)]

    def z_move(array, step):
        perm = [(g * members + r, (g ^ step) * members + r) for g in range(GROUPS) for r in range(members)]
        return lax.ppermute(array, "seq", perm)

    core_move = bit_exchange("member", 0)
    more_moves = [bit_exchange("img", b) for b in range(2, n_img.bit_length() - 1)]
    more_moves += [bit_exchange("member", b) for b in range(1, members.bit_length() - 1)]
    img_bits = [img_here % 2, (img_here // 2) % 2]
    half_here = member % 2

    def place_of(half):
        return jnp.stack([half] + img_bits + [group]).astype(jnp.int32)

    there, here_place = place_of(1 - half_here), place_of(half_here)

    def sum_img_first(kx, sx, ky, sy, after=()):
        return add_pairs(kx, img_moves[0](sx), ky, img_moves[1](sy), after)

    def sum_img_second(kx, sx, ky, sy, after=()):
        return add_fours(kx, img_moves[1](sx), ky, img_moves[0](sy), after)

    def sum_groups(shards, after=()):
        total = sum_shards(
            [shards[0]] + [z_move(shards[step], step) for step in range(1, GROUPS)], after)
        for move in more_moves:
            total = add_low(total, move(total))
        return total

    def quarters(total, after):
        return stack_orders([total] + [z_move(total, step) for step in range(1, GROUPS)], after)

    def halves(parts, after):
        return stack_pairs(parts[0], img_moves[1](parts[0]), parts[1], img_moves[0](parts[1]), after)

    def shift_perm(step):
        return [(g * members + r, ((g + step) % GROUPS) * members + r)
                for g in range(GROUPS) for r in range(members)]

    def member_perm(step):
        return [(g * members + r, g * members + (r ^ step))
                for g in range(GROUPS) for r in range(members)]

    def to_groups(array, after=()):
        pieces = []
        for step in range(GROUPS):
            part = lax.dynamic_index_in_dim(array, (group + step) % GROUPS, 0, keepdims=False)
            if step:
                part = lax.ppermute(hold(part, after) if after else part, "seq", shift_perm(step))
            pieces.append(part)
        return pieces

    def sent_home(rows):
        return [lax.ppermute(rows[step * block_len:(step + 1) * block_len], "seq", shift_perm(-step))
                for step in range(1, GROUPS)]

    def placed(rows, got):
        return place_rows(here_place, [rows[:block_len], *got, rows[main_own:]])

    def to_members(own):
        return [own] + [lax.ppermute(own, "seq", member_perm(step)) for step in range(1, members)]

    def columns_of(weight, who):
        part = lax.dynamic_slice_in_dim(weight, who * mine_cols, mine_cols, 1)
        return jnp.pad(part, ((0, 0), (0, pad_cols))) if pad_cols else part

    gain_one = norm_gain_one.astype(F32)
    gain_two = norm_gain_two.astype(F32)
    steps = jnp.arange(GROUPS, dtype=jnp.int32)
    block_of = ((group - steps) % GROUPS) * members
    inside = jnp.arange(block_len, dtype=jnp.int32)

    def main_positions(who):
        return ((block_of + who) * block_len)[:, None] + inside[None, :]

    count_main = lax.dynamic_index_in_dim(counts, group, 0, keepdims=False)
    count_rest = counts[GROUPS]
    rest_positions = here * block_len + inside
    row_valid = jnp.concatenate([
        (main_positions(member) < count_main).reshape(-1), rest_positions < count_rest])
    row_mask = row_valid.astype(F32)
    key_positions = jnp.concatenate(
        [main_positions(member ^ step).reshape(-1) for step in range(members)])

    def key_extras(valid):
        bias = jnp.where(valid, 0.0, NEG)[:, None]
        lane = jnp.arange(128)[None, :]
        return jnp.where(lane < 3, 1.0, jnp.where(lane == 3, bias, 0.0)).astype(BF)

    ext_main = key_extras(key_positions < count_main)
    ext_rest = key_extras(jnp.arange(seq_len) < count_rest)

    rest_rows = patches[GROUPS]
    rest_f32 = rest_rows.astype(F32)
    first_rest = (rest_f32 * norm_scale(rest_f32) * gain_one).astype(BF)
    moved = to_groups(patches)
    main_rows = jnp.concatenate(moved, axis=0).astype(F32)
    first_main = (main_rows * norm_scale(main_rows) * gain_one).astype(BF)
    first_all = jnp.concatenate(to_members(first_main), axis=0)
    first_rest_sent, _ = lax.optimization_barrier((first_rest, first_main))
    first_rest_all = lax.all_gather(first_rest_sent, "seq", axis=0, tiled=True)

    place = jnp.reshape(slot_of(member), (1,)).astype(jnp.int32)
    zero_place = jnp.zeros((1,), jnp.int32)
    if pad_cols:
        main_weights = [columns_of(w, slot_of(member)) for w in (w_query, w_key, w_value)]
        main_place = zero_place
    else:
        main_weights = [w_query, w_key, w_value]
        main_place = place
    q_rows = min(128, block_len)
    query_main, key_main, value_main, logs_main, attn_main = attend(
        main_place, first_all, first_all, *main_weights, ext_main, pairs, q_rows)
    query_rest, key_rest, value_rest, logs_rest, attn_rest = attend(
        zero_place, first_rest, first_rest_all, w_query, w_key, w_value, ext_rest,
        HEADS // 2, q_rows, (attn_main,), REST_PER)
    grad_moved = to_groups(cotangent, (attn_main,))
    grad_low = pack_rows(grad_moved + [cotangent[GROUPS]], (attn_rest,))

    slots = jnp.stack([slot_of(member ^ step) for step in range(members)]).astype(jnp.int32)
    swapped = []
    for step in range(members):
        part = attn_main[step * main_own:(step + 1) * main_own, :mine_cols]
        swapped.append(part if step == 0 else lax.ppermute(part, "seq", member_perm(step)))
    attn_in = join_heads(slots, swapped, attn_rest)
    resid = jnp.concatenate([main_rows, rest_f32], axis=0)
    branch_one = dot(attn_in, w_out)
    middle = resid + branch_one
    second_in = (middle * norm_scale(middle) * gain_two).astype(BF)
    ff_ins = (second_in, grad_low, w_gate, w_up, w_down)
    sums_two, sums_gs, ff_sent = ff_half(there, *ff_ins, None)
    branch_two, grad_second, ff_kept = ff_half(here_place, *ff_ins, (sums_two, sums_gs))
    ff_now = add_low(ff_kept, core_move(ff_sent))
    img_fours = [list(range(i, i + 4)) for i in range(0, n_img, 4)]
    same_member = [[g * members + r for g in range(GROUPS)] for r in range(members)]
    ff_quarter = lax.psum_scatter(ff_now, "img", scatter_dimension=0, axis_index_groups=img_fours)
    branch_two = hold(branch_two, (ff_now,))
    result = middle + branch_two
    squares = jnp.stack([masked_squares(v, row_mask) for v in (resid, branch_one, branch_two, result)])
    valid_count = jnp.sum(row_mask)
    result_low = result.astype(BF)
    grad_out = grad_low.astype(F32)
    grad_second = hold(grad_second, (ff_now,))
    grad_mid_norm, grad_gain_two = norm_back(middle, gain_two, grad_second)
    grad_mid = grad_out + grad_mid_norm
    grad_mid_low = grad_mid.astype(BF)

    main_grads = []
    for step in range(members):
        rows_of = lax.dynamic_slice_in_dim(w_out, slot_of(member ^ step) * mine_cols, mine_cols, 0)
        part = dot_nt(grad_mid_low[:main_own], rows_of).astype(BF)
        if pad_cols:
            part = jnp.pad(part, ((0, 0), (0, pad_cols)))
        main_grads.append(part if step == 0 else lax.ppermute(part, "seq", member_perm(step)))
    grad_attn_main = pack_rows(main_grads)
    grad_attn_rest = dot_nt(grad_mid_low[main_own:], w_out).astype(BF)

    dq_rest, dk_rest, dv_rest, first_own_rest, first_part_rest = attend_back(
        zero_place, query_rest, key_rest, value_rest, ext_rest, logs_rest, attn_rest, grad_attn_rest,
        (w_query, w_key, w_value), q_rows, 0, (), REST_PER)
    layer_got = hold_all(sent_home(result_low), (dq_rest,))
    layer_out = placed(result_low, layer_got)
    by_owner = hold(first_part_rest, (layer_out,)).reshape(GROUPS, members, block_len, width)
    by_group = lax.dynamic_index_in_dim(by_owner, member, 1, keepdims=False).astype(F32)
    for step in range(1, members):
        part = lax.dynamic_index_in_dim(by_owner, member ^ step, 1, keepdims=False)
        by_group = by_group + lax.ppermute(part, "seq", member_perm(step)).astype(F32)
    by_group = by_group.astype(BF)
    rest_parts = [lax.dynamic_index_in_dim(by_group, group ^ step, 0, keepdims=False) for step in range(GROUPS)]

    half_width = width // 2
    rest_ins = [(first_rest, False), (dq_rest, True), (first_rest_all, False), (dk_rest, True),
                (dv_rest, True), (attn_in, False), (grad_mid_low, True)]
    qkv_sent = grad_part(there, rest_ins, [
        (0, 0, [(0, 1)]), (0, half_width, [(5, 6)]), (1, 0, [(2, 3)]), (1, half_width, [(2, 4)])],
        (dq_rest,))
    rest_got = [z_move(rest_parts[step], step) for step in range(1, GROUPS)]
    rest_got = hold_all(rest_got, (qkv_sent, grad_attn_main))
    ff_quarter = hold(ff_quarter, rest_got)
    ff_shard = lax.psum_scatter(ff_quarter, "seq", scatter_dimension=0, axis_index_groups=same_member)
    for move in more_moves:
        ff_shard = add_low(ff_shard, move(ff_shard))
    dq_main, dk_main, dv_main, first_own_main, first_far_main = attend_back(
        main_place, query_main, key_main, value_main, ext_main, logs_main, attn_main, grad_attn_main,
        main_weights, min(256, block_len * 2), main_own, (ff_quarter,), pairs)

    def in_half(part):
        part = part[:, :mine_cols]
        if mine_cols == width // 2:
            return part
        empty = jnp.zeros((part.shape[0], width // 2), part.dtype)
        return lax.dynamic_update_slice_in_dim(empty, part, (member // 2) * mine_cols, 1)

    main_ins = [(first_all, False), (in_half(dq_main), False), (in_half(dk_main), False),
                (in_half(dv_main), False)]
    qkv_kept = grad_part(here_place, rest_ins + main_ins, [
        (0, 0, [(0, 1), (7, 8)]), (0, half_width, [(5, 6)]),
        (1, 0, [(2, 3), (7, 9)]), (1, half_width, [(2, 4), (7, 10)])])
    ff_shard = hold(ff_shard, (qkv_kept,))
    ff_groups = lax.all_gather(ff_shard, "seq", axis=0, axis_index_groups=same_member)
    kx, sx, ky, sy = split_cores(here_place, qkv_kept, core_move(qkv_sent))

    small = jnp.concatenate([grad_gain_two, squares, valid_count[None]])
    small = jnp.pad(small, (0, -small.size % 1024)).reshape(-1, 128)
    for move in [core_move] + more_moves:
        small = small + move(small)

    got, sx, sy = hold_all([img_moves[0](small), img_moves[0](sx), img_moves[1](sy)])
    small = small + got
    kx, sx, ky, sy = add_pairs(kx, sx, ky, sy)

    ff_groups = hold(ff_groups, (kx,))
    ff_own = lax.all_gather(ff_groups, "img", axis=0, axis_index_groups=img_fours)
    far = [first_far_main[(step - 1) * main_own:step * main_own] for step in range(1, members)]
    got, sx, sy, *far = hold_all(
        [img_moves[1](small), img_moves[1](sx), img_moves[0](sy)]
        + [lax.ppermute(part, "seq", member_perm(step + 1)) for step, part in enumerate(far)])
    small = small + got
    shards = add_fours(kx, sx, ky, sy)
    grad_first_main = first_own_main + sum(part.astype(F32) for part in far)
    grad_first_rest = first_own_rest + rest_parts[0].astype(F32) + sum(part.astype(F32) for part in rest_got)
    grad_first = jnp.concatenate([grad_first_main, grad_first_rest], axis=0)
    grad_input_rows = (grad_mid + norm_back(resid, gain_one, grad_first)[0]).astype(BF)

    got, *pieces = hold_all([z_moves[0](small)] + [z_move(shards[step], step) for step in range(1, GROUPS)])
    small = small + got
    qkv_total = sum_shards([shards[0]] + pieces, (grad_input_rows,))
    for move in more_moves:
        qkv_total = add_low(qkv_total, move(qkv_total))

    got, *pieces = hold_all([z_moves[1](small)] + [z_move(qkv_total, step) for step in range(1, GROUPS)])
    small = (small + got).reshape(-1)
    x, y = stack_orders([qkv_total] + pieces)
    rx, ry, *got = hold_all([img_moves[1](x), img_moves[0](y)] + sent_home(grad_input_rows))
    near = stack_pairs(x, rx, y, ry)
    grad_input = placed(grad_input_rows, got)
    ff_own = hold(ff_own, (rx, ry))
    sum_gate, sum_up, sum_down = assemble_ff(here_place, ff_own, core_move(ff_own), w_gate.shape[1])
    rx, ry, cx, cy = hold_all(
        [img_moves[0](near[0]), img_moves[1](near[1]), core_move(near[0]), core_move(near[1])],
        (grad_input, sum_gate))
    pieces = [near[0], rx, cx, core_move(rx), near[1], ry, cy, core_move(ry)]
    sum_query, sum_out, sum_key, sum_value, sum_gain_one = assemble(
        here_place, pieces, (w_query, w_key, w_value), gain_one[:, None])
    sum_gain_one = sum_gain_one.reshape(width)
    sum_gain_two, sum_squares, sum_count = small[:width], small[width:width + 4], small[width + 4]
    rms_stats = jnp.sqrt(sum_squares / (sum_count * width))
    return (layer_out, grad_input, sum_gain_one, sum_query, sum_key, sum_value, sum_out,
            sum_gain_two, sum_gate, sum_up, sum_down, rms_stats)


def solution(mesh):
    rows = P("img", "seq", None)
    return jax.shard_map(
        functools.partial(body, mesh.shape["img"], mesh.shape["seq"]),
        mesh=mesh,
        in_specs=(rows, P("img"), P(), P(), P(), P(), P(), P(), P(), P(), P(), rows),
        out_specs=(rows, rows, P(), P(), P(), P(), P(), P(), P(), P(), P(), P()),
        check_vma=False,
    )
```

```python
import functools
import math

import jax
import jax.numpy as jnp
from jax import lax
from jax.experimental import pallas as pl
from jax.experimental.pallas import tpu as pltpu
from jax.sharding import PartitionSpec as P

HEADS = 12
GROUPS = 4
REST_PER = 3
SHARDS = 16
EPS = 1e-06
NEG = -1000000000.0
LOG2E = 1.4426950408889634
LN2 = 0.6931471805599453
GELU_C = 0.7978845608028654
GELU_A = 0.044715
BF = jnp.bfloat16
F32 = jnp.float32
VMEM_LIMIT = 56 * 1024 * 1024
ANY = pl.BlockSpec(memory_space=pl.ANY)


def dot(left, right):
    return jnp.dot(left, right, preferred_element_type=F32)


def dot_nt(left, right):
    return lax.dot_general(left, right, (((1,), (1,)), ((), ())), preferred_element_type=F32)


def dot_tn(left, right):
    return lax.dot_general(left, right, (((0,), (0,)), ((), ())), preferred_element_type=F32)


def split_three(column):
    hi = column.astype(BF).astype(F32)
    rest = column - hi
    mid = rest.astype(BF).astype(F32)
    return hi, mid, rest - mid


def extras(rows, columns):
    lane = lax.broadcasted_iota(jnp.int32, (rows, 128), 1)
    out = jnp.zeros((rows, 128), F32)
    for index, column in enumerate(columns):
        if column is not None:
            out = jnp.where(lane == index, column, out)
    return out.astype(BF)


def head_lanes(values, half):
    lane = lax.broadcasted_iota(jnp.int32, values.shape, 1)
    return jnp.where((lane < 64) if half == 0 else (lane >= 64), values, jnp.zeros_like(values))


def stack_heads(values):
    return jnp.concatenate([head_lanes(values, 0), head_lanes(values, 1)], axis=0)


def attend_kernel(q_rows, per, place_ref, fiq_ref, fik_ref, wq_ref, wk_ref, wv_ref, ext_ref, *refs):
    q_ref, k_ref, v_ref, log_ref, out_ref = refs[-5:]
    scale = LOG2E / math.sqrt(64.0)
    both = dot(fik_ref[...], jnp.concatenate([wk_ref[...], wv_ref[...]], axis=1)).astype(BF)
    every_query = (dot(fiq_ref[...], wq_ref[...]) * scale).astype(BF)
    ext = ext_ref[...]
    one = extras(2 * q_rows, (None, None, None, 1.0))
    for pair in range(per):
        lanes = slice(128 * pair, 128 * (pair + 1))
        key_pair, value_pair = both[:, lanes], both[:, 128 * (per + pair):128 * (per + pair + 1)]
        query = every_query[:, lanes]
        k_ref[pair] = key_pair
        v_ref[pair] = value_pair
        q_ref[pair] = query
        keys = jnp.concatenate([key_pair, ext], axis=1)
        values = jnp.concatenate([value_pair, ext], axis=1)
        for start in range(0, fiq_ref.shape[0], q_rows):
            rows = slice(start, start + q_rows)
            scores = dot_nt(jnp.concatenate([stack_heads(query[rows]), one], axis=1), keys)
            top = jnp.max(scores, axis=1, keepdims=True)
            weights = jnp.exp2(scores - top).astype(BF)
            mixed = dot(weights, values)
            norm = mixed[:, 128:129]
            logs = extras(2 * q_rows, split_three(-(top + jnp.log2(norm))) + (1.0,))
            log_ref[2 * pair, rows, :] = logs[:q_rows]
            log_ref[2 * pair + 1, rows, :] = logs[q_rows:]
            scaled = mixed[:, :128] / norm
            lane = lax.broadcasted_iota(jnp.int32, (q_rows, 128), 1)
            out_ref[rows, lanes] = jnp.where(lane < 64, scaled[:q_rows], scaled[q_rows:]).astype(BF)


def attend(place, fi_q, fi_k, w_query, w_key, w_value, ext, pairs, q_rows, after=(), per=1):
    q_total, width = fi_q.shape
    k_total = fi_k.shape[0]
    column = lambda i, p: (0, p[0] * (pairs // per) + i)
    whole = lambda i, p: (0, 0)
    stacked = lambda i, p: (i, 0, 0)
    return pl.pallas_call(
        functools.partial(attend_kernel, q_rows, per),
        grid_spec=pltpu.PrefetchScalarGridSpec(
            num_scalar_prefetch=1,
            grid=(pairs // per,),
            in_specs=[
                pl.BlockSpec((q_total, width), whole),
                pl.BlockSpec((k_total, width), whole),
                pl.BlockSpec((width, 128 * per), column),
                pl.BlockSpec((width, 128 * per), column),
                pl.BlockSpec((width, 128 * per), column),
                pl.BlockSpec((k_total, 128), whole),
            ] + [ANY] * len(after),
            out_specs=[
                pl.BlockSpec((per, q_total, 128), stacked),
                pl.BlockSpec((per, k_total, 128), stacked),
                pl.BlockSpec((per, k_total, 128), stacked),
                pl.BlockSpec((2 * per, q_total, 128), stacked),
                pl.BlockSpec((q_total, 128 * per), lambda i, p: (0, i)),
            ],
        ),
        out_shape=[
            jax.ShapeDtypeStruct((pairs, q_total, 128), BF),
            jax.ShapeDtypeStruct((pairs, k_total, 128), BF),
            jax.ShapeDtypeStruct((pairs, k_total, 128), BF),
            jax.ShapeDtypeStruct((2 * pairs, q_total, 128), BF),
            jax.ShapeDtypeStruct((q_total, pairs * 128), BF),
        ],
        compiler_params=pltpu.CompilerParams(vmem_limit_bytes=VMEM_LIMIT),
        cost_estimate=pl.CostEstimate(
            flops=4 * 128 * pairs * (4 * q_total * k_total + width * (q_total + 2 * k_total)),
            bytes_accessed=2 * (q_total + k_total) * width * 4,
            transcendentals=2 * pairs * q_total * k_total,
        ),
    )(place, fi_q, fi_k, w_query, w_key, w_value, ext, *after)


def attend_back_kernel(q_rows, own_rows, per, place_ref, q_ref, k_ref, v_ref, ext_ref, log_ref, out_ref,
                       grad_ref, wq_ref, wk_ref, wv_ref, *refs):
    dq_ref, dk_ref, dv_ref, own_ref, far_ref, sum_q, sum_k = refs[-7:]
    del place_ref
    step = pl.program_id(0)

    @pl.when(step == 0)
    def _():
        if not own_rows:
            sum_q[...] = jnp.zeros_like(sum_q)
        sum_k[...] = jnp.zeros_like(sum_k)

    ext = ext_ref[...]
    for pair in range(per):
        lanes = slice(128 * pair, 128 * (pair + 1))
        key_pair = k_ref[pair]
        keys = jnp.concatenate([key_pair, ext], axis=1)
        values = jnp.concatenate([v_ref[pair], ext], axis=1)
        keys_trans = jnp.transpose(key_pair.astype(F32)).astype(BF)
        dk_sum = jnp.zeros(key_pair.shape, F32)
        dv_sum = jnp.zeros(key_pair.shape, F32)
        for start in range(0, q_ref.shape[1], q_rows):
            rows = slice(start, start + q_rows)
            grad = grad_ref[rows, lanes]
            product = grad.astype(F32) * out_ref[rows, lanes].astype(F32)
            delta = jnp.sum(stack_heads(product), axis=1, keepdims=True)
            grad_h = stack_heads(grad)
            query_h = stack_heads(q_ref[pair, rows, :])
            logs = jnp.concatenate([log_ref[2 * pair, rows, :], log_ref[2 * pair + 1, rows, :]], axis=0)
            probs = jnp.exp2(dot_nt(keys, jnp.concatenate([query_h, logs], axis=1)))
            centred = dot_nt(
                values, jnp.concatenate([grad_h, extras(2 * q_rows, split_three(-delta))], axis=1))
            grad_scores = (probs * centred).astype(BF)
            dv_sum = dv_sum + dot(probs.astype(BF), grad_h)
            dk_sum = dk_sum + dot(grad_scores, query_h)
            first = dot(keys_trans[:64], grad_scores[:, :q_rows])
            second = dot(keys_trans[64:], grad_scores[:, q_rows:])
            dq_ref[rows, lanes] = (
                jnp.transpose(jnp.concatenate([first, second], axis=0)) * 0.125).astype(BF)
        dk_ref[:, lanes] = (dk_sum * LN2).astype(BF)
        dv_ref[:, lanes] = dv_sum.astype(BF)
    dk, dv = dk_ref[...], dv_ref[...]
    if own_rows:
        sum_k[...] += dot_nt(
            jnp.concatenate([dq_ref[...], dk, dv], axis=1),
            jnp.concatenate([wq_ref[...], wk_ref[...], wv_ref[...]], axis=1))
    else:
        sum_q[...] += dot_nt(dq_ref[...], wq_ref[...])
        sum_k[...] += dot_nt(
            jnp.concatenate([dk, dv], axis=1), jnp.concatenate([wk_ref[...], wv_ref[...]], axis=1))

    @pl.when(step == pl.num_programs(0) - 1)
    def _():
        if own_rows:
            own_ref[...] = sum_k[:own_rows]
            far_ref[...] = sum_k[own_rows:].astype(BF)
        else:
            own_ref[...] = sum_q[...]
            far_ref[...] = sum_k[...].astype(BF)


def attend_back(place, query, key, value, ext, logs, out, grad, weights, q_rows, own_rows, after=(), per=1):
    pairs, q_total, _ = query.shape
    k_total = key.shape[1]
    width = weights[0].shape[0]
    stacked = lambda i, p: (i, 0, 0)
    flat = lambda i, p: (0, i)
    whole = lambda i, p: (0, 0)
    column = pl.BlockSpec((width, 128 * per), lambda i, p: (0, p[0] * (pairs // per) + i))
    shapes = [(own_rows, width), (k_total - own_rows, width)] if own_rows else [(q_total, width), (k_total, width)]
    return pl.pallas_call(
        functools.partial(attend_back_kernel, q_rows, own_rows, per),
        grid_spec=pltpu.PrefetchScalarGridSpec(
            num_scalar_prefetch=1,
            grid=(pairs // per,),
            in_specs=[
                pl.BlockSpec((per, q_total, 128), stacked),
                pl.BlockSpec((per, k_total, 128), stacked),
                pl.BlockSpec((per, k_total, 128), stacked),
                pl.BlockSpec((k_total, 128), whole),
                pl.BlockSpec((2 * per, q_total, 128), stacked),
                pl.BlockSpec((q_total, 128 * per), flat),
                pl.BlockSpec((q_total, 128 * per), flat),
                column, column, column,
            ] + [ANY] * len(after),
            out_specs=[
                pl.BlockSpec((q_total, 128 * per), flat),
                pl.BlockSpec((k_total, 128 * per), flat),
                pl.BlockSpec((k_total, 128 * per), flat),
                pl.BlockSpec(shapes[0], whole),
                pl.BlockSpec(shapes[1], whole),
            ],
            scratch_shapes=[
                pltpu.VMEM((8 if own_rows else q_total, width), F32), pltpu.VMEM((k_total, width), F32)],
        ),
        out_shape=[
            jax.ShapeDtypeStruct((q_total, pairs * 128), BF),
            jax.ShapeDtypeStruct((k_total, pairs * 128), BF),
            jax.ShapeDtypeStruct((k_total, pairs * 128), BF),
            jax.ShapeDtypeStruct(shapes[0], F32),
            jax.ShapeDtypeStruct(shapes[1], BF),
        ],
        compiler_params=pltpu.CompilerParams(vmem_limit_bytes=VMEM_LIMIT),
        cost_estimate=pl.CostEstimate(
            flops=2 * 256 * pairs * 5 * q_total * k_total,
            bytes_accessed=2 * 128 * pairs * (4 * q_total + 4 * k_total),
            transcendentals=2 * pairs * q_total * k_total,
        ),
    )(place, query, key, value, ext, logs, out, grad, *weights, *after)


FF_TILE = 256
FF_STEP = 512


def ff_kernel(pieces, place_ref, second_ref, wg_ref, wu_ref, wd_ref, *refs):
    two_ref, gs_ref, part_ref, second_t_ref = refs[-4:]
    first = pieces > 1
    grad_ref = refs[-5] if first else refs[0]
    step = pl.program_id(0)

    @pl.when(step == 0)
    def _():
        second_t_ref[...] = jnp.transpose(second_ref[...])
        if first:
            at = 0
            for ref in refs[:pieces]:
                grad_ref[at:at + ref.shape[0], :] = ref[...]
                at += ref.shape[0]
            two_ref[...] = jnp.zeros_like(two_ref)
            gs_ref[...] = jnp.zeros_like(gs_ref)
        else:
            two_ref[...] = refs[1][...]
            gs_ref[...] = refs[2][...]

    second, grad = second_ref[...], grad_ref[...]
    gate = dot(second, wg_ref[...])
    up = dot(second, wu_ref[...])
    grad_inner = dot_nt(grad, wd_ref[...])
    square = gate * gate
    half_plus = 0.5 + 0.5 * jnp.tanh(gate * (GELU_C + (GELU_C * GELU_A) * square))
    gelu = gate * half_plus
    slope = half_plus + gelu * (1.0 - half_plus) * (2.0 * GELU_C + (6.0 * GELU_C * GELU_A) * square)
    inner = (gelu * up).astype(BF)
    grad_gate = (grad_inner * up * slope).astype(BF)
    grad_up = (grad_inner * gelu).astype(BF)
    two_ref[...] += dot(inner, wd_ref[...])
    gs_ref[...] += dot_nt(grad_gate, wg_ref[...]) + dot_nt(grad_up, wu_ref[...])
    width = second.shape[1]
    shard, shard_down = width // SHARDS, 2 * FF_TILE // SHARDS
    part_gate = dot(second_t_ref[...], grad_gate).astype(BF)
    part_up = dot(second_t_ref[...], grad_up).astype(BF)
    part_down = dot_tn(inner, grad).astype(BF)
    shape = (4, 4, shard, FF_TILE)
    for odd in range(FF_STEP // FF_TILE):
        here = slice(FF_TILE * odd, FF_TILE * (odd + 1))
        part_ref[:, :, shard * odd:shard * (odd + 1), :] = part_gate[:, here].reshape(shape)
        part_ref[:, :, shard * (2 + odd):shard * (3 + odd), :] = part_up[:, here].reshape(shape)
        for tile in range(width // FF_TILE):
            at = 4 * shard + shard_down * tile
            part_ref[2 * odd:2 * odd + 2, :, at:at + shard_down, :] = (
                part_down[here, FF_TILE * tile:FF_TILE * (tile + 1)].reshape(2, 4, shard_down, FF_TILE))


def ff_half(place, second, grads, w_gate, w_up, w_down, sums, after=()):
    rows, width = second.shape
    tiles = w_gate.shape[1] // FF_STEP // 2
    tile_at = lambda j, p: j * 2 + p[0]
    whole = lambda j, p: (0, 0)
    sum_spec = pl.BlockSpec((rows, width), whole)
    columns = pl.BlockSpec((width, FF_STEP), lambda j, p: (0, tile_at(j, p)))
    shard_rows = 4 * (width // SHARDS) + (2 * FF_TILE // SHARDS) * (width // FF_TILE)
    return pl.pallas_call(
        functools.partial(ff_kernel, len(grads)),
        grid_spec=pltpu.PrefetchScalarGridSpec(
            num_scalar_prefetch=1,
            grid=(tiles,),
            in_specs=[
                pl.BlockSpec((rows, width), whole),
                columns, columns, pl.BlockSpec((FF_STEP, width), lambda j, p: (tile_at(j, p), 0)),
            ] + [pl.BlockSpec(g.shape, whole) for g in grads] + [sum_spec] * (0 if sums is None else 2) + [ANY] * len(after),
            out_specs=[sum_spec] * (sums is None) + [sum_spec, sum_spec,
                       pl.BlockSpec((4, 4, shard_rows, FF_TILE), lambda j, p: (0, 0, j, 0))],
            scratch_shapes=[pltpu.VMEM((width, rows), BF)],
        ),
        out_shape=[jax.ShapeDtypeStruct((rows, width), BF)] * (sums is None)
        + [jax.ShapeDtypeStruct((rows, width), F32)] * 2
        + [jax.ShapeDtypeStruct((4, 4, 2 * shard_rows, FF_TILE), BF)],
        compiler_params=pltpu.CompilerParams(vmem_limit_bytes=VMEM_LIMIT),
        cost_estimate=pl.CostEstimate(
            flops=18 * rows * width * tiles * FF_STEP,
            bytes_accessed=12 * width * tiles * FF_STEP + 16 * rows * width,
            transcendentals=rows * tiles * FF_STEP),
    )(place, second, w_gate, w_up, w_down, *grads, *(sums or ()), *after)


def split_kernel(place_ref, *refs):
    ins, outs = refs[:8], refs[-4:]
    for index, out in enumerate(outs):
        for step in range(4):
            at = jnp.bitwise_xor(place_ref[3], step)
            out[0, step] = (ins[index][0, 0, at].astype(F32) + ins[4 + index][0, 0, at].astype(F32)).astype(BF)


def split_cores(place, kept, got, after=()):
    tail = kept.shape[3:]

    def spec(order, away):
        def at(b, p):
            first, second = p[1 + order] ^ away, p[2 - order] ^ b
            return (order, first + 2 * second if order == 0 else second + 2 * first, 0, 0, 0)
        return pl.BlockSpec((1, 1, 4) + tail, at)

    specs = [spec(order, away) for order in range(2) for away in range(2)]
    out = pl.BlockSpec((1, 4) + tail, lambda b, p: (b, 0, 0, 0))
    return pl.pallas_call(
        split_kernel,
        grid_spec=pltpu.PrefetchScalarGridSpec(
            num_scalar_prefetch=1, grid=(2,), in_specs=specs * 2 + [ANY] * len(after), out_specs=[out] * 4),
        out_shape=[jax.ShapeDtypeStruct((2, 4) + tail, BF)] * 4,
        compiler_params=pltpu.CompilerParams(vmem_limit_bytes=VMEM_LIMIT),
        cost_estimate=pl.CostEstimate(flops=0, bytes_accessed=6 * kept.size, transcendentals=0),
    )(place, *([kept] * 4), *([got] * 4), *after)


def hold(array, after):
    return pl.pallas_call(
        lambda *refs: None,
        in_specs=[ANY] * (1 + len(after)),
        out_specs=ANY,
        out_shape=jax.ShapeDtypeStruct(array.shape, array.dtype),
        input_output_aliases={0: 0},
        cost_estimate=pl.CostEstimate(flops=0, bytes_accessed=0, transcendentals=0),
    )(array, *after)


def hold_all(arrays, after=()):
    return pl.pallas_call(
        lambda *refs: None,
        in_specs=[ANY] * (len(arrays) + len(after)),
        out_specs=[ANY] * len(arrays),
        out_shape=[jax.ShapeDtypeStruct(a.shape, a.dtype) for a in arrays],
        input_output_aliases={i: i for i in range(len(arrays))},
        cost_estimate=pl.CostEstimate(flops=0, bytes_accessed=0, transcendentals=0),
    )(*arrays, *after)


def pack_rows_kernel(count, *refs):
    at = 0
    for ref in refs[:count]:
        rows = ref.shape[0]
        refs[-1][at:at + rows, :] = ref[...]
        at += rows


def pack_rows(pieces, after=()):
    rows = sum(p.shape[0] for p in pieces)
    shape = (rows, pieces[0].shape[1])
    return pl.pallas_call(
        functools.partial(pack_rows_kernel, len(pieces)),
        in_specs=[pl.BlockSpec(p.shape, lambda: (0, 0)) for p in pieces] + [ANY] * len(after),
        out_specs=pl.BlockSpec(shape, lambda: (0, 0)),
        out_shape=jax.ShapeDtypeStruct(shape, pieces[0].dtype),
        cost_estimate=pl.CostEstimate(flops=0, bytes_accessed=0, transcendentals=0),
    )(*pieces, *after)


def join_heads_kernel(members, slots_ref, *refs):
    pieces, rest_ref, out_ref = refs[:members], refs[members], refs[members + 1]
    rows, cols = pieces[0].shape
    for index in range(members):
        for slot in range(members):
            @pl.when(slots_ref[index] == slot)
            def _():
                out_ref[0:rows, slot * cols:(slot + 1) * cols] = pieces[index][...]
    out_ref[rows:, :] = rest_ref[...]


def join_heads(slots, pieces, rest):
    rows, cols = pieces[0].shape
    members = len(pieces)
    shape = (rows + rest.shape[0], members * cols)
    block = lambda a: pl.BlockSpec(a.shape, lambda j, p: (0, 0))
    return pl.pallas_call(
        functools.partial(join_heads_kernel, members),
        grid_spec=pltpu.PrefetchScalarGridSpec(
            num_scalar_prefetch=1, grid=(1,), in_specs=[block(p) for p in pieces] + [block(rest)],
            out_specs=pl.BlockSpec(shape, lambda j, p: (0, 0))),
        out_shape=jax.ShapeDtypeStruct(shape, rest.dtype),
        cost_estimate=pl.CostEstimate(flops=0, bytes_accessed=0, transcendentals=0),
    )(slots, *pieces, rest)


def place_rows_kernel(place_ref, *refs):
    pieces, out_ref = refs[:-1], refs[-1]
    for step in range(GROUPS):
        out_ref[(place_ref[3] + step) % GROUPS] = pieces[step][...]
    for index in range(GROUPS, len(pieces)):
        out_ref[index] = pieces[index][...]


def place_rows(place, pieces):
    block = pl.BlockSpec(pieces[0].shape, lambda j, p: (0, 0))
    shape = (len(pieces),) + pieces[0].shape
    return pl.pallas_call(
        place_rows_kernel,
        grid_spec=pltpu.PrefetchScalarGridSpec(
            num_scalar_prefetch=1, grid=(1,), in_specs=[block] * len(pieces),
            out_specs=pl.BlockSpec(shape, lambda j, p: (0, 0, 0))),
        out_shape=jax.ShapeDtypeStruct(shape, pieces[0].dtype),
        cost_estimate=pl.CostEstimate(flops=0, bytes_accessed=0, transcendentals=0),
    )(place, *pieces)


def add_kernel(x_ref, rx_ref, y_ref, ry_ref, *refs):
    outs = refs[-4:]
    for index in range(2):
        outs[index][...] = add_low(x_ref[index], rx_ref[index])
        outs[2 + index][...] = add_low(y_ref[index], ry_ref[index])


def add_pairs(x, rx, y, ry, after=()):
    tail = x.shape[2:]
    return pl.pallas_call(
        add_kernel,
        grid=(4,),
        in_specs=[pl.BlockSpec((2, 1) + tail, lambda j: (0, j, 0, 0))] * 4 + [ANY] * len(after),
        out_specs=[pl.BlockSpec((1,) + tail, lambda j: (j, 0, 0))] * 4,
        out_shape=[jax.ShapeDtypeStruct((4,) + tail, BF)] * 4,
        compiler_params=pltpu.CompilerParams(vmem_limit_bytes=VMEM_LIMIT),
        cost_estimate=pl.CostEstimate(flops=0, bytes_accessed=12 * x.size, transcendentals=0),
    )(x, rx, y, ry, *after)


def add_four_kernel(x_ref, rx_ref, y_ref, ry_ref, *refs):
    outs = refs[-4:]
    for index in range(4):
        outs[index][0] = add_low(x_ref[index], rx_ref[index])
        outs[index][1] = add_low(y_ref[index], ry_ref[index])


def add_fours(x, rx, y, ry, after=()):
    tail = x.shape[1:]
    whole = pl.BlockSpec(x.shape, lambda j: (0, 0, 0))
    return pl.pallas_call(
        add_four_kernel,
        grid=(1,),
        in_specs=[whole] * 4 + [ANY] * len(after),
        out_specs=[pl.BlockSpec((2,) + tail, lambda j: (0, 0, 0))] * 4,
        out_shape=[jax.ShapeDtypeStruct((2,) + tail, BF)] * 4,
        compiler_params=pltpu.CompilerParams(vmem_limit_bytes=VMEM_LIMIT),
        cost_estimate=pl.CostEstimate(flops=0, bytes_accessed=12 * x.size, transcendentals=0),
    )(x, rx, y, ry, *after)


def sum_kernel(*refs):
    total = refs[0][...].astype(F32)
    for ref in refs[1:GROUPS]:
        total = total + ref[...].astype(F32)
    refs[-1][...] = total.astype(BF)


def sum_shards(shards, after=()):
    whole = pl.BlockSpec(shards[0].shape, lambda: (0, 0, 0))
    return pl.pallas_call(
        sum_kernel,
        in_specs=[whole] * GROUPS + [ANY] * len(after),
        out_specs=whole,
        out_shape=jax.ShapeDtypeStruct(shards[0].shape, BF),
        cost_estimate=pl.CostEstimate(flops=0, bytes_accessed=0, transcendentals=0),
    )(*shards, *after)


def stack_orders_kernel(*refs):
    for order in range(2):
        for index in range(GROUPS):
            refs[order - 2][index] = refs[index][order]


def stack_orders(pieces, after=()):
    tail = pieces[0].shape[1:]
    return pl.pallas_call(
        stack_orders_kernel,
        in_specs=[pl.BlockSpec((2,) + tail, lambda: (0, 0, 0))] * GROUPS + [ANY] * len(after),
        out_specs=[pl.BlockSpec((GROUPS,) + tail, lambda: (0, 0, 0))] * 2,
        out_shape=[jax.ShapeDtypeStruct((GROUPS,) + tail, BF)] * 2,
        cost_estimate=pl.CostEstimate(flops=0, bytes_accessed=0, transcendentals=0),
    )(*pieces, *after)


def stack_pairs_kernel(x_ref, rx_ref, y_ref, ry_ref, *refs):
    refs[-2][0] = x_ref[...]
    refs[-2][1] = rx_ref[...]
    refs[-1][0] = y_ref[...]
    refs[-1][1] = ry_ref[...]


def stack_pairs(x, rx, y, ry, after=()):
    tail = x.shape[1:]
    block = pl.BlockSpec((1,) + tail, lambda j: (j, 0, 0))
    return pl.pallas_call(
        stack_pairs_kernel,
        grid=(GROUPS,),
        in_specs=[block] * 4 + [ANY] * len(after),
        out_specs=[pl.BlockSpec((2, 1) + tail, lambda j: (0, j, 0, 0))] * 2,
        out_shape=[jax.ShapeDtypeStruct((2,) + x.shape, BF)] * 2,
        cost_estimate=pl.CostEstimate(flops=0, bytes_accessed=0, transcendentals=0),
    )(x, rx, y, ry, *after)


def grad_kernel(columns, place_ref, *refs):
    ins, part_ref = refs[:-1], refs[-1]
    for order, at, terms in columns:
        total = None
        for left, right in terms:
            term = dot_tn(ins[left][...], ins[right][...])
            total = term if total is None else total + term
        rows, cols = total.shape
        part_ref[order, :, :, :, at:at + cols] = total.astype(BF).reshape(4, 4, rows // SHARDS, cols)


def grad_part(place, ins, columns, after=()):
    specs = []
    for array, halved in ins:
        depth, cols = array.shape
        if halved:
            specs.append(pl.BlockSpec((depth, cols // 2), lambda j, p: (0, p[0])))
        else:
            specs.append(pl.BlockSpec((depth, cols), lambda j, p: (0, 0)))
    rows = ins[0][0].shape[1]
    shape = (2, 4, 4, rows // SHARDS, rows)
    return pl.pallas_call(
        functools.partial(grad_kernel, columns),
        grid_spec=pltpu.PrefetchScalarGridSpec(
            num_scalar_prefetch=1,
            grid=(1,),
            in_specs=specs + [ANY] * len(after),
            out_specs=pl.BlockSpec(shape, lambda j, p: (0, 0, 0, 0, 0)),
        ),
        out_shape=jax.ShapeDtypeStruct(shape, BF),
        compiler_params=pltpu.CompilerParams(vmem_limit_bytes=VMEM_LIMIT),
        cost_estimate=pl.CostEstimate(
            flops=sum(2 * rows * (rows // 2) * ins[left][0].shape[0]
                      for _, _, terms in columns for left, _ in terms),
            bytes_accessed=sum(2 * a.size for a, _ in ins), transcendentals=0),
    )(place, *[a for a, _ in ins], *after)


def from_pieces(place_ref, refs, order, group):
    here_ref, away_ref, other_here_ref, other_away_ref = refs[4 * order:4 * order + 4]
    quarter = pl.program_id(0)
    bit = quarter % 2 if order == 0 else quarter // 2
    near = place_ref[1 + order] == bit
    at = jnp.bitwise_xor(place_ref[3], group)
    own = jnp.where(near, here_ref[0, at], away_ref[0, at]).astype(F32)
    other = jnp.where(near, other_here_ref[0, at], other_away_ref[0, at]).astype(F32)
    lower = place_ref[0] == 0
    return jnp.where(lower, own, other), jnp.where(lower, other, own)


def assemble_ff_kernel(place_ref, own_ref, other_ref, gate_ref, up_ref, down_ref):
    shard, down = gate_ref.shape[0] // 4, down_ref.shape[2] // 4
    shard_rows = own_ref.shape[2] // 2

    def write(halves):
        for group in range(4):
            rows = slice(shard * group, shard * (group + 1))
            for half, source in enumerate(halves):
                for order in range(2):
                    base = order * shard_rows
                    for tile in range(2):
                        at = ((order * 2 + half) * 2 + tile) * FF_TILE
                        gate_ref[rows, at:at + FF_TILE] = source[
                            0, group, base + shard * tile:base + shard * (tile + 1)].astype(F32)
                        up_ref[rows, at:at + FF_TILE] = source[
                            0, group, base + shard * (2 + tile):base + shard * (3 + tile)].astype(F32)
                    for tile in range(down_ref.shape[3] // FF_TILE):
                        at = base + 4 * shard + down * tile
                        down_ref[order * 2 + half, 0, down * group:down * (group + 1),
                                 FF_TILE * tile:FF_TILE * (tile + 1)] = source[
                                     0, group, at:at + down].astype(F32)

    pl.when(place_ref[0] == 0)(lambda: write((own_ref, other_ref)))
    pl.when(place_ref[0] != 0)(lambda: write((other_ref, own_ref)))


def assemble_ff(place, own, other, hidden):
    quarter = lambda rows: pl.BlockSpec((rows, hidden), lambda q, p: (q, 0))
    part = pl.BlockSpec((1,) + own.shape[1:], lambda q, p: (q, 0, 0, 0))
    rows = own.shape[2] // 2
    width = (rows * FF_TILE * SHARDS * 4) // (3 * hidden)
    gate, up, down = pl.pallas_call(
        assemble_ff_kernel,
        grid_spec=pltpu.PrefetchScalarGridSpec(
            num_scalar_prefetch=1, grid=(4,), in_specs=[part, part],
            out_specs=[quarter(width // 4), quarter(width // 4),
                       pl.BlockSpec((4, 1, hidden // 16, width), lambda q, p: (0, q, 0, 0))]),
        out_shape=[jax.ShapeDtypeStruct((width, hidden), F32)] * 2
        + [jax.ShapeDtypeStruct((4, 4, hidden // 16, width), F32)],
        compiler_params=pltpu.CompilerParams(vmem_limit_bytes=VMEM_LIMIT),
        cost_estimate=pl.CostEstimate(flops=0, bytes_accessed=12 * own.size, transcendentals=0),
    )(place, own, other)
    return gate, up, down.reshape(hidden, width)


def assemble_kernel(place_ref, *refs):
    wq_ref, wk_ref, wv_ref, gain_ref = refs[8:12]
    outs = refs[-5:-1]
    shard = outs[0].shape[0] // 4
    for order in range(2):
        for group in range(4):
            rows = slice(shard * group, shard * (group + 1))
            for half, value in enumerate(from_pieces(place_ref, refs, order, group)):
                width = value.shape[1] // 2
                for which in range(2):
                    outs[2 * order + which][rows, half * width:(half + 1) * width] = (
                        value[:, which * width:(which + 1) * width])
    products = (outs[0][...] * wq_ref[...].astype(F32) + outs[2][...] * wk_ref[...].astype(F32)
                + outs[3][...] * wv_ref[...].astype(F32))
    refs[-1][...] = jnp.sum(products, axis=1, keepdims=True) / gain_ref[...]


def assemble(place, pieces, weights, gain, after=()):
    tail = pieces[0].shape[1:]
    width = gain.shape[0]
    near = pl.BlockSpec((1,) + tail, lambda q, p: (p[2] ^ (q // 2), 0, 0, 0))
    far = pl.BlockSpec((1,) + tail, lambda q, p: (p[1] ^ (q % 2), 0, 0, 0))
    rows = pl.BlockSpec((width // 4, width), lambda q, p: (q, 0))
    column = pl.BlockSpec((width // 4, 1), lambda q, p: (q, 0))
    return pl.pallas_call(
        assemble_kernel,
        grid_spec=pltpu.PrefetchScalarGridSpec(
            num_scalar_prefetch=1, grid=(4,),
            in_specs=[near] * 4 + [far] * 4 + [rows] * 3 + [column] + [ANY] * len(after),
            out_specs=[rows] * 4 + [column]),
        out_shape=[jax.ShapeDtypeStruct((width, width), F32)] * 4 + [jax.ShapeDtypeStruct((width, 1), F32)],
        compiler_params=pltpu.CompilerParams(vmem_limit_bytes=VMEM_LIMIT),
        cost_estimate=pl.CostEstimate(
            flops=0, bytes_accessed=16 * 8 * pieces[0].size // 4, transcendentals=0),
    )(place, *pieces, *weights, gain, *after)


def add_low(left, right):
    return (left.astype(F32) + right.astype(F32)).astype(BF)


def norm_scale(values):
    return lax.rsqrt(jnp.mean(values * values, axis=-1, keepdims=True) + EPS)


def norm_back(values, gain, grad):
    scale = norm_scale(values)
    scaled = values * scale
    weighted = grad * gain
    inner = jnp.mean(weighted * scaled, axis=-1, keepdims=True)
    return scale * (weighted - scaled * inner), jnp.sum(grad * scaled, axis=0)


def masked_squares(values_in, row_mask):
    return jnp.sum(row_mask * jnp.sum(values_in * values_in, axis=-1))


def body(n_img, n_seq, patches, counts, norm_gain_one, w_query, w_key, w_value, w_out,
         norm_gain_two, w_gate, w_up, w_down, cotangent):
    charts, block_len, width = patches.shape
    members = n_seq // GROUPS
    head_count = HEADS // members
    pairs = -(-head_count // 2)
    pad_cols = pairs * 128 - head_count * 64
    mine_cols = head_count * 64
    main_own = GROUPS * block_len
    seq_len = n_seq * block_len
    here = lax.axis_index("seq")
    group, member = here // members, here % members
    img_here = lax.axis_index("img")

    def slot_of(who):
        return (who % 2) * (members // 2) + who // 2

    def bit_exchange(axis, bit):
        def move(array):
            if axis == "img":
                perm = [(i, i ^ (1 << bit)) for i in range(n_img)]
            elif axis == "group":
                perm = [(g * members + r, (g ^ (1 << bit)) * members + r)
                        for g in range(GROUPS) for r in range(members)]
            else:
                perm = [(g * members + r, g * members + (r ^ (1 << bit)))
                        for g in range(GROUPS) for r in range(members)]
            return lax.ppermute(array, "img" if axis == "img" else "seq", perm)
        return move

    img_moves = [bit_exchange("img", 0), bit_exchange("img", 1)]
    z_moves = [bit_exchange("group", 0), bit_exchange("group", 1)]

    def z_move(array, step):
        perm = [(g * members + r, (g ^ step) * members + r) for g in range(GROUPS) for r in range(members)]
        return lax.ppermute(array, "seq", perm)

    core_move = bit_exchange("member", 0)
    more_moves = [bit_exchange("img", b) for b in range(2, n_img.bit_length() - 1)]
    more_moves += [bit_exchange("member", b) for b in range(1, members.bit_length() - 1)]
    img_bits = [img_here % 2, (img_here // 2) % 2]
    half_here = member % 2

    def place_of(half):
        return jnp.stack([half] + img_bits + [group]).astype(jnp.int32)

    there, here_place = place_of(1 - half_here), place_of(half_here)

    def sum_img_first(kx, sx, ky, sy, after=()):
        return add_pairs(kx, img_moves[0](sx), ky, img_moves[1](sy), after)

    def sum_img_second(kx, sx, ky, sy, after=()):
        return add_fours(kx, img_moves[1](sx), ky, img_moves[0](sy), after)

    def sum_groups(shards, after=()):
        total = sum_shards(
            [shards[0]] + [z_move(shards[step], step) for step in range(1, GROUPS)], after)
        for move in more_moves:
            total = add_low(total, move(total))
        return total

    def quarters(total, after):
        return stack_orders([total] + [z_move(total, step) for step in range(1, GROUPS)], after)

    def halves(parts, after):
        return stack_pairs(parts[0], img_moves[1](parts[0]), parts[1], img_moves[0](parts[1]), after)

    def shift_perm(step):
        return [(g * members + r, ((g + step) % GROUPS) * members + r)
                for g in range(GROUPS) for r in range(members)]

    def member_perm(step):
        return [(g * members + r, g * members + (r ^ step))
                for g in range(GROUPS) for r in range(members)]

    def to_groups(array, after=()):
        pieces = []
        for step in range(GROUPS):
            part = lax.dynamic_index_in_dim(array, (group + step) % GROUPS, 0, keepdims=False)
            if step:
                part = lax.ppermute(hold(part, after) if after else part, "seq", shift_perm(step))
            pieces.append(part)
        return pieces

    def sent_home(rows):
        return [lax.ppermute(rows[step * block_len:(step + 1) * block_len], "seq", shift_perm(-step))
                for step in range(1, GROUPS)]

    def placed(rows, got):
        return place_rows(here_place, [rows[:block_len], *got, rows[main_own:]])

    def to_members(own):
        return [own] + [lax.ppermute(own, "seq", member_perm(step)) for step in range(1, members)]

    def columns_of(weight, who):
        part = lax.dynamic_slice_in_dim(weight, who * mine_cols, mine_cols, 1)
        return jnp.pad(part, ((0, 0), (0, pad_cols))) if pad_cols else part

    gain_one = norm_gain_one.astype(F32)
    gain_two = norm_gain_two.astype(F32)
    steps = jnp.arange(GROUPS, dtype=jnp.int32)
    block_of = ((group - steps) % GROUPS) * members
    inside = jnp.arange(block_len, dtype=jnp.int32)

    def main_positions(who):
        return ((block_of + who) * block_len)[:, None] + inside[None, :]

    count_main = lax.dynamic_index_in_dim(counts, group, 0, keepdims=False)
    count_rest = counts[GROUPS]
    rest_positions = here * block_len + inside
    row_valid = jnp.concatenate([
        (main_positions(member) < count_main).reshape(-1), rest_positions < count_rest])
    row_mask = row_valid.astype(F32)
    key_positions = jnp.concatenate(
        [main_positions(member ^ step).reshape(-1) for step in range(members)])

    def key_extras(valid):
        bias = jnp.where(valid, 0.0, NEG)[:, None]
        lane = jnp.arange(128)[None, :]
        return jnp.where(lane < 3, 1.0, jnp.where(lane == 3, bias, 0.0)).astype(BF)

    ext_main = key_extras(key_positions < count_main)
    ext_rest = key_extras(jnp.arange(seq_len) < count_rest)

    rest_rows = patches[GROUPS]
    rest_f32 = rest_rows.astype(F32)
    first_rest = (rest_f32 * norm_scale(rest_f32) * gain_one).astype(BF)
    moved = to_groups(patches)
    main_rows = jnp.concatenate(moved, axis=0).astype(F32)
    first_main = (main_rows * norm_scale(main_rows) * gain_one).astype(BF)
    first_all = jnp.concatenate(to_members(first_main), axis=0)
    first_rest_sent, _ = lax.optimization_barrier((first_rest, first_main))
    first_rest_all = lax.all_gather(first_rest_sent, "seq", axis=0, tiled=True)

    place = jnp.reshape(slot_of(member), (1,)).astype(jnp.int32)
    zero_place = jnp.zeros((1,), jnp.int32)
    if pad_cols:
        main_weights = [columns_of(w, slot_of(member)) for w in (w_query, w_key, w_value)]
        main_place = zero_place
    else:
        main_weights = [w_query, w_key, w_value]
        main_place = place
    q_rows = min(128, block_len)
    query_main, key_main, value_main, logs_main, attn_main = attend(
        main_place, first_all, first_all, *main_weights, ext_main, pairs, q_rows)
    query_rest, key_rest, value_rest, logs_rest, attn_rest = attend(
        zero_place, first_rest, first_rest_all, w_query, w_key, w_value, ext_rest,
        HEADS // 2, q_rows, (attn_main,), REST_PER)
    grad_moved = to_groups(cotangent, (attn_main,))

    slots = jnp.stack([slot_of(member ^ step) for step in range(members)]).astype(jnp.int32)
    swapped = []
    for step in range(members):
        part = attn_main[step * main_own:(step + 1) * main_own, :mine_cols]
        swapped.append(part if step == 0 else lax.ppermute(part, "seq", member_perm(step)))
    attn_in = join_heads(slots, swapped, attn_rest)
    resid = jnp.concatenate([main_rows, rest_f32], axis=0)
    branch_one = dot(attn_in, w_out)
    middle = resid + branch_one
    second_in = (middle * norm_scale(middle) * gain_two).astype(BF)
    ff_weights = (w_gate, w_up, w_down)
    grad_low, sums_two, sums_gs, ff_sent = ff_half(
        there, second_in, grad_moved + [cotangent[GROUPS]], *ff_weights, None)
    branch_two, grad_second, ff_kept = ff_half(here_place, second_in, [grad_low], *ff_weights, (sums_two, sums_gs))
    ff_now = add_low(ff_kept, core_move(ff_sent))
    img_fours = [list(range(i, i + 4)) for i in range(0, n_img, 4)]
    same_member = [[g * members + r for g in range(GROUPS)] for r in range(members)]
    ff_quarter = lax.psum_scatter(ff_now, "img", scatter_dimension=0, axis_index_groups=img_fours)
    branch_two = hold(branch_two, (ff_now,))
    result = middle + branch_two
    squares = jnp.stack([masked_squares(v, row_mask) for v in (resid, branch_one, branch_two, result)])
    valid_count = jnp.sum(row_mask)
    result_low = result.astype(BF)
    grad_out = grad_low.astype(F32)
    grad_second = hold(grad_second, (ff_now,))
    grad_mid_norm, grad_gain_two = norm_back(middle, gain_two, grad_second)
    grad_mid = grad_out + grad_mid_norm
    grad_mid_low = grad_mid.astype(BF)

    main_grads = []
    for step in range(members):
        rows_of = lax.dynamic_slice_in_dim(w_out, slot_of(member ^ step) * mine_cols, mine_cols, 0)
        part = dot_nt(grad_mid_low[:main_own], rows_of).astype(BF)
        if pad_cols:
            part = jnp.pad(part, ((0, 0), (0, pad_cols)))
        main_grads.append(part if step == 0 else lax.ppermute(part, "seq", member_perm(step)))
    grad_attn_main = pack_rows(main_grads)
    grad_attn_rest = dot_nt(grad_mid_low[main_own:], w_out).astype(BF)

    dq_rest, dk_rest, dv_rest, first_own_rest, first_part_rest = attend_back(
        zero_place, query_rest, key_rest, value_rest, ext_rest, logs_rest, attn_rest, grad_attn_rest,
        (w_query, w_key, w_value), q_rows, 0, (), REST_PER)
    layer_got = hold_all(sent_home(result_low), (dq_rest,))
    layer_out = placed(result_low, layer_got)
    by_owner = hold(first_part_rest, (layer_out,)).reshape(GROUPS, members, block_len, width)
    by_group = lax.dynamic_index_in_dim(by_owner, member, 1, keepdims=False).astype(F32)
    for step in range(1, members):
        part = lax.dynamic_index_in_dim(by_owner, member ^ step, 1, keepdims=False)
        by_group = by_group + lax.ppermute(part, "seq", member_perm(step)).astype(F32)
    by_group = by_group.astype(BF)
    rest_parts = [lax.dynamic_index_in_dim(by_group, group ^ step, 0, keepdims=False) for step in range(GROUPS)]

    half_width = width // 2
    rest_ins = [(first_rest, False), (dq_rest, True), (first_rest_all, False), (dk_rest, True),
                (dv_rest, True), (attn_in, False), (grad_mid_low, True)]
    qkv_sent = grad_part(there, rest_ins, [
        (0, 0, [(0, 1)]), (0, half_width, [(5, 6)]), (1, 0, [(2, 3)]), (1, half_width, [(2, 4)])],
        (dq_rest,))
    rest_got = [z_move(rest_parts[step], step) for step in range(1, GROUPS)]
    rest_got = hold_all(rest_got, (qkv_sent, grad_attn_main))
    ff_quarter = hold(ff_quarter, rest_got)
    ff_shard = lax.psum_scatter(ff_quarter, "seq", scatter_dimension=0, axis_index_groups=same_member)
    for move in more_moves:
        ff_shard = add_low(ff_shard, move(ff_shard))
    dq_main, dk_main, dv_main, first_own_main, first_far_main = attend_back(
        main_place, query_main, key_main, value_main, ext_main, logs_main, attn_main, grad_attn_main,
        main_weights, min(256, block_len * 2), main_own, (ff_quarter,), pairs)

    def in_half(part):
        part = part[:, :mine_cols]
        if mine_cols == width // 2:
            return part
        empty = jnp.zeros((part.shape[0], width // 2), part.dtype)
        return lax.dynamic_update_slice_in_dim(empty, part, (member // 2) * mine_cols, 1)

    main_ins = [(first_all, False), (in_half(dq_main), False), (in_half(dk_main), False),
                (in_half(dv_main), False)]
    qkv_kept = grad_part(here_place, rest_ins + main_ins, [
        (0, 0, [(0, 1), (7, 8)]), (0, half_width, [(5, 6)]),
        (1, 0, [(2, 3), (7, 9)]), (1, half_width, [(2, 4), (7, 10)])])
    ff_shard = hold(ff_shard, (qkv_kept,))
    ff_groups = lax.all_gather(ff_shard, "seq", axis=0, axis_index_groups=same_member)
    kx, sx, ky, sy = split_cores(here_place, qkv_kept, core_move(qkv_sent))

    small = jnp.concatenate([grad_gain_two, squares, valid_count[None]])
    small = jnp.pad(small, (0, -small.size % 1024)).reshape(-1, 128)
    for move in [core_move] + more_moves:
        small = small + move(small)

    got, sx, sy = hold_all([img_moves[0](small), img_moves[0](sx), img_moves[1](sy)])
    small = small + got
    kx, sx, ky, sy = add_pairs(kx, sx, ky, sy)

    ff_groups = hold(ff_groups, (kx,))
    ff_own = lax.all_gather(ff_groups, "img", axis=0, axis_index_groups=img_fours)
    far = [first_far_main[(step - 1) * main_own:step * main_own] for step in range(1, members)]
    got, sx, sy, *far = hold_all(
        [img_moves[1](small), img_moves[1](sx), img_moves[0](sy)]
        + [lax.ppermute(part, "seq", member_perm(step + 1)) for step, part in enumerate(far)])
    small = small + got
    shards = add_fours(kx, sx, ky, sy)
    grad_first_main = first_own_main + sum(part.astype(F32) for part in far)
    grad_first_rest = first_own_rest + rest_parts[0].astype(F32) + sum(part.astype(F32) for part in rest_got)
    grad_first = jnp.concatenate([grad_first_main, grad_first_rest], axis=0)
    grad_input_rows = (grad_mid + norm_back(resid, gain_one, grad_first)[0]).astype(BF)

    got, *pieces = hold_all([z_moves[0](small)] + [z_move(shards[step], step) for step in range(1, GROUPS)])
    small = small + got
    qkv_total = sum_shards([shards[0]] + pieces, (grad_input_rows,))
    for move in more_moves:
        qkv_total = add_low(qkv_total, move(qkv_total))

    got, *pieces = hold_all([z_moves[1](small)] + [z_move(qkv_total, step) for step in range(1, GROUPS)])
    small = (small + got).reshape(-1)
    x, y = stack_orders([qkv_total] + pieces)
    rx, ry, *got = hold_all([img_moves[1](x), img_moves[0](y)] + sent_home(grad_input_rows))
    near = stack_pairs(x, rx, y, ry)
    grad_input = placed(grad_input_rows, got)
    ff_own = hold(ff_own, (rx, ry))
    sum_gate, sum_up, sum_down = assemble_ff(here_place, ff_own, core_move(ff_own), w_gate.shape[1])
    rx, ry, cx, cy = hold_all(
        [img_moves[0](near[0]), img_moves[1](near[1]), core_move(near[0]), core_move(near[1])],
        (grad_input, sum_gate))
    pieces = [near[0], rx, cx, core_move(rx), near[1], ry, cy, core_move(ry)]
    sum_query, sum_out, sum_key, sum_value, sum_gain_one = assemble(
        here_place, pieces, (w_query, w_key, w_value), gain_one[:, None])
    sum_gain_one = sum_gain_one.reshape(width)
    sum_gain_two, sum_squares, sum_count = small[:width], small[width:width + 4], small[width + 4]
    rms_stats = jnp.sqrt(sum_squares / (sum_count * width))
    return (layer_out, grad_input, sum_gain_one, sum_query, sum_key, sum_value, sum_out,
            sum_gain_two, sum_gate, sum_up, sum_down, rms_stats)


def solution(mesh):
    rows = P("img", "seq", None)
    return jax.shard_map(
        functools.partial(body, mesh.shape["img"], mesh.shape["seq"]),
        mesh=mesh,
        in_specs=(rows, P("img"), P(), P(), P(), P(), P(), P(), P(), P(), P(), rows),
        out_specs=(rows, rows, P(), P(), P(), P(), P(), P(), P(), P(), P(), P()),
        check_vma=False,
    )
```
